32 devices in a mesh: face: 4 (over y, x), tile: 8 (over z, core).
Axes of the slice: x: 2, y: 2, z: 4, core: 2. Of those that a mesh axis runs over, the one named last changes fastest.
Arguments:
- latitude_rows: bfloat16 [128, 4096, 128], P(None, ('face', 'tile')), may hold values from -6 to 6
- tile_order: int32 [128], replicated, may hold values from 0 to 127, each once
- neighbours: int32 [128, 8], P(('face', 'tile')), may hold values from 0 to 127, as said below
- rotations: int32 [128, 8], P(('face', 'tile')), may hold values from 0 to 3
- w_first: bfloat16 [3, 3, 128, 128], replicated, may hold values from -0.1875 to 0.1875
- b_first: float32 [128], replicated, may hold values from -3 to 3
- w_second: bfloat16 [3, 3, 128, 128], replicated, may hold values from -0.1875 to 0.1875
- b_second: float32 [128], replicated, may hold values from -3 to 3
Outputs:
- level_output: bfloat16 [128, 64, 64, 128], P(('face', 'tile'))
The draws below stay inside these ranges and needn't reach their ends.
Inputs may be any that keep to these rules, and one draw needn't show every extreme that they name: `neighbours`: tiles are held in order, 4 a device, devices ordered face-major. Entry k of a row names a tile held by the device whose face index and tile index differ, counted cyclically, from those of the device that holds the row's tile by (-1,0), (+1,0), (0,-1), (0,+1), (-1,-1), (-1,+1), (+1,-1), (+1,+1) for k = 0 to 7.
All inputs are finite; a program needn't handle non-finite values.
Results may differ from the reference program's by a relative error of at most 0.0033.
Values may be sent and summed in bfloat16 or wider, within the bound.
No kernel may reach another device: no remote copies, remote signals or barrier semaphores. Data moves between devices by JAX's collectives and lax.ppermute only.
A program may use at most 64 MiB of HBM per device.

```python
from functools import partial
import jax
import jax.numpy as jnp
from jax import lax

SIDE = 64
CHANNELS = 128
TILES_DEV = 4
FACE_RANKS = 4
TILE_RANKS = 8
TILES = 128


def draw_neighbours(key, part):
    total = TILES_DEV * FACE_RANKS * TILE_RANKS
    tile_ids = jnp.arange(total, dtype=jnp.int32)
    home = tile_ids // TILES_DEV
    home_face = home // TILE_RANKS
    home_tile = home % TILE_RANKS
    local_key = jax.random.fold_in(key, 37)
    local_slot = jax.random.randint(local_key, (total, 8), 0, TILES_DEV, dtype=jnp.int32)
    face_step = jnp.array([-1, 1, 0, 0, -1, -1, 1, 1], jnp.int32)[None]
    tile_step = jnp.array([0, 0, -1, 1, -1, 1, -1, 1], jnp.int32)[None]
    owner_face = (home_face[:, None] + face_step) % FACE_RANKS
    owner_tile = (home_tile[:, None] + tile_step) % TILE_RANKS
    owner = owner_face * TILE_RANKS + owner_tile
    return (owner * TILES_DEV + local_slot).astype(jnp.int32)


def touch_ends(result, own_key, smallest, high):
    extent = result.shape
    place = [jax.random.randint(jax.random.fold_in(own_key, axis), (), 0, extent[axis]) for axis in range(len(extent))]
    result = result.at[tuple(place)].set(smallest)
    longest = extent.index(max(extent))
    place[longest] = (place[longest] + 1) % extent[longest]
    return result.at[tuple(place)].set(high)


def block_scale(key, extent, pieces, low, largest):
    level = 1.0
    for axis_at, blocks in pieces:
        heights = jax.random.uniform(jax.random.fold_in(jax.random.fold_in(key, 6), axis_at), (blocks,), jnp.float32, low / len(pieces), largest / len(pieces))
        level = level * jnp.repeat(jnp.exp(heights), extent[axis_at] // blocks).reshape((-1,) + (1,) * (len(extent) - 1 - axis_at))
    return level


def normal_values(own_key, shape, scale, limit, shards=(), kind=jnp.bfloat16):
    entries = jax.random.normal(own_key, shape, jnp.float32) * scale
    if len(shards) > 0:
        entries = block_scale(own_key, shape, shards, -0.22, 0.18) * entries
    return jnp.clip(entries, min=-limit, max=limit).astype(kind)


def setup_inputs(seed: int = 0) -> dict:
    splits = jax.random.split(jax.random.key(seed), 9)
    latitude_rows = normal_values(splits[0], (TILES, SIDE * SIDE, CHANNELS), 1.0, 6.0, ((1, 32),))
    tile_order = jax.random.permutation(splits[1], TILES).astype(jnp.int32)
    neighbours = draw_neighbours(jax.random.fold_in(splits[8], 71), 0)
    rotations = touch_ends(jax.random.randint(splits[3], (TILES, 8), 0, 4), jax.random.fold_in(splits[3], 1), 0, 3).astype(jnp.int32)
    w_first = normal_values(splits[4], (3, 3, CHANNELS, CHANNELS), (9 * CHANNELS) ** -0.5, 0.1875)
    b_first = normal_values(splits[5], (CHANNELS,), 0.5, 3.0, (), jnp.float32)
    w_second = normal_values(splits[6], (3, 3, CHANNELS, CHANNELS), (9 * CHANNELS) ** -0.5, 0.1875)
    b_second = normal_values(splits[7], (CHANNELS,), 0.5, 3.0, (), jnp.float32)
    return {"latitude_rows": latitude_rows, "tile_order": tile_order, "neighbours": neighbours, "rotations": rotations, "w_first": w_first, "b_first": b_first, "w_second": w_second, "b_second": b_second}


def convolve(padded, weight, bias):
    summed = lax.conv_general_dilated(padded, weight, (1, 1), "VALID", dimension_numbers=("NHWC", "HWIO", "NHWC"), preferred_element_type=jnp.float32)
    return summed + bias


def pad_one(source_tiles, centre, sources, turns):
    turners = [partial(jnp.rot90, k=quarter, axes=(0, 1)) for quarter in range(4)]

    def rotate_tile(other, rotation):
        return lax.switch(rotation, turners, other)

    others = jnp.take(source_tiles, sources, axis=0)
    turned = jax.vmap(rotate_tile)(others, turns)
    upper = jnp.concatenate([turned[4, -1, -1][None], turned[0, -1], turned[5, -1, 0][None]], 0)
    lower = jnp.concatenate([turned[6, 0, -1][None], turned[1, 0], turned[7, 0, 0][None]], 0)
    middle = jnp.concatenate([turned[2][:, -1][:, None], centre, turned[3][:, 0][:, None]], 1)
    return jnp.concatenate([upper[None], middle, lower[None]], 0)


def reference(latitude_rows, tile_order, neighbours, rotations, w_first, b_first, w_second, b_second):
    nested = jnp.take(latitude_rows, tile_order, axis=0).reshape(TILES, SIDE, SIDE, CHANNELS)

    def first_layer(inputs):
        centre, sources, turns = inputs
        padded = pad_one(nested, centre, sources, turns)
        first = convolve(padded[None], w_first, b_first)[0]
        return jax.nn.gelu(first, approximate=False).astype(jnp.bfloat16)

    hidden = lax.map(first_layer, (nested, neighbours, rotations))

    def second_layer(inputs):
        centre, sources, turns, residual_tile = inputs
        padded = pad_one(hidden, centre, sources, turns)
        second = convolve(padded[None], w_second, b_second)[0]
        return (residual_tile.astype(jnp.float32) + second).astype(jnp.bfloat16)

    return lax.map(second_layer, (hidden, neighbours, rotations, nested))
```

```python
import functools

import jax
import jax.numpy as jnp
import numpy as np
from jax import lax
from jax.experimental import pallas as pl
from jax.experimental.pallas import tpu as pltpu
from jax.sharding import PartitionSpec as P

STRIP_TABLE = np.array(
    [
        [1, 2, 0, 3],
        [0, 3, 1, 2],
        [3, 1, 2, 0],
        [2, 0, 3, 1],
        [1, 2, 0, 3],
        [1, 2, 0, 3],
        [0, 3, 1, 2],
        [0, 3, 1, 2],
    ],
    np.int32,
)
FLIP_TABLE = np.array(
    [
        [0, 0, 1, 1],
        [0, 0, 1, 1],
        [0, 1, 1, 0],
        [0, 1, 1, 0],
        [0, 0, 1, 1],
        [0, 0, 1, 1],
        [0, 0, 1, 1],
        [0, 0, 1, 1],
    ],
    np.int32,
)
DIRECTIONS = [(-1, 0), (1, 0), (0, -1), (0, 1), (-1, -1), (-1, 1), (1, -1), (1, 1)]
AXES = ("face", "tile")
VMEM = pltpu.VMEM
F32 = jnp.float32
BF16 = jnp.bfloat16
LIMIT = 48 * 1024 * 1024


def shift_down(line, first):
    moved = pltpu.roll(line, 1, 0)
    rows = lax.broadcasted_iota(jnp.int32, moved.shape, 0)
    return jnp.where(rows == 0, first, moved)


def shift_up(line, last):
    size = line.shape[0]
    moved = pltpu.roll(line, size - 1, 0)
    rows = lax.broadcasted_iota(jnp.int32, moved.shape, 0)
    return jnp.where(rows == size - 1, last, moved)


def gelu(value):
    return (0.5 * value) * (1.0 + lax.erf(value * np.float32(np.sqrt(0.5))))


def pick_lines(codes_ref, req_ref, lines, edge_refs, corner_refs):
    tiles = edge_refs[0].shape[0]
    side = edge_refs[0].shape[1]
    rows = lax.broadcasted_iota(jnp.int32, corner_refs[0].shape, 0)
    for direction in range(8):
        corner = jnp.zeros(corner_refs[0].shape, F32)
        for tile in range(tiles):
            code = codes_ref[req_ref[direction], tile * 8 + direction]
            line = lines[code]
            if direction < 4:
                edge_refs[direction][tile] = line
            else:
                at = side - 1 if direction in (4, 6) else 0
                pixel = line.astype(F32)[at : at + 1]
                corner = jnp.where(rows == tile, pixel, corner)
        if direction >= 4:
            corner_refs[direction - 4][...] = corner.astype(BF16)


def flip_line(line):
    size = line.shape[0]
    row = lax.broadcasted_iota(jnp.int32, (size, size), 0)
    col = lax.broadcasted_iota(jnp.int32, (size, size), 1)
    turn = jnp.where(row + col == size - 1, 1.0, 0.0).astype(BF16)
    return jnp.dot(turn, line, preferred_element_type=F32).astype(BF16)


def border_kernel(side, codes_ref, req_ref, x_ref, ring_ref, *rest):
    edge_refs, corner_refs, lines = rest[:4], rest[4:8], rest[8]
    tile = pl.program_id(0)
    tiles = edge_refs[0].shape[0]
    image = x_ref[...].reshape(side, side, x_ref.shape[-1])
    ring = [image[0], image[1], image[side - 2], image[side - 1]]
    low = image[:, :16].astype(F32)
    high = image[:, side - 16 :].astype(F32)
    ring += [v.astype(BF16) for v in (low[:, 0], low[:, 1], high[:, 14], high[:, 15])]
    for at, line in enumerate(ring):
        ring_ref[0, at] = line
    for strip, at in enumerate((0, 3, 4, 7)):
        lines[tile * 4 + strip] = ring[at]
        lines[tiles * 4 + tile * 4 + strip] = flip_line(ring[at])

    @pl.when(tile == tiles - 1)
    def _():
        pick_lines(codes_ref, req_ref, lines, edge_refs, corner_refs)


def ring_kernel(codes_ref, req_ref, ring_ref, w_ref, b_ref, *rest):
    pad_refs, pad_corner_refs = rest[:4], rest[4:8]
    edge_refs, corner_refs, lines = rest[8:12], rest[12:16], rest[16]
    tiles = ring_ref.shape[0]
    side = ring_ref.shape[2]
    corners = [ref[...].astype(F32) for ref in pad_corner_refs]
    plans = [
        (0, 0, 1, 0, 1, 2, 3, 0, 1),
        (1, 2, 3, 3, 2, 2, 3, side - 1, side - 2),
        (2, 0, 2, 4, 5, 0, 1, 0, 1),
        (3, 1, 3, 7, 6, 0, 1, side - 1, side - 2),
    ]
    for edge, (pad, c_first, c_last, line_0, line_1, end_a, end_b, at_0, at_1) in enumerate(plans):
        stacked = []
        for tile in range(tiles):
            begin = pad_refs[end_a][tile].astype(F32)
            finish = pad_refs[end_b][tile].astype(F32)
            parts = []
            for line, first, last in (
                (
                    pad_refs[pad][tile],
                    corners[c_first][tile : tile + 1],
                    corners[c_last][tile : tile + 1],
                ),
                (ring_ref[tile, line_0], begin[at_0 : at_0 + 1], finish[at_0 : at_0 + 1]),
                (ring_ref[tile, line_1], begin[at_1 : at_1 + 1], finish[at_1 : at_1 + 1]),
            ):
                wide = line.astype(F32)
                parts += [
                    shift_down(wide, first).astype(BF16),
                    line,
                    shift_up(wide, last).astype(BF16),
                ]
            stacked.append(jnp.concatenate(parts, axis=1))
        summed = jnp.dot(
            jnp.concatenate(stacked, axis=0), w_ref[edge], preferred_element_type=F32
        )
        hidden = gelu(summed + b_ref[...]).astype(BF16)
        for tile in range(tiles):
            line = hidden[tile * side : (tile + 1) * side]
            lines[tile * 4 + edge] = line
            lines[tiles * 4 + tile * 4 + edge] = flip_line(line)
    pick_lines(codes_ref, req_ref, lines, edge_refs, corner_refs)


def convolve_tile(padded, left, right, c_left, c_right, w_ref, w_side_ref, bias, y, ends, finish):
    side = padded.shape[2]
    chan = padded.shape[3]
    for at, (column, (first, last)) in enumerate(((left, c_left), (right, c_right))):
        wide = column.astype(F32)
        taps = jnp.concatenate(
            [
                shift_down(wide, first).astype(BF16),
                column,
                shift_up(wide, last).astype(BF16),
            ],
            axis=1,
        )
        ends[at] = jnp.dot(taps, w_side_ref[at], preferred_element_type=F32)
    pairs = side // 2
    blocks = y.shape[0]
    step = pairs // blocks
    rows = lax.broadcasted_iota(jnp.int32, (side, chan), 0)
    for block in range(blocks):
        lhs = jnp.concatenate(
            [
                padded[pl.ds(step * block + j // 2, step), j % 2].reshape(step * side, chan)
                for j in range(4)
            ],
            axis=1,
        )
        y[block] = jnp.dot(lhs, w_ref[...], preferred_element_type=F32)
    for block in range(blocks):
        for i in range(step):
            for half in range(2):
                row = (block * step + i) * 2 + half
                a, b, c = (
                    y[block, pl.ds(i * side, side), pl.ds((half * 3 + dx) * chan, chan)]
                    for dx in range(3)
                )
                a = jnp.where(rows == 0, ends[0, row : row + 1], pltpu.roll(a, 1, 0))
                c = jnp.where(
                    rows == side - 1, ends[1, row : row + 1], pltpu.roll(c, side - 1, 0)
                )
                finish(row, (a + c) + (b + bias))


def level_kernel(side, x_ref, *rest):
    pads = (rest[0:4], rest[8:12])
    corners = (rest[4:8], rest[12:16])
    w_refs, w_side_refs, b_refs = rest[16:18], rest[18:20], rest[20:22]
    out_ref, padded, hidden, y, ends = rest[22:]
    chan = x_ref.shape[-1]
    half = side // 2
    image = x_ref[...].reshape(side, side, chan)
    fields = (padded, hidden)
    for field, pad in zip(fields, pads):
        field[0, 0] = pad[0][0]
        field[half, 1] = pad[1][0]
    padded[0, 1] = image[0]
    padded[1:half] = image[1 : side - 1].reshape(half - 1, 2, side, chan)
    padded[half, 0] = image[side - 1]

    def keep_hidden(row, value):
        hidden[(row + 1) // 2, (row + 1) % 2] = gelu(value).astype(BF16)

    def keep_out(row, value):
        centre = padded[(row + 1) // 2, (row + 1) % 2].astype(F32)
        out_ref[0, row] = (centre + value).astype(BF16)

    for at, finish in enumerate((keep_hidden, keep_out)):
        upper_left, upper_right, lower_left, lower_right = (
            ref[0, 0:1].astype(F32) for ref in corners[at]
        )
        convolve_tile(
            fields[at],
            pads[at][2][0],
            pads[at][3][0],
            (upper_left, lower_left),
            (upper_right, lower_right),
            w_refs[at],
            w_side_refs[at],
            b_refs[at][...],
            y,
            ends,
            finish,
        )


def paired_weights(weight):
    chan_in, chan_out = weight.shape[2:]
    by_tap = weight.transpose(0, 2, 1, 3).reshape(3, chan_in, 3 * chan_out)
    zero = jnp.zeros((1, chan_in, 3 * chan_out), weight.dtype)
    first = jnp.concatenate([by_tap, zero], 0)
    second = jnp.concatenate([zero, by_tap], 0)
    return jnp.stack([first, second], 2).reshape(4 * chan_in, 6 * chan_out)


def side_weights(weight):
    chan_in, chan_out = weight.shape[2:]
    return jnp.stack([weight[:, 0], weight[:, 2]], 0).reshape(2, 3 * chan_in, chan_out)


def edge_weights(weight):
    chan_in, chan_out = weight.shape[2:]
    turned = weight.transpose(1, 0, 2, 3)
    stacked = jnp.stack([weight, weight[::-1], turned, turned[::-1]], 0)
    return stacked.reshape(4, 9 * chan_in, chan_out)


def exchange(arrays, faces, columns):
    got = []
    for array, (face_off, tile_off) in zip(arrays, DIRECTIONS):
        pairs = []
        for face in range(faces):
            for tile in range(columns):
                to = ((face - face_off) % faces) * columns + (tile - tile_off) % columns
                pairs.append((face * columns + tile, to))
        got.append(lax.ppermute(array, AXES, pairs))
    return got


def shards(latitude_rows, tile_order, neighbours, rotations, w_first, b_first, w_second, b_second):
    faces, columns = lax.axis_size("face"), lax.axis_size("tile")
    devices = faces * columns
    tiles = neighbours.shape[0]
    piece, chan = latitude_rows.shape[1:]
    side = int(round((piece * devices) ** 0.5))
    vmem_spec = pl.BlockSpec(memory_space=VMEM)
    smem_spec = pl.BlockSpec(memory_space=pltpu.SMEM)
    params = pltpu.CompilerParams(vmem_limit_bytes=LIMIT)

    turn = rotations[..., None] == jnp.arange(4, dtype=jnp.int32)
    strip = jnp.sum(jnp.where(turn, jnp.asarray(STRIP_TABLE)[None], 0), -1)
    flip = jnp.sum(jnp.where(turn, jnp.asarray(FLIP_TABLE)[None], 0), -1)
    code = (flip * tiles + neighbours % tiles) * 4 + strip
    codes = lax.all_gather(code.reshape(1, tiles * 8), AXES, axis=0, tiled=True)
    face, column = lax.axis_index("face"), lax.axis_index("tile")
    asking = jnp.stack(
        [((face - f) % faces) * columns + (column - t) % columns for f, t in DIRECTIONS]
    ).astype(jnp.int32)

    ordered = latitude_rows.at[tile_order].get(mode="promise_in_bounds")
    gathered = lax.all_to_all(ordered, AXES, split_axis=0, concat_axis=0, tiled=True)
    pieces = gathered.reshape(devices, tiles, piece, chan)
    tile_spec = pl.BlockSpec((devices, 1, piece, chan), lambda t: (0, t, 0, 0))

    edge_shape = jax.ShapeDtypeStruct((tiles, side, chan), BF16)
    corner_shape = jax.ShapeDtypeStruct((16, chan), BF16)
    lines_scratch = VMEM((8 * tiles, side, chan), BF16)
    edge_out = pl.BlockSpec((tiles, side, chan), lambda t: (0, 0, 0))
    corner_out = pl.BlockSpec((16, chan), lambda t: (0, 0))
    ring, *sends = pl.pallas_call(
        functools.partial(border_kernel, side),
        grid=(tiles,),
        in_specs=[smem_spec, smem_spec, tile_spec],
        out_specs=[pl.BlockSpec((1, 8, side, chan), lambda t: (t, 0, 0, 0))]
        + [edge_out] * 4
        + [corner_out] * 4,
        out_shape=[jax.ShapeDtypeStruct((tiles, 8, side, chan), BF16)]
        + [edge_shape] * 4
        + [corner_shape] * 4,
        scratch_shapes=[lines_scratch],
        compiler_params=params,
        name="borders",
    )(codes, asking, pieces)
    pads_first = exchange(sends, faces, columns)

    sends = pl.pallas_call(
        ring_kernel,
        in_specs=[smem_spec, smem_spec] + [vmem_spec] * 11,
        out_specs=[vmem_spec] * 8,
        out_shape=[edge_shape] * 4 + [corner_shape] * 4,
        scratch_shapes=[lines_scratch],
        compiler_params=params,
        name="hidden_ring",
    )(codes, asking, ring, edge_weights(w_first), b_first.reshape(1, chan), *pads_first)
    pads_second = exchange(sends, faces, columns)

    edge_in = pl.BlockSpec((1, side, chan), lambda t: (t, 0, 0))
    corner_in = pl.BlockSpec((1, 8, chan), lambda t: (t, 0, 0))

    def whole(array):
        return pl.BlockSpec(array.shape, lambda t: (0,) * array.ndim)

    def spread(pads):
        corners = [jnp.broadcast_to(c[:tiles, None], (tiles, 8, chan)) for c in pads[4:]]
        return list(pads[:4]) + corners

    constants = [
        paired_weights(w_first),
        paired_weights(w_second),
        side_weights(w_first),
        side_weights(w_second),
        b_first.reshape(1, chan),
        b_second.reshape(1, chan),
    ]
    blocks = 4
    field = VMEM((side // 2 + 1, 2, side, chan), BF16)
    return pl.pallas_call(
        functools.partial(level_kernel, side),
        grid=(tiles,),
        in_specs=[tile_spec]
        + ([edge_in] * 4 + [corner_in] * 4) * 2
        + [whole(c) for c in constants],
        out_specs=pl.BlockSpec((1, side, side, chan), lambda t: (t, 0, 0, 0)),
        out_shape=jax.ShapeDtypeStruct((tiles, side, side, chan), BF16),
        scratch_shapes=[
            field,
            field,
            VMEM((blocks, side // 2 // blocks * side, 6 * chan), F32),
            VMEM((2, side, chan), F32),
        ],
        compiler_params=params,
        name="level",
    )(pieces, *spread(pads_first), *spread(pads_second), *constants)


def solution(mesh):
    return jax.shard_map(
        shards,
        mesh=mesh,
        in_specs=(
            P(None, ("face", "tile"), None),
            P(),
            P(("face", "tile"), None),
            P(("face", "tile"), None),
            P(),
            P(),
            P(),
            P(),
        ),
        out_specs=P(("face", "tile"), None, None, None),
        check_vma=False,
    )
```

```python
import functools

import jax
import jax.numpy as jnp
import numpy as np
from jax import lax
from jax.experimental import pallas as pl
from jax.experimental.pallas import tpu as pltpu
from jax.sharding import PartitionSpec as P

STRIP_TABLE = np.array(
    [
        [1, 2, 0, 3],
        [0, 3, 1, 2],
        [3, 1, 2, 0],
        [2, 0, 3, 1],
        [1, 2, 0, 3],
        [1, 2, 0, 3],
        [0, 3, 1, 2],
        [0, 3, 1, 2],
    ],
    np.int32,
)
FLIP_TABLE = np.array(
    [
        [0, 0, 1, 1],
        [0, 0, 1, 1],
        [0, 1, 1, 0],
        [0, 1, 1, 0],
        [0, 0, 1, 1],
        [0, 0, 1, 1],
        [0, 0, 1, 1],
        [0, 0, 1, 1],
    ],
    np.int32,
)
DIRECTIONS = [(-1, 0), (1, 0), (0, -1), (0, 1), (-1, -1), (-1, 1), (1, -1), (1, 1)]
AXES = ("face", "tile")
VMEM = pltpu.VMEM
F32 = jnp.float32
BF16 = jnp.bfloat16
LIMIT = 48 * 1024 * 1024
CORNERS = 16


def shift_down(line, first):
    moved = pltpu.roll(line, 1, 0)
    rows = lax.broadcasted_iota(jnp.int32, moved.shape, 0)
    return jnp.where(rows == 0, first, moved)


def shift_up(line, last):
    size = line.shape[0]
    moved = pltpu.roll(line, size - 1, 0)
    rows = lax.broadcasted_iota(jnp.int32, moved.shape, 0)
    return jnp.where(rows == size - 1, last, moved)


def gelu(value):
    return (0.5 * value) * (1.0 + lax.erf(value * np.float32(np.sqrt(0.5))))


def pick_lines(codes_ref, lines, message_refs, tiles):
    side = lines.shape[1]
    shape = (CORNERS, lines.shape[2])
    rows = lax.broadcasted_iota(jnp.int32, shape, 0)
    for direction in range(8):
        corner = jnp.zeros(shape, F32)
        for tile in range(tiles):
            line = lines[codes_ref[direction, tile * 8 + direction]]
            if direction < 4:
                message_refs[direction][pl.ds(tile * side, side), :] = line
            else:
                at = side - 1 if direction in (4, 6) else 0
                pixel = line.astype(F32)[at : at + 1]
                corner = jnp.where(rows == tile, pixel, corner)
        if direction >= 4:
            group = tiles * side + (direction % 2) * CORNERS
            message_refs[direction // 2 - 2][pl.ds(group, CORNERS), :] = corner.astype(BF16)


def flip_line(line):
    size = line.shape[0]
    row = lax.broadcasted_iota(jnp.int32, (size, size), 0)
    col = lax.broadcasted_iota(jnp.int32, (size, size), 1)
    turn = jnp.where(row + col == size - 1, 1.0, 0.0).astype(BF16)
    return jnp.dot(turn, line, preferred_element_type=F32).astype(BF16)


def gather_kernel(order_ref, x_ref, o_ref, sem):
    def start(at, carry):
        pltpu.make_async_copy(x_ref.at[order_ref[at]], o_ref.at[at], sem).start()
        return carry

    lax.fori_loop(0, order_ref.shape[0], start, 0)
    pltpu.make_async_copy(x_ref, o_ref, sem).wait()


def border_kernel(side, tiles, codes_ref, x_ref, ring_ref, *rest):
    message_refs, lines = rest[:4], rest[4]
    tile = pl.program_id(0)
    image = x_ref[...].reshape(side, side, x_ref.shape[-1])
    ring = [image[0], image[1], image[side - 2], image[side - 1]]
    low = image[:, :16].astype(F32)
    high = image[:, side - 16 :].astype(F32)
    ring += [v.astype(BF16) for v in (low[:, 0], low[:, 1], high[:, 14], high[:, 15])]
    for at, line in enumerate(ring):
        ring_ref[0, at] = line
    for strip, at in enumerate((0, 3, 4, 7)):
        lines[tile * 4 + strip] = ring[at]
        lines[tiles * 4 + tile * 4 + strip] = flip_line(ring[at])

    @pl.when(tile == tiles - 1)
    def _():
        pick_lines(codes_ref, lines, message_refs, tiles)


def ring_kernel(codes_ref, ring_ref, w_ref, b_ref, *rest):
    got_refs, message_refs, lines = rest[:4], rest[4:8], rest[8]
    tiles = ring_ref.shape[0]
    side = ring_ref.shape[2]
    pads = [[ref[pl.ds(t * side, side), :] for t in range(tiles)] for ref in got_refs]
    corners = [
        got_refs[2 + k % 2][pl.ds(tiles * side + k // 2 * CORNERS, CORNERS), :].astype(F32)
        for k in range(4)
    ]
    plans = [
        (0, 0, 1, 0, 1, 2, 3, 0, 1),
        (1, 2, 3, 3, 2, 2, 3, side - 1, side - 2),
        (2, 0, 2, 4, 5, 0, 1, 0, 1),
        (3, 1, 3, 7, 6, 0, 1, side - 1, side - 2),
    ]
    for edge, (pad, c_first, c_last, line_0, line_1, end_a, end_b, at_0, at_1) in enumerate(plans):
        stacked = []
        for tile in range(tiles):
            begin = pads[end_a][tile].astype(F32)
            finish = pads[end_b][tile].astype(F32)
            parts = []
            for line, first, last in (
                (
                    pads[pad][tile],
                    corners[c_first][tile : tile + 1],
                    corners[c_last][tile : tile + 1],
                ),
                (ring_ref[tile, line_0], begin[at_0 : at_0 + 1], finish[at_0 : at_0 + 1]),
                (ring_ref[tile, line_1], begin[at_1 : at_1 + 1], finish[at_1 : at_1 + 1]),
            ):
                wide = line.astype(F32)
                parts += [
                    shift_down(wide, first).astype(BF16),
                    line,
                    shift_up(wide, last).astype(BF16),
                ]
            stacked.append(jnp.concatenate(parts, axis=1))
        summed = jnp.dot(
            jnp.concatenate(stacked, axis=0), w_ref[edge], preferred_element_type=F32
        )
        hidden = gelu(summed + b_ref[...]).astype(BF16)
        for tile in range(tiles):
            line = hidden[tile * side : (tile + 1) * side]
            lines[tile * 4 + edge] = line
            lines[tiles * 4 + tile * 4 + edge] = flip_line(line)
    pick_lines(codes_ref, lines, message_refs, tiles)


def convolve_tile(padded, left, right, c_left, c_right, w_ref, w_side_ref, bias, y, ends, finish):
    side = padded.shape[2]
    chan = padded.shape[3]
    for at, (column, (first, last)) in enumerate(((left, c_left), (right, c_right))):
        wide = column.astype(F32)
        taps = jnp.concatenate(
            [
                shift_down(wide, first).astype(BF16),
                column,
                shift_up(wide, last).astype(BF16),
            ],
            axis=1,
        )
        ends[at] = jnp.dot(taps, w_side_ref[at], preferred_element_type=F32)
    pairs = side // 2
    blocks = y.shape[0]
    step = pairs // blocks
    rows = lax.broadcasted_iota(jnp.int32, (side, chan), 0)
    for block in range(blocks):
        lhs = jnp.concatenate(
            [
                padded[pl.ds(step * block + j // 2, step), j % 2].reshape(step * side, chan)
                for j in range(4)
            ],
            axis=1,
        )
        y[block] = jnp.dot(lhs, w_ref[...], preferred_element_type=F32)
    for block in range(blocks):
        for i in range(step):
            for half in range(2):
                row = (block * step + i) * 2 + half
                a, b, c = (
                    y[block, pl.ds(i * side, side), pl.ds((half * 3 + dx) * chan, chan)]
                    for dx in range(3)
                )
                a = jnp.where(rows == 0, ends[0, row : row + 1], pltpu.roll(a, 1, 0))
                c = jnp.where(
                    rows == side - 1, ends[1, row : row + 1], pltpu.roll(c, side - 1, 0)
                )
                finish(row, (a + c) + (b + bias))


def level_kernel(side, x_ref, *rest):
    pads = (rest[0:4], rest[8:12])
    corners = (rest[4:8], rest[12:16])
    w_refs, w_side_refs, b_refs = rest[16:18], rest[18:20], rest[20:22]
    out_ref, padded, hidden, y, ends = rest[22:]
    chan = x_ref.shape[-1]
    half = side // 2
    image = x_ref[...].reshape(side, side, chan)
    fields = (padded, hidden)
    for field, pad in zip(fields, pads):
        field[0, 0] = pad[0][...]
        field[half, 1] = pad[1][...]
    padded[0, 1] = image[0]
    padded[1:half] = image[1 : side - 1].reshape(half - 1, 2, side, chan)
    padded[half, 0] = image[side - 1]

    def keep_hidden(row, value):
        hidden[(row + 1) // 2, (row + 1) % 2] = gelu(value).astype(BF16)

    def keep_out(row, value):
        centre = padded[(row + 1) // 2, (row + 1) % 2].astype(F32)
        out_ref[0, row] = (centre + value).astype(BF16)

    for at, finish in enumerate((keep_hidden, keep_out)):
        own = lax.broadcasted_iota(jnp.int32, (CORNERS, chan), 0) == pl.program_id(0)
        upper_left, upper_right, lower_left, lower_right = (
            jnp.sum(jnp.where(own, ref[...].astype(F32), 0.0), axis=0, keepdims=True)
            for ref in corners[at]
        )
        convolve_tile(
            fields[at],
            pads[at][2][...],
            pads[at][3][...],
            (upper_left, lower_left),
            (upper_right, lower_right),
            w_refs[at],
            w_side_refs[at],
            b_refs[at][...],
            y,
            ends,
            finish,
        )


def paired_weights(weight):
    chan_in, chan_out = weight.shape[2:]
    by_tap = weight.transpose(0, 2, 1, 3).reshape(3, chan_in, 3 * chan_out)
    zero = jnp.zeros((1, chan_in, 3 * chan_out), weight.dtype)
    first = jnp.concatenate([by_tap, zero], 0)
    second = jnp.concatenate([zero, by_tap], 0)
    return jnp.stack([first, second], 2).reshape(4 * chan_in, 6 * chan_out)


def side_weights(weight):
    chan_in, chan_out = weight.shape[2:]
    return jnp.stack([weight[:, 0], weight[:, 2]], 0).reshape(2, 3 * chan_in, chan_out)


def edge_weights(weight):
    chan_in, chan_out = weight.shape[2:]
    turned = weight.transpose(1, 0, 2, 3)
    stacked = jnp.stack([weight, weight[::-1], turned, turned[::-1]], 0)
    return stacked.reshape(4, 9 * chan_in, chan_out)


def along(array, axis, step):
    size = lax.axis_size(axis)
    return lax.ppermute(array, axis, [(i, (i + step) % size) for i in range(size)])


def exchange(messages, split):
    upper = along(messages[0], "face", 1)
    lower = along(messages[1], "face", -1)
    right = jnp.concatenate(
        [messages[2][:split], upper[split : split + CORNERS], lower[split : split + CORNERS]], 0
    )
    left = jnp.concatenate(
        [messages[3][:split], upper[split + CORNERS :], lower[split + CORNERS :]], 0
    )
    return [upper, lower, along(right, "tile", 1), along(left, "tile", -1)]


def shards(latitude_rows, tile_order, neighbours, rotations, w_first, b_first, w_second, b_second):
    devices = lax.axis_size("face") * lax.axis_size("tile")
    tiles = neighbours.shape[0]
    piece, chan = latitude_rows.shape[1:]
    side = int(round((piece * devices) ** 0.5))
    vmem_spec = pl.BlockSpec(memory_space=VMEM)
    smem_spec = pl.BlockSpec(memory_space=pltpu.SMEM)
    any_spec = pl.BlockSpec(memory_space=pl.ANY)
    params = pltpu.CompilerParams(vmem_limit_bytes=LIMIT)

    turn = rotations[..., None] == jnp.arange(4, dtype=jnp.int32)
    strip = jnp.sum(jnp.where(turn, jnp.asarray(STRIP_TABLE)[None], 0), -1)
    flip = jnp.sum(jnp.where(turn, jnp.asarray(FLIP_TABLE)[None], 0), -1)
    code = ((flip * tiles + neighbours % tiles) * 4 + strip).reshape(1, tiles * 8)
    after, before = along(code, "face", -1), along(code, "face", 1)

    ordered = pl.pallas_call(
        gather_kernel,
        in_specs=[smem_spec, any_spec],
        out_specs=any_spec,
        out_shape=jax.ShapeDtypeStruct(latitude_rows.shape, latitude_rows.dtype),
        scratch_shapes=[pltpu.SemaphoreType.DMA],
        compiler_params=params,
        name="order",
    )(tile_order, latitude_rows)
    ordered, after, before = lax.optimization_barrier((ordered, after, before))
    gathered = lax.all_to_all(ordered, AXES, split_axis=0, concat_axis=0, tiled=True)
    column = jnp.concatenate([code, after, before], 0)
    on, back = along(column, "tile", -1), along(column, "tile", 1)
    codes = jnp.concatenate(
        [after, before] + [side_rows[i : i + 1] for i in range(3) for side_rows in (on, back)], 0
    )
    constants = [
        paired_weights(w_first),
        paired_weights(w_second),
        side_weights(w_first),
        side_weights(w_second),
        b_first.reshape(1, chan),
        b_second.reshape(1, chan),
    ]
    w_edges = edge_weights(w_first)
    gathered, codes, w_edges, *constants = lax.optimization_barrier(
        (gathered, codes, w_edges, *constants)
    )
    pieces = gathered.reshape(devices, tiles, piece, chan)
    tile_spec = pl.BlockSpec((devices, 1, piece, chan), lambda t: (0, t, 0, 0))

    split = tiles * side
    message_shape = jax.ShapeDtypeStruct((split + 2 * CORNERS, chan), BF16)
    lines_scratch = VMEM((8 * tiles, side, chan), BF16)
    ring, *sends = pl.pallas_call(
        functools.partial(border_kernel, side, tiles),
        grid=(tiles,),
        in_specs=[smem_spec, tile_spec],
        out_specs=[pl.BlockSpec((1, 8, side, chan), lambda t: (t, 0, 0, 0))]
        + [pl.BlockSpec(message_shape.shape, lambda t: (0, 0))] * 4,
        out_shape=[jax.ShapeDtypeStruct((tiles, 8, side, chan), BF16)] + [message_shape] * 4,
        scratch_shapes=[lines_scratch],
        compiler_params=params,
        name="borders",
    )(codes, pieces)
    got_first = exchange(sends, split)

    sends = pl.pallas_call(
        ring_kernel,
        in_specs=[smem_spec] + [vmem_spec] * 7,
        out_specs=[vmem_spec] * 4,
        out_shape=[message_shape] * 4,
        scratch_shapes=[lines_scratch],
        compiler_params=params,
        name="hidden_ring",
    )(codes, ring, w_edges, b_first.reshape(1, chan), *got_first)
    got_second = exchange(sends, split)

    def whole(array):
        return pl.BlockSpec(array.shape, lambda t: (0,) * array.ndim)

    def group(at):
        return pl.BlockSpec((CORNERS, chan), lambda t: (split // CORNERS + at, 0))

    edge_in = pl.BlockSpec((side, chan), lambda t: (t, 0))
    pad_specs = [edge_in] * 4 + [group(0), group(0), group(1), group(1)]

    def pads(got):
        return got + [got[2], got[3], got[2], got[3]]

    blocks = 4
    field = VMEM((side // 2 + 1, 2, side, chan), BF16)
    return pl.pallas_call(
        functools.partial(level_kernel, side),
        grid=(tiles,),
        in_specs=[tile_spec] + pad_specs * 2 + [whole(c) for c in constants],
        out_specs=pl.BlockSpec((1, side, side, chan), lambda t: (t, 0, 0, 0)),
        out_shape=jax.ShapeDtypeStruct((tiles, side, side, chan), BF16),
        scratch_shapes=[
            field,
            field,
            VMEM((blocks, side // 2 // blocks * side, 6 * chan), F32),
            VMEM((2, side, chan), F32),
        ],
        compiler_params=params,
        name="level",
    )(pieces, *pads(got_first), *pads(got_second), *constants)


def solution(mesh):
    return jax.shard_map(
        shards,
        mesh=mesh,
        in_specs=(
            P(None, ("face", "tile"), None),
            P(),
            P(("face", "tile"), None),
            P(("face", "tile"), None),
            P(),
            P(),
            P(),
            P(),
        ),
        out_specs=P(("face", "tile"), None, None, None),
        check_vma=False,
    )
```

```python
import functools

import jax
import jax.numpy as jnp
import numpy as np
from jax import lax
from jax.experimental import pallas as pl
from jax.experimental.pallas import tpu as pltpu
from jax.sharding import PartitionSpec as P

STRIP_TABLE = np.array(
    [
        [1, 2, 0, 3],
        [0, 3, 1, 2],
        [3, 1, 2, 0],
        [2, 0, 3, 1],
        [1, 2, 0, 3],
        [1, 2, 0, 3],
        [0, 3, 1, 2],
        [0, 3, 1, 2],
    ],
    np.int32,
)
FLIP_TABLE = np.array(
    [
        [0, 0, 1, 1],
        [0, 0, 1, 1],
        [0, 1, 1, 0],
        [0, 1, 1, 0],
        [0, 0, 1, 1],
        [0, 0, 1, 1],
        [0, 0, 1, 1],
        [0, 0, 1, 1],
    ],
    np.int32,
)
DIRECTIONS = [(-1, 0), (1, 0), (0, -1), (0, 1), (-1, -1), (-1, 1), (1, -1), (1, 1)]
AXES = ("face", "tile")
VMEM = pltpu.VMEM
F32 = jnp.float32
BF16 = jnp.bfloat16
LIMIT = 48 * 1024 * 1024
CORNERS = 16


def shift_down(line, first):
    moved = pltpu.roll(line, 1, 0)
    rows = lax.broadcasted_iota(jnp.int32, moved.shape, 0)
    return jnp.where(rows == 0, first, moved)


def shift_up(line, last):
    size = line.shape[0]
    moved = pltpu.roll(line, size - 1, 0)
    rows = lax.broadcasted_iota(jnp.int32, moved.shape, 0)
    return jnp.where(rows == size - 1, last, moved)


def gelu(value):
    return (0.5 * value) * (1.0 + lax.erf(value * np.float32(np.sqrt(0.5))))


def pick_lines(codes_ref, lines, message_refs, tiles):
    side = lines.shape[1]
    shape = (CORNERS, lines.shape[2])
    rows = lax.broadcasted_iota(jnp.int32, shape, 0)
    for direction in range(8):
        corner = jnp.zeros(shape, F32)
        for tile in range(tiles):
            line = lines[codes_ref[direction, tile * 8 + direction]]
            if direction < 4:
                message_refs[direction][pl.ds(tile * side, side), :] = line
            else:
                at = side - 1 if direction in (4, 6) else 0
                pixel = line.astype(F32)[at : at + 1]
                corner = jnp.where(rows == tile, pixel, corner)
        if direction >= 4:
            group = tiles * side + (direction % 2) * CORNERS
            message_refs[direction // 2 - 2][pl.ds(group, CORNERS), :] = corner.astype(BF16)


def flip_line(line):
    size = line.shape[0]
    row = lax.broadcasted_iota(jnp.int32, (size, size), 0)
    col = lax.broadcasted_iota(jnp.int32, (size, size), 1)
    turn = jnp.where(row + col == size - 1, 1.0, 0.0).astype(BF16)
    return jnp.dot(turn, line, preferred_element_type=F32).astype(BF16)


def gather_kernel(order_ref, x_ref, o_ref, held, in_sems, out_sem):
    groups = in_sems.shape[0]
    size = held.shape[0] // groups

    def start(at, carry):
        pltpu.make_async_copy(
            x_ref.at[order_ref[at]], held.at[at], in_sems.at[at // size]
        ).start()
        return carry

    lax.fori_loop(0, held.shape[0], start, 0)
    for group in range(groups):
        part = pl.ds(group * size, size)
        pltpu.make_async_copy(x_ref.at[part], held.at[part], in_sems.at[group]).wait()
        pltpu.make_async_copy(held.at[part], o_ref.at[part], out_sem).start()
    pltpu.make_async_copy(held, o_ref, out_sem).wait()


def border_kernel(side, tiles, codes_ref, top_ref, low_ref, left_ref, right_ref, ring_ref, *rest):
    message_refs, lines = rest[:4], rest[4]
    tile = pl.program_id(0)
    chan = ring_ref.shape[-1]
    top = top_ref[...].reshape(-1, side, chan)
    low = low_ref[...].reshape(-1, side, chan)
    ring = [top[0], top[1], low[low.shape[0] - 2], low[low.shape[0] - 1]]
    low = left_ref[...].reshape(side, 16, chan).astype(F32)
    high = right_ref[...].reshape(side, 16, chan).astype(F32)
    ring += [v.astype(BF16) for v in (low[:, 0], low[:, 1], high[:, 14], high[:, 15])]
    for at, line in enumerate(ring):
        ring_ref[0, at] = line
    for strip, at in enumerate((0, 3, 4, 7)):
        lines[tile * 4 + strip] = ring[at]
        lines[tiles * 4 + tile * 4 + strip] = flip_line(ring[at])

    @pl.when(tile == tiles - 1)
    def _():
        pick_lines(codes_ref, lines, message_refs, tiles)


def ring_kernel(codes_ref, ring_ref, w_ref, b_ref, *rest):
    got_refs, message_refs, own_ref, lines = rest[:4], rest[4:8], rest[8], rest[9]
    tiles = ring_ref.shape[0]
    side = ring_ref.shape[2]
    pads = [[ref[pl.ds(t * side, side), :] for t in range(tiles)] for ref in got_refs]
    corners = [
        got_refs[2 + k % 2][pl.ds(tiles * side + k // 2 * CORNERS, CORNERS), :].astype(F32)
        for k in range(4)
    ]
    plans = [
        (0, 0, 1, 0, 1, 2, 3, 0, 1),
        (1, 2, 3, 3, 2, 2, 3, side - 1, side - 2),
        (2, 0, 2, 4, 5, 0, 1, 0, 1),
        (3, 1, 3, 7, 6, 0, 1, side - 1, side - 2),
    ]
    for edge, (pad, c_first, c_last, line_0, line_1, end_a, end_b, at_0, at_1) in enumerate(plans):
        stacked = []
        for tile in range(tiles):
            begin = pads[end_a][tile].astype(F32)
            finish = pads[end_b][tile].astype(F32)
            parts = []
            for line, first, last in (
                (
                    pads[pad][tile],
                    corners[c_first][tile : tile + 1],
                    corners[c_last][tile : tile + 1],
                ),
                (ring_ref[tile, line_0], begin[at_0 : at_0 + 1], finish[at_0 : at_0 + 1]),
                (ring_ref[tile, line_1], begin[at_1 : at_1 + 1], finish[at_1 : at_1 + 1]),
            ):
                wide = line.astype(F32)
                parts += [
                    shift_down(wide, first).astype(BF16),
                    line,
                    shift_up(wide, last).astype(BF16),
                ]
            stacked.append(jnp.concatenate(parts, axis=1))
        summed = jnp.dot(
            jnp.concatenate(stacked, axis=0), w_ref[edge], preferred_element_type=F32
        )
        hidden = gelu(summed + b_ref[...]).astype(BF16)
        for tile in range(tiles):
            line = hidden[tile * side : (tile + 1) * side]
            own_ref[tile, edge] = line
            lines[tile * 4 + edge] = line
            lines[tiles * 4 + tile * 4 + edge] = flip_line(line)
    pick_lines(codes_ref, lines, message_refs, tiles)


def moved_columns(pads, corners, w_side_ref, ends):
    for at in range(2):
        taps = jnp.concatenate(
            [
                shift_down(pads[at].astype(F32), corners[at]).astype(BF16),
                pads[at],
                shift_up(pads[at].astype(F32), corners[2 + at]).astype(BF16),
            ],
            axis=1,
        )
        ends[at] = jnp.dot(taps, w_side_ref[at], preferred_element_type=F32)


def convolve_tile(padded, w_ref, bias, y, ends, finish):
    side = padded.shape[2]
    chan = padded.shape[3]
    blocks = y.shape[0]
    step = side // 2 // blocks
    rows = lax.broadcasted_iota(jnp.int32, (side, chan), 0)

    def multiply(block):
        lhs = jnp.concatenate(
            [
                padded[pl.ds(step * block + j // 2, step), j % 2].reshape(step * side, chan)
                for j in range(4)
            ],
            axis=1,
        )
        y[block] = jnp.dot(lhs, w_ref[...], preferred_element_type=F32)

    multiply(0)
    for block in range(blocks):
        if block + 1 < blocks:
            multiply(block + 1)
        for i in range(step):
            for half in range(2):
                row = (block * step + i) * 2 + half
                a, b, c = (
                    y[block, pl.ds(i * side, side), pl.ds((half * 3 + dx) * chan, chan)]
                    for dx in range(3)
                )
                a = pltpu.roll(a, 1, 0)
                c = pltpu.roll(c, side - 1, 0)
                if ends is not None:
                    a = jnp.where(rows == 0, ends[0, row : row + 1], a)
                    c = jnp.where(rows == side - 1, ends[1, row : row + 1], c)
                finish(row, (a + c) + (b + bias))


def first_kernel(side, *refs):
    x_ref, w_ref, b_ref = refs[:3]
    out_ref, padded, y = refs[-3:]
    chan = x_ref.shape[-1]
    half = side // 2
    image = x_ref[...].reshape(side, side, chan)
    padded[0, 0] = jnp.zeros((side, chan), BF16)
    padded[half, 1] = jnp.zeros((side, chan), BF16)
    padded[0, 1] = image[0]
    padded[1:half] = image[1 : side - 1].reshape(half - 1, 2, side, chan)
    padded[half, 0] = image[side - 1]

    def finish(row, value):
        out_ref[0, row] = gelu(value).astype(BF16)

    convolve_tile(padded, w_ref, b_ref[...], y, None, finish)


def second_kernel(side, x_ref, h_ref, ring_ref, *rest):
    pad_refs, corner_refs = rest[:4], rest[4:8]
    w_ref, w_side_ref, b_ref, out_ref, padded, y, ends = rest[8:]
    chan = x_ref.shape[-1]
    half = side // 2
    own = lax.broadcasted_iota(jnp.int32, (CORNERS, chan), 0) == pl.program_id(0)
    corners = [
        jnp.sum(jnp.where(own, ref[...].astype(F32), 0.0), axis=0, keepdims=True)
        for ref in corner_refs
    ]
    padded[0, 0] = pad_refs[0][...]
    padded[half, 1] = pad_refs[1][...]
    padded[0, 1] = ring_ref[0, 0]
    padded[1:half] = h_ref[0, 1 : side - 1].reshape(half - 1, 2, side, chan)
    padded[half, 0] = ring_ref[0, 1]
    ends[0] = ring_ref[0, 2].astype(F32)
    ends[1] = ring_ref[0, 3].astype(F32)
    rows = lax.broadcasted_iota(jnp.int32, (16, chan), 0)
    for row in range(1, side - 1):
        m, e = (row + 1) // 2, (row + 1) % 2
        for at, first, last in ((0, 0, 0), (1, side - 16, 15)):
            old = h_ref[0, row, first : first + 16].astype(F32)
            new = jnp.where(rows == last, ends[at, row : row + 1], old)
            padded[m, e, first : first + 16] = new.astype(BF16)
    moved_columns([pad_refs[2][...], pad_refs[3][...]], corners, w_side_ref, ends)
    per_piece = x_ref.shape[2]

    def finish(row, value):
        at = row * side // per_piece
        if per_piece >= side:
            start = row * side % per_piece
            centre = x_ref[at, 0, start : start + side].astype(F32)
        else:
            count = side // per_piece
            centre = x_ref[at : at + count].reshape(side, chan).astype(F32)
        out_ref[0, row] = (centre + value).astype(BF16)

    convolve_tile(padded, w_ref, b_ref[...], y, ends, finish)


def paired_weights(weight):
    chan_in, chan_out = weight.shape[2:]
    by_tap = weight.transpose(0, 2, 1, 3).reshape(3, chan_in, 3 * chan_out)
    zero = jnp.zeros((1, chan_in, 3 * chan_out), weight.dtype)
    first = jnp.concatenate([by_tap, zero], 0)
    second = jnp.concatenate([zero, by_tap], 0)
    return jnp.stack([first, second], 2).reshape(4 * chan_in, 6 * chan_out)


def side_weights(weight):
    chan_in, chan_out = weight.shape[2:]
    return jnp.stack([weight[:, 0], weight[:, 2]], 0).reshape(2, 3 * chan_in, chan_out)


def edge_weights(weight):
    chan_in, chan_out = weight.shape[2:]
    turned = weight.transpose(1, 0, 2, 3)
    stacked = jnp.stack([weight, weight[::-1], turned, turned[::-1]], 0)
    return stacked.reshape(4, 9 * chan_in, chan_out)


def along(array, axis, step):
    size = lax.axis_size(axis)
    return lax.ppermute(array, axis, [(i, (i + step) % size) for i in range(size)])


def relay(message, upper, lower, split, at):
    group = slice(split + at * CORNERS, split + (at + 1) * CORNERS)
    return jnp.concatenate([message[:split], upper[group], lower[group]], 0)


def shards(latitude_rows, tile_order, neighbours, rotations, w_first, b_first, w_second, b_second):
    devices = lax.axis_size("face") * lax.axis_size("tile")
    tiles = neighbours.shape[0]
    piece, chan = latitude_rows.shape[1:]
    side = int(round((piece * devices) ** 0.5))
    vmem_spec = pl.BlockSpec(memory_space=VMEM)
    smem_spec = pl.BlockSpec(memory_space=pltpu.SMEM)
    hbm_spec = pl.BlockSpec(memory_space=pltpu.HBM)
    params = pltpu.CompilerParams(vmem_limit_bytes=LIMIT)

    asked = (neighbours % tiles * 4 + rotations).reshape(1, tiles * 8)
    after, before = along(asked, "face", -1), along(asked, "face", 1)

    groups = 8 if latitude_rows.shape[0] % 8 == 0 else 1
    ordered = pl.pallas_call(
        gather_kernel,
        in_specs=[smem_spec, hbm_spec],
        out_specs=hbm_spec,
        out_shape=jax.ShapeDtypeStruct(latitude_rows.shape, latitude_rows.dtype),
        scratch_shapes=[
            VMEM(latitude_rows.shape, latitude_rows.dtype),
            pltpu.SemaphoreType.DMA((groups,)),
            pltpu.SemaphoreType.DMA,
        ],
        compiler_params=params,
        name="order",
    )(tile_order, latitude_rows)
    ordered, after, before = lax.optimization_barrier((ordered, after, before))
    gathered = lax.all_to_all(ordered, AXES, split_axis=0, concat_axis=0, tiled=True)
    column = jnp.concatenate([asked, after, before], 0)
    on, back = along(column, "tile", -1), along(column, "tile", 1)
    asked = jnp.concatenate(
        [after, before] + [side_rows[i : i + 1] for i in range(3) for side_rows in (on, back)], 0
    ).reshape(8, tiles, 8)
    turn = (asked % 4)[..., None] == jnp.arange(4, dtype=jnp.int32)
    strip = jnp.sum(jnp.where(turn, jnp.asarray(STRIP_TABLE), 0), -1)
    flip = jnp.sum(jnp.where(turn, jnp.asarray(FLIP_TABLE), 0), -1)
    codes = ((flip * tiles + asked // 4) * 4 + strip).reshape(8, tiles * 8)
    constants = (
        paired_weights(w_first),
        paired_weights(w_second),
        side_weights(w_second),
        edge_weights(w_first),
        b_first.reshape(1, chan),
        b_second.reshape(1, chan),
    )
    gathered, codes, constants = lax.optimization_barrier((gathered, codes, constants))
    w_one, w_two, w_side, w_edges, b_one, b_two = constants
    pieces = gathered.reshape(devices, tiles, piece, chan)

    split = tiles * side
    message_shape = jax.ShapeDtypeStruct((split + 2 * CORNERS, chan), BF16)
    line_shape = (tiles, 8, side, chan)
    lines_scratch = VMEM((8 * tiles, side, chan), BF16)
    if piece >= 2 * side:
        count = piece // side
        view = gathered.reshape(devices, tiles, count, side, chan)
        border_specs = [
            pl.BlockSpec((1, 1, count, side, chan), lambda t: (0, t, 0, 0, 0)),
            pl.BlockSpec((1, 1, count, side, chan), lambda t: (devices - 1, t, 0, 0, 0)),
            pl.BlockSpec((devices, 1, count, 16, chan), lambda t: (0, t, 0, 0, 0)),
            pl.BlockSpec((devices, 1, count, 16, chan), lambda t: (0, t, 0, side // 16 - 1, 0)),
        ]
    else:
        count = side // piece
        view = gathered.reshape(side, count, tiles, piece, chan)
        border_specs = [
            pl.BlockSpec((2, count, 1, piece, chan), lambda t: (0, 0, t, 0, 0)),
            pl.BlockSpec((2, count, 1, piece, chan), lambda t: (side // 2 - 1, 0, t, 0, 0)),
            pl.BlockSpec((side, 1, 1, 16, chan), lambda t: (0, 0, t, 0, 0)),
            pl.BlockSpec((side, 1, 1, 16, chan), lambda t: (0, count - 1, t, piece // 16 - 1, 0)),
        ]
    ring, *sends = pl.pallas_call(
        functools.partial(border_kernel, side, tiles),
        grid=(tiles,),
        in_specs=[smem_spec] + border_specs,
        out_specs=[pl.BlockSpec((1,) + line_shape[1:], lambda t: (t, 0, 0, 0))]
        + [pl.BlockSpec(message_shape.shape, lambda t: (0, 0))] * 4,
        out_shape=[jax.ShapeDtypeStruct(line_shape, BF16)] + [message_shape] * 4,
        scratch_shapes=[lines_scratch],
        compiler_params=params,
        name="borders",
    )(codes, view, view, view, view)

    def whole(array):
        return pl.BlockSpec(array.shape, lambda t: (0,) * array.ndim)

    blocks = 4
    field = VMEM((side // 2 + 1, 2, side, chan), BF16)
    products = VMEM((blocks, side // 2 // blocks * side, 6 * chan), F32)
    field_shape = jax.ShapeDtypeStruct((tiles, side, side, chan), BF16)

    def first(begin, end, hidden):
        return pl.pallas_call(
            functools.partial(first_kernel, side),
            grid=(end - begin,),
            in_specs=[
                pl.BlockSpec((devices, 1, piece, chan), lambda t: (0, begin + t, 0, 0)),
                whole(w_one),
                whole(b_one),
            ]
            + [hbm_spec] * len(hidden),
            out_specs=pl.BlockSpec((1, side, side, chan), lambda t: (begin + t, 0, 0, 0)),
            out_shape=field_shape,
            input_output_aliases={3: 0} if hidden else {},
            scratch_shapes=[field, products],
            compiler_params=params,
            name="first",
        )(pieces, w_one, b_one, *hidden)

    upper, lower = along(sends[0], "face", 1), along(sends[1], "face", -1)
    middle = tiles // 2
    hidden = first(0, middle, ()) if middle else None
    upper, lower, hidden = lax.optimization_barrier((upper, lower, hidden))
    right = along(relay(sends[2], upper, lower, split, 0), "tile", 1)
    left = along(relay(sends[3], upper, lower, split, 1), "tile", -1)
    hidden = first(middle, tiles, (hidden,) if middle else ())
    right, left, hidden = lax.optimization_barrier((right, left, hidden))

    *sends, hidden_ring = pl.pallas_call(
        ring_kernel,
        in_specs=[smem_spec] + [vmem_spec] * 7,
        out_specs=[vmem_spec] * 5,
        out_shape=[message_shape] * 4 + [jax.ShapeDtypeStruct((tiles, 4, side, chan), BF16)],
        scratch_shapes=[lines_scratch],
        compiler_params=params,
        name="hidden_ring",
    )(codes, ring, w_edges, b_one, upper, lower, right, left)
    upper, lower = along(sends[0], "face", 1), along(sends[1], "face", -1)
    right = along(relay(sends[2], upper, lower, split, 0), "tile", 1)
    left = along(relay(sends[3], upper, lower, split, 1), "tile", -1)

    def group(at):
        return pl.BlockSpec((CORNERS, chan), lambda t: (split // CORNERS + at, 0))

    return pl.pallas_call(
        functools.partial(second_kernel, side),
        grid=(tiles,),
        in_specs=[
            pl.BlockSpec((devices, 1, piece, chan), lambda t: (0, t, 0, 0)),
            pl.BlockSpec((1, side, side, chan), lambda t: (t, 0, 0, 0)),
            pl.BlockSpec((1, 4, side, chan), lambda t: (t, 0, 0, 0)),
        ]
        + [pl.BlockSpec((side, chan), lambda t: (t, 0))] * 4
        + [group(0), group(0), group(1), group(1)]
        + [whole(w_two), whole(w_side), whole(b_two)],
        out_specs=pl.BlockSpec((1, side, side, chan), lambda t: (t, 0, 0, 0)),
        out_shape=field_shape,
        scratch_shapes=[field, products, VMEM((2, side, chan), F32)],
        compiler_params=params,
        name="second",
    )(
        pieces,
        hidden,
        hidden_ring,
        upper,
        lower,
        right,
        left,
        right,
        left,
        right,
        left,
        w_two,
        w_side,
        b_two,
    )


def solution(mesh):
    return jax.shard_map(
        shards,
        mesh=mesh,
        in_specs=(
            P(None, ("face", "tile"), None),
            P(),
            P(("face", "tile"), None),
            P(("face", "tile"), None),
            P(),
            P(),
            P(),
            P(),
        ),
        out_specs=P(("face", "tile"), None, None, None),
        check_vma=False,
    )
```

```python
import functools

import jax
import jax.numpy as jnp
import numpy as np
from jax import lax
from jax.experimental import pallas as pl
from jax.experimental.pallas import tpu as pltpu
from jax.sharding import PartitionSpec as P

STRIP_TABLE = np.array(
    [
        [1, 2, 0, 3],
        [0, 3, 1, 2],
        [3, 1, 2, 0],
        [2, 0, 3, 1],
        [1, 2, 0, 3],
        [1, 2, 0, 3],
        [0, 3, 1, 2],
        [0, 3, 1, 2],
    ],
    np.int32,
)
FLIP_TABLE = np.array(
    [
        [0, 0, 1, 1],
        [0, 0, 1, 1],
        [0, 1, 1, 0],
        [0, 1, 1, 0],
        [0, 0, 1, 1],
        [0, 0, 1, 1],
        [0, 0, 1, 1],
        [0, 0, 1, 1],
    ],
    np.int32,
)
DIRECTIONS = [(-1, 0), (1, 0), (0, -1), (0, 1), (-1, -1), (-1, 1), (1, -1), (1, 1)]
AXES = ("face", "tile")
VMEM = pltpu.VMEM
F32 = jnp.float32
BF16 = jnp.bfloat16
LIMIT = 24 * 1024 * 1024
WIDE_LIMIT = 60 * 1024 * 1024
CORNERS = 16


def shift_down(line, first):
    moved = pltpu.roll(line, 1, 0)
    rows = lax.broadcasted_iota(jnp.int32, moved.shape, 0)
    return jnp.where(rows == 0, first, moved)


def shift_up(line, last):
    size = line.shape[0]
    moved = pltpu.roll(line, size - 1, 0)
    rows = lax.broadcasted_iota(jnp.int32, moved.shape, 0)
    return jnp.where(rows == size - 1, last, moved)


def gelu(value):
    return (0.5 * value) * (1.0 + lax.erf(value * np.float32(np.sqrt(0.5))))


def pick_lines(codes_ref, lines, message_refs, tiles):
    side = lines.shape[1]
    shape = (CORNERS, lines.shape[2])
    rows = lax.broadcasted_iota(jnp.int32, shape, 0)
    for direction in range(8):
        corner = jnp.zeros(shape, F32)
        for tile in range(tiles):
            line = lines[codes_ref[direction, tile * 8 + direction]]
            if direction < 4:
                message_refs[direction][pl.ds(tile * side, side), :] = line
            else:
                at = side - 1 if direction in (4, 6) else 0
                pixel = line.astype(F32)[at : at + 1]
                corner = jnp.where(rows == tile, pixel, corner)
        if direction >= 4:
            group = tiles * side + (direction % 2) * CORNERS
            message_refs[direction // 2 - 2][pl.ds(group, CORNERS), :] = corner.astype(BF16)


def flip_line(line):
    size = line.shape[0]
    row = lax.broadcasted_iota(jnp.int32, (size, size), 0)
    col = lax.broadcasted_iota(jnp.int32, (size, size), 1)
    turn = jnp.where(row + col == size - 1, 1.0, 0.0).astype(BF16)
    return jnp.dot(turn, line, preferred_element_type=F32).astype(BF16)


def gather_kernel(order_ref, x_ref, o_ref, held, in_sems, out_sem):
    groups = in_sems.shape[0]
    size = held.shape[0] // groups

    def start(at, carry):
        pltpu.make_async_copy(
            x_ref.at[order_ref[at]], held.at[at], in_sems.at[at // size]
        ).start()
        return carry

    lax.fori_loop(0, held.shape[0], start, 0)
    for group in range(groups):
        part = pl.ds(group * size, size)
        pltpu.make_async_copy(x_ref.at[part], held.at[part], in_sems.at[group]).wait()
        pltpu.make_async_copy(held.at[part], o_ref.at[part], out_sem).start()
    pltpu.make_async_copy(held, o_ref, out_sem).wait()


def border_kernel(side, tiles, codes_ref, top_ref, low_ref, left_ref, right_ref, ring_ref, *rest):
    message_refs, lines = rest[:4], rest[4]
    tile = pl.program_id(0)
    chan = ring_ref.shape[-1]
    top = top_ref[...].reshape(-1, side, chan)
    low = low_ref[...].reshape(-1, side, chan)
    ring = [top[0], top[1], low[low.shape[0] - 2], low[low.shape[0] - 1]]
    low = left_ref[...].reshape(side, 16, chan).astype(F32)
    high = right_ref[...].reshape(side, 16, chan).astype(F32)
    ring += [v.astype(BF16) for v in (low[:, 0], low[:, 1], high[:, 14], high[:, 15])]
    for at, line in enumerate(ring):
        ring_ref[0, at] = line
    for strip, at in enumerate((0, 3, 4, 7)):
        lines[tile * 4 + strip] = ring[at]
        lines[tiles * 4 + tile * 4 + strip] = flip_line(ring[at])

    @pl.when(tile == tiles - 1)
    def _():
        pick_lines(codes_ref, lines, message_refs, tiles)


def ring_kernel(codes_ref, ring_ref, w_ref, b_ref, *rest):
    got_refs, message_refs, own_ref, lines = rest[:4], rest[4:8], rest[8], rest[9]
    tiles = ring_ref.shape[0]
    side = ring_ref.shape[2]
    pads = [[ref[pl.ds(t * side, side), :] for t in range(tiles)] for ref in got_refs]
    corners = [
        got_refs[2 + k % 2][pl.ds(tiles * side + k // 2 * CORNERS, CORNERS), :].astype(F32)
        for k in range(4)
    ]
    plans = [
        (0, 0, 1, 0, 1, 2, 3, 0, 1),
        (1, 2, 3, 3, 2, 2, 3, side - 1, side - 2),
        (2, 0, 2, 4, 5, 0, 1, 0, 1),
        (3, 1, 3, 7, 6, 0, 1, side - 1, side - 2),
    ]
    for edge, (pad, c_first, c_last, line_0, line_1, end_a, end_b, at_0, at_1) in enumerate(plans):
        stacked = []
        for tile in range(tiles):
            begin = pads[end_a][tile].astype(F32)
            finish = pads[end_b][tile].astype(F32)
            parts = []
            for line, first, last in (
                (
                    pads[pad][tile],
                    corners[c_first][tile : tile + 1],
                    corners[c_last][tile : tile + 1],
                ),
                (ring_ref[tile, line_0], begin[at_0 : at_0 + 1], finish[at_0 : at_0 + 1]),
                (ring_ref[tile, line_1], begin[at_1 : at_1 + 1], finish[at_1 : at_1 + 1]),
            ):
                wide = line.astype(F32)
                parts += [
                    shift_down(wide, first).astype(BF16),
                    line,
                    shift_up(wide, last).astype(BF16),
                ]
            stacked.append(jnp.concatenate(parts, axis=1))
        summed = jnp.dot(
            jnp.concatenate(stacked, axis=0), w_ref[edge], preferred_element_type=F32
        )
        hidden = gelu(summed + b_ref[...]).astype(BF16)
        for tile in range(tiles):
            line = hidden[tile * side : (tile + 1) * side]
            own_ref[tile, edge] = line
            lines[tile * 4 + edge] = line
            lines[tiles * 4 + tile * 4 + edge] = flip_line(line)
    pick_lines(codes_ref, lines, message_refs, tiles)


def moved_columns(pads, corners, w_side_ref, ends):
    for at in range(2):
        taps = jnp.concatenate(
            [
                shift_down(pads[at].astype(F32), corners[at]).astype(BF16),
                pads[at],
                shift_up(pads[at].astype(F32), corners[2 + at]).astype(BF16),
            ],
            axis=1,
        )
        ends[at] = jnp.dot(taps, w_side_ref[at], preferred_element_type=F32)


def read_row(x_ref, row, side):
    piece = x_ref.shape[2]
    at = row * side // piece
    if piece >= side:
        start = row * side % piece
        return x_ref[at, 0, start : start + side]
    return x_ref[at : at + side // piece].reshape(side, x_ref.shape[3])


def convolve_tile(padded, prepare, w_ref, bias, y, ends, finish):
    side = padded.shape[2]
    chan = padded.shape[3]
    blocks = y.shape[0]
    step = side // 2 // blocks
    rows = lax.broadcasted_iota(jnp.int32, (side, chan), 0)

    def multiply(block):
        begin = 2 * step * block
        for row in range(begin + 1 if block else -1, begin + 2 * step + 1):
            prepare(row)
        lhs = jnp.concatenate(
            [
                padded[pl.ds(step * block + j // 2, step), j % 2].reshape(step * side, chan)
                for j in range(4)
            ],
            axis=1,
        )
        y[block] = jnp.dot(lhs, w_ref[...], preferred_element_type=F32)

    multiply(0)
    for block in range(blocks):
        if block + 1 < blocks:
            multiply(block + 1)
        for i in range(step):
            for half in range(2):
                row = (block * step + i) * 2 + half
                a, b, c = (
                    y[block, pl.ds(i * side, side), pl.ds((half * 3 + dx) * chan, chan)]
                    for dx in range(3)
                )
                a = pltpu.roll(a, 1, 0)
                c = pltpu.roll(c, side - 1, 0)
                if ends is not None:
                    a = jnp.where(rows == 0, ends[0, row : row + 1], a)
                    c = jnp.where(rows == side - 1, ends[1, row : row + 1], c)
                finish(row, (a + c) + (b + bias))


def first_kernel(side, *refs):
    x_ref, w_ref, b_ref = refs[:3]
    out_ref, padded, y = refs[-3:]

    def prepare(row):
        if 0 <= row < side:
            line = read_row(x_ref, row, side)
        else:
            line = jnp.zeros(padded.shape[2:], BF16)
        padded[(row + 1) // 2, (row + 1) % 2] = line

    def finish(row, value):
        out_ref[0, row] = gelu(value).astype(BF16)

    convolve_tile(padded, prepare, w_ref, b_ref[...], y, None, finish)


def second_kernel(side, x_ref, h_ref, ring_ref, *rest):
    pad_refs, corner_refs = rest[:4], rest[4:8]
    w_ref, w_side_ref, b_ref, out_ref, padded, y, ends, columns = rest[8:]
    chan = x_ref.shape[-1]
    own = lax.broadcasted_iota(jnp.int32, (CORNERS, chan), 0) == pl.program_id(0)
    corners = [
        jnp.sum(jnp.where(own, ref[...].astype(F32), 0.0), axis=0, keepdims=True)
        for ref in corner_refs
    ]
    columns[0] = ring_ref[0, 2].astype(F32)
    columns[1] = ring_ref[0, 3].astype(F32)
    rows = lax.broadcasted_iota(jnp.int32, (16, chan), 0)

    def prepare(row):
        m, e = (row + 1) // 2, (row + 1) % 2
        if row < 0 or row == side:
            padded[m, e] = pad_refs[0 if row < 0 else 1][...]
        elif row == 0 or row == side - 1:
            padded[m, e] = ring_ref[0, 0 if row == 0 else 1]
        else:
            padded[m, e, 16 : side - 16] = h_ref[0, row, 16 : side - 16]
            for at, begin, place in ((0, 0, 0), (1, side - 16, 15)):
                old = h_ref[0, row, begin : begin + 16].astype(F32)
                new = jnp.where(rows == place, columns[at, row : row + 1], old)
                padded[m, e, begin : begin + 16] = new.astype(BF16)

    moved_columns([pad_refs[2][...], pad_refs[3][...]], corners, w_side_ref, ends)

    def finish(row, value):
        centre = read_row(x_ref, row, side).astype(F32)
        out_ref[0, row] = (centre + value).astype(BF16)

    convolve_tile(padded, prepare, w_ref, b_ref[...], y, ends, finish)


def paired_weights(weight):
    chan_in, chan_out = weight.shape[2:]
    by_tap = weight.transpose(0, 2, 1, 3).reshape(3, chan_in, 3 * chan_out)
    zero = jnp.zeros((1, chan_in, 3 * chan_out), weight.dtype)
    first = jnp.concatenate([by_tap, zero], 0)
    second = jnp.concatenate([zero, by_tap], 0)
    return jnp.stack([first, second], 2).reshape(4 * chan_in, 6 * chan_out)


def side_weights(weight):
    chan_in, chan_out = weight.shape[2:]
    return jnp.stack([weight[:, 0], weight[:, 2]], 0).reshape(2, 3 * chan_in, chan_out)


def edge_weights(weight):
    chan_in, chan_out = weight.shape[2:]
    turned = weight.transpose(1, 0, 2, 3)
    stacked = jnp.stack([weight, weight[::-1], turned, turned[::-1]], 0)
    return stacked.reshape(4, 9 * chan_in, chan_out)


def along(array, axis, step):
    size = lax.axis_size(axis)
    return lax.ppermute(array, axis, [(i, (i + step) % size) for i in range(size)])


def relay(message, upper, lower, split, at):
    group = slice(split + at * CORNERS, split + (at + 1) * CORNERS)
    return jnp.concatenate([message[:split], upper[group], lower[group]], 0)


def shards(latitude_rows, tile_order, neighbours, rotations, w_first, b_first, w_second, b_second):
    devices = lax.axis_size("face") * lax.axis_size("tile")
    tiles = neighbours.shape[0]
    piece, chan = latitude_rows.shape[1:]
    side = int(round((piece * devices) ** 0.5))
    vmem_spec = pl.BlockSpec(memory_space=VMEM)
    smem_spec = pl.BlockSpec(memory_space=pltpu.SMEM)
    hbm_spec = pl.BlockSpec(memory_space=pltpu.HBM)
    params = pltpu.CompilerParams(vmem_limit_bytes=LIMIT)

    asked = (neighbours % tiles * 4 + rotations).reshape(1, tiles * 8)
    after, before = along(asked, "face", -1), along(asked, "face", 1)

    groups = 8 if latitude_rows.shape[0] % 8 == 0 else 1
    ordered = pl.pallas_call(
        gather_kernel,
        in_specs=[smem_spec, hbm_spec],
        out_specs=hbm_spec,
        out_shape=jax.ShapeDtypeStruct(latitude_rows.shape, latitude_rows.dtype),
        scratch_shapes=[
            VMEM(latitude_rows.shape, latitude_rows.dtype),
            pltpu.SemaphoreType.DMA((groups,)),
            pltpu.SemaphoreType.DMA,
        ],
        compiler_params=pltpu.CompilerParams(vmem_limit_bytes=WIDE_LIMIT),
        name="order",
    )(tile_order, latitude_rows)
    ordered, after, before = lax.optimization_barrier((ordered, after, before))
    gathered = lax.all_to_all(ordered, AXES, split_axis=0, concat_axis=0, tiled=True)
    column = jnp.concatenate([asked, after, before], 0)
    on, back = along(column, "tile", -1), along(column, "tile", 1)
    asked = jnp.concatenate(
        [after, before] + [side_rows[i : i + 1] for i in range(3) for side_rows in (on, back)], 0
    ).reshape(8, tiles, 8)
    turn = (asked % 4)[..., None] == jnp.arange(4, dtype=jnp.int32)
    strip = jnp.sum(jnp.where(turn, jnp.asarray(STRIP_TABLE), 0), -1)
    flip = jnp.sum(jnp.where(turn, jnp.asarray(FLIP_TABLE), 0), -1)
    codes = ((flip * tiles + asked // 4) * 4 + strip).reshape(8, tiles * 8)
    constants = (
        paired_weights(w_first),
        paired_weights(w_second),
        side_weights(w_second),
        edge_weights(w_first),
        b_first.reshape(1, chan),
        b_second.reshape(1, chan),
    )
    gathered, codes, constants = lax.optimization_barrier((gathered, codes, constants))
    w_one, w_two, w_side, w_edges, b_one, b_two = constants
    pieces = gathered.reshape(devices, tiles, piece, chan)

    split = tiles * side
    message_shape = jax.ShapeDtypeStruct((split + 2 * CORNERS, chan), BF16)
    line_shape = (tiles, 8, side, chan)
    lines_scratch = VMEM((8 * tiles, side, chan), BF16)
    if piece >= 2 * side:
        count = piece // side
        view = gathered.reshape(devices, tiles, count, side, chan)
        border_specs = [
            pl.BlockSpec((1, 1, count, side, chan), lambda t: (0, t, 0, 0, 0)),
            pl.BlockSpec((1, 1, count, side, chan), lambda t: (devices - 1, t, 0, 0, 0)),
            pl.BlockSpec((devices, 1, count, 16, chan), lambda t: (0, t, 0, 0, 0)),
            pl.BlockSpec((devices, 1, count, 16, chan), lambda t: (0, t, 0, side // 16 - 1, 0)),
        ]
    else:
        count = side // piece
        view = gathered.reshape(side, count, tiles, piece, chan)
        border_specs = [
            pl.BlockSpec((2, count, 1, piece, chan), lambda t: (0, 0, t, 0, 0)),
            pl.BlockSpec((2, count, 1, piece, chan), lambda t: (side // 2 - 1, 0, t, 0, 0)),
            pl.BlockSpec((side, 1, 1, 16, chan), lambda t: (0, 0, t, 0, 0)),
            pl.BlockSpec((side, 1, 1, 16, chan), lambda t: (0, count - 1, t, piece // 16 - 1, 0)),
        ]
    ring, *sends = pl.pallas_call(
        functools.partial(border_kernel, side, tiles),
        grid=(tiles,),
        in_specs=[smem_spec] + border_specs,
        out_specs=[pl.BlockSpec((1,) + line_shape[1:], lambda t: (t, 0, 0, 0))]
        + [pl.BlockSpec(message_shape.shape, lambda t: (0, 0))] * 4,
        out_shape=[jax.ShapeDtypeStruct(line_shape, BF16)] + [message_shape] * 4,
        scratch_shapes=[lines_scratch],
        compiler_params=params,
        name="borders",
    )(codes, view, view, view, view)

    def whole(array):
        return pl.BlockSpec(array.shape, lambda t: (0,) * array.ndim)

    blocks = 4
    field = VMEM((side // 2 + 1, 2, side, chan), BF16)
    products = VMEM((blocks, side // 2 // blocks * side, 6 * chan), F32)
    field_shape = jax.ShapeDtypeStruct((tiles, side, side, chan), BF16)

    def first(begin, end, hidden):
        return pl.pallas_call(
            functools.partial(first_kernel, side),
            grid=(end - begin,),
            in_specs=[
                pl.BlockSpec((devices, 1, piece, chan), lambda t: (0, begin + t, 0, 0)),
                whole(w_one),
                whole(b_one),
            ]
            + [hbm_spec] * len(hidden),
            out_specs=pl.BlockSpec((1, side, side, chan), lambda t: (begin + t, 0, 0, 0)),
            out_shape=field_shape,
            input_output_aliases={3: 0} if hidden else {},
            scratch_shapes=[field, products],
            compiler_params=params,
            name="first",
        )(pieces, w_one, b_one, *hidden)

    ends = [(tiles * i // 4, tiles * (i + 1) // 4) for i in range(4)]
    hidden = ()

    def quarter(i, hidden):
        begin, end = ends[i]
        return (first(begin, end, hidden),) if end > begin else hidden

    upper = along(sends[0], "face", 1)
    hidden = quarter(0, hidden)
    send, hidden = lax.optimization_barrier((sends[1], hidden))
    lower = along(send, "face", -1)
    hidden = quarter(1, hidden)
    upper, lower, hidden = lax.optimization_barrier((upper, lower, hidden))
    right = along(relay(sends[2], upper, lower, split, 0), "tile", 1)
    hidden = quarter(2, hidden)
    send, hidden = lax.optimization_barrier((relay(sends[3], upper, lower, split, 1), hidden))
    left = along(send, "tile", -1)
    (hidden,) = quarter(3, hidden)
    right, left, hidden = lax.optimization_barrier((right, left, hidden))

    *sends, hidden_ring = pl.pallas_call(
        ring_kernel,
        in_specs=[smem_spec] + [vmem_spec] * 7,
        out_specs=[vmem_spec] * 5,
        out_shape=[message_shape] * 4 + [jax.ShapeDtypeStruct((tiles, 4, side, chan), BF16)],
        scratch_shapes=[lines_scratch],
        compiler_params=params,
        name="hidden_ring",
    )(codes, ring, w_edges, b_one, upper, lower, right, left)
    upper, lower = along(sends[0], "face", 1), along(sends[1], "face", -1)
    right = along(relay(sends[2], upper, lower, split, 0), "tile", 1)
    left = along(relay(sends[3], upper, lower, split, 1), "tile", -1)

    def group(at):
        return pl.BlockSpec((CORNERS, chan), lambda t: (split // CORNERS + at, 0))

    return pl.pallas_call(
        functools.partial(second_kernel, side),
        grid=(tiles,),
        in_specs=[
            pl.BlockSpec((devices, 1, piece, chan), lambda t: (0, t, 0, 0)),
            pl.BlockSpec((1, side, side, chan), lambda t: (t, 0, 0, 0)),
            pl.BlockSpec((1, 4, side, chan), lambda t: (t, 0, 0, 0)),
        ]
        + [pl.BlockSpec((side, chan), lambda t: (t, 0))] * 4
        + [group(0), group(0), group(1), group(1)]
        + [whole(w_two), whole(w_side), whole(b_two)],
        out_specs=pl.BlockSpec((1, side, side, chan), lambda t: (t, 0, 0, 0)),
        out_shape=field_shape,
        scratch_shapes=[field, products] + [VMEM((2, side, chan), F32)] * 2,
        compiler_params=params,
        name="second",
    )(
        pieces,
        hidden,
        hidden_ring,
        upper,
        lower,
        right,
        left,
        right,
        left,
        right,
        left,
        w_two,
        w_side,
        b_two,
    )


def solution(mesh):
    return jax.shard_map(
        shards,
        mesh=mesh,
        in_specs=(
            P(None, ("face", "tile"), None),
            P(),
            P(("face", "tile"), None),
            P(("face", "tile"), None),
            P(),
            P(),
            P(),
            P(),
        ),
        out_specs=P(("face", "tile"), None, None, None),
        check_vma=False,
    )
```

```python
import functools

import jax
import jax.numpy as jnp
import numpy as np
from jax import lax
from jax.experimental import pallas as pl
from jax.experimental.pallas import tpu as pltpu
from jax.sharding import PartitionSpec as P

STRIP_TABLE = np.array(
    [
        [1, 2, 0, 3],
        [0, 3, 1, 2],
        [3, 1, 2, 0],
        [2, 0, 3, 1],
        [1, 2, 0, 3],
        [1, 2, 0, 3],
        [0, 3, 1, 2],
        [0, 3, 1, 2],
    ],
    np.int32,
)
FLIP_TABLE = np.array(
    [
        [0, 0, 1, 1],
        [0, 0, 1, 1],
        [0, 1, 1, 0],
        [0, 1, 1, 0],
        [0, 0, 1, 1],
        [0, 0, 1, 1],
        [0, 0, 1, 1],
        [0, 0, 1, 1],
    ],
    np.int32,
)
DIRECTIONS = [(-1, 0), (1, 0), (0, -1), (0, 1), (-1, -1), (-1, 1), (1, -1), (1, 1)]
AXES = ("face", "tile")
VMEM = pltpu.VMEM
F32 = jnp.float32
BF16 = jnp.bfloat16
LIMIT = 32 * 1024 * 1024
WIDE_LIMIT = 60 * 1024 * 1024
CORNERS = 16


def shift_down(line, first):
    moved = pltpu.roll(line, 1, 0)
    rows = lax.broadcasted_iota(jnp.int32, moved.shape, 0)
    return jnp.where(rows == 0, first, moved)


def shift_up(line, last):
    size = line.shape[0]
    moved = pltpu.roll(line, size - 1, 0)
    rows = lax.broadcasted_iota(jnp.int32, moved.shape, 0)
    return jnp.where(rows == size - 1, last, moved)


def gelu(value):
    return (0.5 * value) * (1.0 + lax.erf(value * np.float32(np.sqrt(0.5))))


def pick_lines(codes_ref, lines, message_refs, tiles):
    side = lines.shape[1]
    shape = (CORNERS, lines.shape[2])
    rows = lax.broadcasted_iota(jnp.int32, shape, 0)
    for direction in range(8):
        corner = jnp.zeros(shape, F32)
        for tile in range(tiles):
            line = lines[codes_ref[direction, tile * 8 + direction]]
            if direction < 4:
                message_refs[direction][pl.ds(tile * side, side), :] = line
            else:
                at = side - 1 if direction in (4, 6) else 0
                pixel = line.astype(F32)[at : at + 1]
                corner = jnp.where(rows == tile, pixel, corner)
        if direction >= 4:
            group = tiles * side + (direction % 2) * CORNERS
            message_refs[direction // 2 - 2][pl.ds(group, CORNERS), :] = corner.astype(BF16)


def flip_line(line):
    size = line.shape[0]
    row = lax.broadcasted_iota(jnp.int32, (size, size), 0)
    col = lax.broadcasted_iota(jnp.int32, (size, size), 1)
    turn = jnp.where(row + col == size - 1, 1.0, 0.0).astype(BF16)
    return jnp.dot(turn, line, preferred_element_type=F32).astype(BF16)


def gather_kernel(order_ref, x_ref, o_ref, held, in_sems, out_sem):
    groups = in_sems.shape[0]
    size = held.shape[0] // groups

    def start(at, carry):
        pltpu.make_async_copy(
            x_ref.at[order_ref[at]], held.at[at], in_sems.at[at // size]
        ).start()
        return carry

    lax.fori_loop(0, held.shape[0], start, 0)
    for group in range(groups):
        part = pl.ds(group * size, size)
        pltpu.make_async_copy(x_ref.at[part], held.at[part], in_sems.at[group]).wait()
        pltpu.make_async_copy(held.at[part], o_ref.at[part], out_sem).start()
    pltpu.make_async_copy(held, o_ref, out_sem).wait()


def border_kernel(side, codes_ref, source, x_ref, ring_ref, *rest):
    message_refs, lines, sems = rest[:4], rest[4], rest[5]
    devices, tiles, piece, chan = x_ref.shape
    copies = [
        pltpu.make_async_copy(source.at[:, tile], x_ref.at[:, tile], sems.at[tile])
        for tile in range(tiles)
    ]
    for copy in copies:
        copy.start()
    for tile in range(tiles):
        copies[tile].wait()
        ring = [read_row(x_ref, tile, row, side) for row in (0, 1, side - 2, side - 1)]
        if piece >= side:
            low, high = (
                jnp.stack(
                    [
                        x_ref[:, tile, row * side + at : row * side + at + 16]
                        for row in range(piece // side)
                    ],
                    1,
                ).reshape(side, 16, chan)
                for at in (0, side - 16)
            )
        else:
            image = x_ref[:, tile].reshape(side, side // piece, piece, chan)
            low, high = image[:, 0, :16], image[:, -1, piece - 16 :]
        low, high = low.astype(F32), high.astype(F32)
        ring += [v.astype(BF16) for v in (low[:, 0], low[:, 1], high[:, 14], high[:, 15])]
        for at, line in enumerate(ring):
            ring_ref[tile, at] = line
        for strip, at in enumerate((0, 3, 4, 7)):
            lines[tile * 4 + strip] = ring[at]
            lines[tiles * 4 + tile * 4 + strip] = flip_line(ring[at])
    pick_lines(codes_ref, lines, message_refs, tiles)


def ring_kernel(codes_ref, ring_ref, w_ref, b_ref, *rest):
    got_refs, message_refs, own_ref, lines = rest[:4], rest[4:8], rest[8], rest[9]
    tiles = ring_ref.shape[0]
    side = ring_ref.shape[2]
    pads = [[ref[pl.ds(t * side, side), :] for t in range(tiles)] for ref in got_refs]
    corners = [
        got_refs[2 + k % 2][pl.ds(tiles * side + k // 2 * CORNERS, CORNERS), :].astype(F32)
        for k in range(4)
    ]
    plans = [
        (0, 0, 1, 0, 1, 2, 3, 0, 1),
        (1, 2, 3, 3, 2, 2, 3, side - 1, side - 2),
        (2, 0, 2, 4, 5, 0, 1, 0, 1),
        (3, 1, 3, 7, 6, 0, 1, side - 1, side - 2),
    ]
    for edge, (pad, c_first, c_last, line_0, line_1, end_a, end_b, at_0, at_1) in enumerate(plans):
        stacked = []
        for tile in range(tiles):
            begin = pads[end_a][tile].astype(F32)
            finish = pads[end_b][tile].astype(F32)
            parts = []
            for line, first, last in (
                (
                    pads[pad][tile],
                    corners[c_first][tile : tile + 1],
                    corners[c_last][tile : tile + 1],
                ),
                (ring_ref[tile, line_0], begin[at_0 : at_0 + 1], finish[at_0 : at_0 + 1]),
                (ring_ref[tile, line_1], begin[at_1 : at_1 + 1], finish[at_1 : at_1 + 1]),
            ):
                wide = line.astype(F32)
                parts += [
                    shift_down(wide, first).astype(BF16),
                    line,
                    shift_up(wide, last).astype(BF16),
                ]
            stacked.append(jnp.concatenate(parts, axis=1))
        summed = jnp.dot(
            jnp.concatenate(stacked, axis=0), w_ref[edge], preferred_element_type=F32
        )
        hidden = gelu(summed + b_ref[...]).astype(BF16)
        for tile in range(tiles):
            line = hidden[tile * side : (tile + 1) * side]
            own_ref[tile, edge] = line
            lines[tile * 4 + edge] = line
            lines[tiles * 4 + tile * 4 + edge] = flip_line(line)
    pick_lines(codes_ref, lines, message_refs, tiles)


def moved_columns(pads, corners, w_side_ref, ends):
    for at in range(2):
        taps = jnp.concatenate(
            [
                shift_down(pads[at].astype(F32), corners[at]).astype(BF16),
                pads[at],
                shift_up(pads[at].astype(F32), corners[2 + at]).astype(BF16),
            ],
            axis=1,
        )
        ends[at] = jnp.dot(taps, w_side_ref[at], preferred_element_type=F32)


def read_row(x_ref, tile, row, side):
    piece = x_ref.shape[2]
    at = row * side // piece
    if piece >= side:
        start = row * side % piece
        return x_ref[at, tile, start : start + side]
    return x_ref[at : at + side // piece, tile].reshape(side, x_ref.shape[3])


def convolve_tile(padded, prepare, w_ref, bias, y, ends, finish):
    side = padded.shape[2]
    chan = padded.shape[3]
    blocks = y.shape[0]
    step = side // 2 // blocks
    rows = lax.broadcasted_iota(jnp.int32, (side, chan), 0)

    def multiply(block):
        begin = 2 * step * block
        for row in range(begin + 1 if block else -1, begin + 2 * step + 1):
            prepare(row)
        lhs = jnp.concatenate(
            [
                padded[pl.ds(step * block + j // 2, step), j % 2].reshape(step * side, chan)
                for j in range(4)
            ],
            axis=1,
        )
        y[block] = jnp.dot(lhs, w_ref[...], preferred_element_type=F32)

    multiply(0)
    for block in range(blocks):
        if block + 1 < blocks:
            multiply(block + 1)
        for i in range(step):
            for half in range(2):
                row = (block * step + i) * 2 + half
                a, b, c = (
                    y[block, pl.ds(i * side, side), pl.ds((half * 3 + dx) * chan, chan)]
                    for dx in range(3)
                )
                a = pltpu.roll(a, 1, 0)
                c = pltpu.roll(c, side - 1, 0)
                if ends is not None:
                    a = jnp.where(rows == 0, ends[0, row : row + 1], a)
                    c = jnp.where(rows == side - 1, ends[1, row : row + 1], c)
                finish(row, (a + c) + (b + bias))


def first_kernel(side, tiles, *refs):
    x_ref, w_ref, b_ref = refs[:3]
    out_ref, padded, y = refs[-3:]
    for tile in tiles:

        def prepare(row):
            if 0 <= row < side:
                line = read_row(x_ref, tile, row, side)
            else:
                line = jnp.zeros(padded.shape[2:], BF16)
            padded[(row + 1) // 2, (row + 1) % 2] = line

        def finish(row, value):
            out_ref[tile, row] = gelu(value).astype(BF16)

        convolve_tile(padded, prepare, w_ref, b_ref[...], y, None, finish)


def second_kernel(side, x_ref, h_ref, ring_ref, *rest):
    got_refs, (w_ref, w_side_ref, b_ref), out_ref = rest[:4], rest[4:7], rest[7]
    padded, y, ends, columns, result, sem = rest[8:]
    tiles, chan = x_ref.shape[1], x_ref.shape[3]
    split = tiles * side
    blocks = y.shape[0]
    corner_rows = lax.broadcasted_iota(jnp.int32, (CORNERS, chan), 0)
    rows = lax.broadcasted_iota(jnp.int32, (16, chan), 0)
    bias = b_ref[...]

    def one_tile(tile, carry):
        def corner(k):
            group = got_refs[2 + k % 2][pl.ds(split + k // 2 * CORNERS, CORNERS), :]
            own = jnp.where(corner_rows == tile, group.astype(F32), 0.0)
            return jnp.sum(own, axis=0, keepdims=True)

        span = pl.ds(pl.multiple_of(tile * side, side), side)
        columns[0] = ring_ref[tile, 2].astype(F32)
        columns[1] = ring_ref[tile, 3].astype(F32)

        def prepare(row):
            m, e = (row + 1) // 2, (row + 1) % 2
            if row < 0 or row == side:
                padded[m, e] = got_refs[0 if row < 0 else 1][span, :]
            elif row == 0 or row == side - 1:
                padded[m, e] = ring_ref[tile, 0 if row == 0 else 1]
            else:
                padded[m, e, 16 : side - 16] = h_ref[tile, row, 16 : side - 16]
                for at, begin, place in ((0, 0, 0), (1, side - 16, 15)):
                    old = h_ref[tile, row, begin : begin + 16].astype(F32)
                    new = jnp.where(rows == place, columns[at, row : row + 1], old)
                    padded[m, e, begin : begin + 16] = new.astype(BF16)

        moved_columns(
            [got_refs[2][span, :], got_refs[3][span, :]],
            [corner(k) for k in range(4)],
            w_side_ref,
            ends,
        )
        size = side // blocks

        def finish(row, value):
            centre = read_row(x_ref, tile, row, side).astype(F32)
            result[tile, row] = (centre + value).astype(BF16)
            if (row + 1) % size == 0:
                part = pl.ds(row + 1 - size, size)
                pltpu.make_async_copy(
                    result.at[tile, part], out_ref.at[tile, part], sem
                ).start()

        convolve_tile(padded, prepare, w_ref, bias, y, ends, finish)
        return carry

    lax.fori_loop(0, tiles, one_tile, 0)
    pltpu.make_async_copy(result, out_ref, sem).wait()


def paired_weights(weight):
    chan_in, chan_out = weight.shape[2:]
    by_tap = weight.transpose(0, 2, 1, 3).reshape(3, chan_in, 3 * chan_out)
    zero = jnp.zeros((1, chan_in, 3 * chan_out), weight.dtype)
    first = jnp.concatenate([by_tap, zero], 0)
    second = jnp.concatenate([zero, by_tap], 0)
    return jnp.stack([first, second], 2).reshape(4 * chan_in, 6 * chan_out)


def side_weights(weight):
    chan_in, chan_out = weight.shape[2:]
    return jnp.stack([weight[:, 0], weight[:, 2]], 0).reshape(2, 3 * chan_in, chan_out)


def edge_weights(weight):
    chan_in, chan_out = weight.shape[2:]
    turned = weight.transpose(1, 0, 2, 3)
    stacked = jnp.stack([weight, weight[::-1], turned, turned[::-1]], 0)
    return stacked.reshape(4, 9 * chan_in, chan_out)


def along(array, axis, step):
    size = lax.axis_size(axis)
    return lax.ppermute(array, axis, [(i, (i + step) % size) for i in range(size)])


def relay(message, upper, lower, split, at):
    group = slice(split + at * CORNERS, split + (at + 1) * CORNERS)
    return jnp.concatenate([message[:split], upper[group], lower[group]], 0)


def shards(latitude_rows, tile_order, neighbours, rotations, w_first, b_first, w_second, b_second):
    devices = lax.axis_size("face") * lax.axis_size("tile")
    tiles = neighbours.shape[0]
    piece, chan = latitude_rows.shape[1:]
    side = int(round((piece * devices) ** 0.5))
    vmem_spec = pl.BlockSpec(memory_space=VMEM)
    smem_spec = pl.BlockSpec(memory_space=pltpu.SMEM)
    hbm_spec = pl.BlockSpec(memory_space=pltpu.HBM)
    params = pltpu.CompilerParams(vmem_limit_bytes=LIMIT)

    asked = (neighbours % tiles * 4 + rotations).reshape(1, tiles * 8)
    after, before = along(asked, "face", -1), along(asked, "face", 1)

    groups = 8 if latitude_rows.shape[0] % 8 == 0 else 1
    ordered = pl.pallas_call(
        gather_kernel,
        in_specs=[smem_spec, hbm_spec],
        out_specs=hbm_spec,
        out_shape=jax.ShapeDtypeStruct(latitude_rows.shape, latitude_rows.dtype),
        scratch_shapes=[
            VMEM(latitude_rows.shape, latitude_rows.dtype),
            pltpu.SemaphoreType.DMA((groups,)),
            pltpu.SemaphoreType.DMA,
        ],
        compiler_params=pltpu.CompilerParams(vmem_limit_bytes=WIDE_LIMIT),
        name="order",
    )(tile_order, latitude_rows)
    ordered, after, before = lax.optimization_barrier((ordered, after, before))
    gathered = lax.all_to_all(ordered, AXES, split_axis=0, concat_axis=0, tiled=True)
    column = jnp.concatenate([asked, after, before], 0)
    on, back = along(column, "tile", -1), along(column, "tile", 1)
    asked = jnp.concatenate(
        [after, before] + [side_rows[i : i + 1] for i in range(3) for side_rows in (on, back)], 0
    ).reshape(8, tiles, 8)
    turn = (asked % 4)[..., None] == jnp.arange(4, dtype=jnp.int32)
    strip = jnp.sum(jnp.where(turn, jnp.asarray(STRIP_TABLE), 0), -1)
    flip = jnp.sum(jnp.where(turn, jnp.asarray(FLIP_TABLE), 0), -1)
    codes = ((flip * tiles + asked // 4) * 4 + strip).reshape(8, tiles * 8)
    constants = (
        paired_weights(w_first),
        paired_weights(w_second),
        side_weights(w_second),
        edge_weights(w_first),
        b_first.reshape(1, chan),
        b_second.reshape(1, chan),
    )
    gathered, codes, constants = lax.optimization_barrier((gathered, codes, constants))
    w_one, w_two, w_side, w_edges, b_one, b_two = constants
    pieces = gathered.reshape(devices, tiles, piece, chan)

    split = tiles * side
    message_shape = jax.ShapeDtypeStruct((split + 2 * CORNERS, chan), BF16)
    line_shape = (tiles, 8, side, chan)
    lines_scratch = VMEM((8 * tiles, side, chan), BF16)
    x, ring, *sends = pl.pallas_call(
        functools.partial(border_kernel, side),
        in_specs=[smem_spec, hbm_spec],
        out_specs=[vmem_spec] * 6,
        out_shape=[
            jax.ShapeDtypeStruct(pieces.shape, BF16),
            jax.ShapeDtypeStruct((tiles, 8, side, chan), BF16),
        ]
        + [message_shape] * 4,
        scratch_shapes=[lines_scratch, pltpu.SemaphoreType.DMA((tiles,))],
        compiler_params=params,
        name="borders",
    )(codes, pieces)

    blocks = 4
    field = VMEM((side // 2 + 1, 2, side, chan), BF16)
    products = VMEM((blocks, side // 2 // blocks * side, 6 * chan), F32)
    field_shape = jax.ShapeDtypeStruct((tiles, side, side, chan), BF16)

    def first(part, hidden):
        return pl.pallas_call(
            functools.partial(first_kernel, side, part),
            in_specs=[vmem_spec] * (3 + len(hidden)),
            out_specs=vmem_spec,
            out_shape=field_shape,
            input_output_aliases={3: 0} if hidden else {},
            scratch_shapes=[field, products],
            compiler_params=params,
            name="first",
        )(x, w_one, b_one, *hidden)

    hidden = ()

    def quarter(i, hidden):
        part = range(tiles * i // 4, tiles * (i + 1) // 4)
        return (first(part, hidden),) if part else hidden

    def halo(sends, at, hidden):
        upper, lower = along(sends[0], "face", 1), along(sends[1], "face", -1)
        hidden = quarter(at, hidden)
        upper, lower, hidden = lax.optimization_barrier((upper, lower, hidden))
        right = along(relay(sends[2], upper, lower, split, 0), "tile", 1)
        left = along(relay(sends[3], upper, lower, split, 1), "tile", -1)
        hidden = quarter(at + 1, hidden)
        right, left, hidden = lax.optimization_barrier((right, left, hidden))
        return (upper, lower, right, left), hidden

    got_first, hidden = halo(sends, 0, hidden)
    *sends, hidden_ring = pl.pallas_call(
        ring_kernel,
        in_specs=[smem_spec] + [vmem_spec] * 7,
        out_specs=[vmem_spec] * 5,
        out_shape=[message_shape] * 4 + [jax.ShapeDtypeStruct((tiles, 4, side, chan), BF16)],
        scratch_shapes=[lines_scratch],
        compiler_params=params,
        name="hidden_ring",
    )(codes, ring, w_edges, b_one, *got_first)
    got_second, hidden = halo(sends, 2, hidden)

    return pl.pallas_call(
        functools.partial(second_kernel, side),
        in_specs=[vmem_spec] * 10,
        out_specs=hbm_spec,
        out_shape=field_shape,
        scratch_shapes=[
            field,
            products,
            VMEM((2, side, chan), F32),
            VMEM((2, side, chan), F32),
            VMEM(field_shape.shape, BF16),
            pltpu.SemaphoreType.DMA,
        ],
        compiler_params=params,
        name="second",
    )(x, *hidden, hidden_ring, *got_second, w_two, w_side, b_two)


def solution(mesh):
    return jax.shard_map(
        shards,
        mesh=mesh,
        in_specs=(
            P(None, ("face", "tile"), None),
            P(),
            P(("face", "tile"), None),
            P(("face", "tile"), None),
            P(),
            P(),
            P(),
            P(),
        ),
        out_specs=P(("face", "tile"), None, None, None),
        check_vma=False,
    )
```

```python
import functools

import jax
import jax.numpy as jnp
import numpy as np
from jax import lax
from jax.experimental import pallas as pl
from jax.experimental.pallas import tpu as pltpu
from jax.sharding import PartitionSpec as P

STRIP_TABLE = np.array(
    [
        [1, 2, 0, 3],
        [0, 3, 1, 2],
        [3, 1, 2, 0],
        [2, 0, 3, 1],
        [1, 2, 0, 3],
        [1, 2, 0, 3],
        [0, 3, 1, 2],
        [0, 3, 1, 2],
    ],
    np.int32,
)
FLIP_TABLE = np.array(
    [
        [0, 0, 1, 1],
        [0, 0, 1, 1],
        [0, 1, 1, 0],
        [0, 1, 1, 0],
        [0, 0, 1, 1],
        [0, 0, 1, 1],
        [0, 0, 1, 1],
        [0, 0, 1, 1],
    ],
    np.int32,
)
DIRECTIONS = [(-1, 0), (1, 0), (0, -1), (0, 1), (-1, -1), (-1, 1), (1, -1), (1, 1)]
AXES = ("face", "tile")
VMEM = pltpu.VMEM
F32 = jnp.float32
BF16 = jnp.bfloat16
LIMIT = 32 * 1024 * 1024
WIDE_LIMIT = 60 * 1024 * 1024
CORNERS = 16


def shift_down(line, first):
    moved = pltpu.roll(line, 1, 0)
    rows = lax.broadcasted_iota(jnp.int32, moved.shape, 0)
    return jnp.where(rows == 0, first, moved)


def shift_up(line, last):
    size = line.shape[0]
    moved = pltpu.roll(line, size - 1, 0)
    rows = lax.broadcasted_iota(jnp.int32, moved.shape, 0)
    return jnp.where(rows == size - 1, last, moved)


def gelu(value):
    return (0.5 * value) * (1.0 + lax.erf(value * np.float32(np.sqrt(0.5))))


def pick_lines(codes_ref, lines, picked, message_refs, tiles):
    side = lines.shape[1]
    shape = (CORNERS, lines.shape[2])
    rows = lax.broadcasted_iota(jnp.int32, shape, 0)
    for direction in range(8):
        corner = jnp.zeros(shape, F32)
        for tile in range(tiles):
            line = lines[codes_ref[direction, tile * 8 + direction]]
            if direction < 4:
                picked[direction, pl.ds(tile * side, side), :] = line
            else:
                at = side - 1 if direction in (4, 6) else 0
                pixel = line.astype(F32)[at : at + 1]
                corner = jnp.where(rows == tile, pixel, corner)
        if direction >= 4:
            group = tiles * side + (direction % 2) * CORNERS
            picked[direction // 2 - 2, pl.ds(group, CORNERS), :] = corner.astype(BF16)
            picked[direction // 2, pl.ds(group, CORNERS), :] = jnp.zeros(shape, BF16)
    for axis in range(2):
        odd = codes_ref[8, axis]
        message_refs[2 * axis][...] = picked[2 * axis + odd]
        message_refs[2 * axis + 1][...] = picked[2 * axis + 1 - odd]


def in_order(odd, first_ref, second_ref):
    first, second = first_ref[...], second_ref[...]
    return jnp.where(odd == 1, first, second), jnp.where(odd == 1, second, first)


def flip_line(line):
    size = line.shape[0]
    row = lax.broadcasted_iota(jnp.int32, (size, size), 0)
    col = lax.broadcasted_iota(jnp.int32, (size, size), 1)
    turn = jnp.where(row + col == size - 1, 1.0, 0.0).astype(BF16)
    return jnp.dot(turn, line, preferred_element_type=F32).astype(BF16)


def gather_kernel(order_ref, x_ref, o_ref, held, in_sems, out_sem):
    groups = in_sems.shape[0]
    size = held.shape[0] // groups

    def start(at, carry):
        pltpu.make_async_copy(
            x_ref.at[order_ref[at]], held.at[at], in_sems.at[at // size]
        ).start()
        return carry

    lax.fori_loop(0, held.shape[0], start, 0)
    for group in range(groups):
        part = pl.ds(group * size, size)
        pltpu.make_async_copy(x_ref.at[part], held.at[part], in_sems.at[group]).wait()
        pltpu.make_async_copy(held.at[part], o_ref.at[part], out_sem).start()
    pltpu.make_async_copy(held, o_ref, out_sem).wait()


def border_kernel(side, codes_ref, source, fields, ring_ref, *rest):
    x_ref = fields.at[0]
    message_refs, lines, picked, sems = rest[:4], rest[4], rest[5], rest[6]
    devices, tiles, piece, chan = x_ref.shape
    copies = [
        pltpu.make_async_copy(source.at[:, tile], x_ref.at[:, tile], sems.at[tile])
        for tile in range(tiles)
    ]
    for copy in copies:
        copy.start()
    for tile in range(tiles):
        copies[tile].wait()
        ring = [read_row(x_ref, tile, row, side) for row in (0, 1, side - 2, side - 1)]
        if piece >= side:
            low, high = (
                jnp.stack(
                    [
                        x_ref[:, tile, row * side + at : row * side + at + 16]
                        for row in range(piece // side)
                    ],
                    1,
                ).reshape(side, 16, chan)
                for at in (0, side - 16)
            )
        else:
            image = x_ref[:, tile].reshape(side, side // piece, piece, chan)
            low, high = image[:, 0, :16], image[:, -1, piece - 16 :]
        low, high = low.astype(F32), high.astype(F32)
        ring += [v.astype(BF16) for v in (low[:, 0], low[:, 1], high[:, 14], high[:, 15])]
        for at, line in enumerate(ring):
            ring_ref[tile, at] = line
        for strip, at in enumerate((0, 3, 4, 7)):
            lines[tile * 4 + strip] = ring[at]
            lines[tiles * 4 + tile * 4 + strip] = flip_line(ring[at])
    pick_lines(codes_ref, lines, picked, message_refs, tiles)


def ring_kernel(codes_ref, ring_ref, w_ref, b_ref, *rest):
    got_refs, message_refs, (own_ref, lines, picked, got) = rest[:4], rest[4:8], rest[8:]
    got[0], got[1] = in_order(codes_ref[8, 0], got_refs[0], got_refs[1])
    got[2], got[3] = in_order(codes_ref[8, 1], got_refs[2], got_refs[3])
    tiles = ring_ref.shape[0]
    side = ring_ref.shape[2]
    pads = [[got[k, pl.ds(t * side, side), :] for t in range(tiles)] for k in range(4)]
    corners = [
        got[2 + k % 2, pl.ds(tiles * side + k // 2 * CORNERS, CORNERS), :].astype(F32)
        for k in range(4)
    ]
    plans = [
        (0, 0, 1, 0, 1, 2, 3, 0, 1, lambda dy, dx: (dy, dx)),
        (1, 2, 3, 3, 2, 2, 3, side - 1, side - 2, lambda dy, dx: (2 - dy, dx)),
        (2, 0, 2, 4, 5, 0, 1, 0, 1, lambda dy, dx: (dx, dy)),
        (3, 1, 3, 7, 6, 0, 1, side - 1, side - 2, lambda dy, dx: (2 - dx, dy)),
    ]
    stacked = []
    for pad, c_first, c_last, line_0, line_1, end_a, end_b, at_0, at_1, tap in plans:
        for tile in range(tiles):
            begin = pads[end_a][tile].astype(F32)
            finish = pads[end_b][tile].astype(F32)
            parts = []
            for line, first, last in (
                (
                    pads[pad][tile],
                    corners[c_first][tile : tile + 1],
                    corners[c_last][tile : tile + 1],
                ),
                (ring_ref[tile, line_0], begin[at_0 : at_0 + 1], finish[at_0 : at_0 + 1]),
                (ring_ref[tile, line_1], begin[at_1 : at_1 + 1], finish[at_1 : at_1 + 1]),
            ):
                wide = line.astype(F32)
                parts.append(
                    (
                        shift_down(wide, first).astype(BF16),
                        line,
                        shift_up(wide, last).astype(BF16),
                    )
                )
            taps = [tap(dy, dx) for dy in range(3) for dx in range(3)]
            stacked.append(jnp.concatenate([parts[d][j] for d, j in taps], axis=1))
    summed = jnp.dot(
        jnp.concatenate(stacked, axis=0), w_ref[...], preferred_element_type=F32
    )
    hidden = gelu(summed + b_ref[...]).astype(BF16)
    for edge in range(4):
        for tile in range(tiles):
            at = (edge * tiles + tile) * side
            line = hidden[at : at + side]
            own_ref[tile, edge] = line
            lines[tile * 4 + edge] = line
            lines[tiles * 4 + tile * 4 + edge] = flip_line(line)
    pick_lines(codes_ref, lines, picked, message_refs, tiles)


def read_row(x_ref, tile, row, side):
    piece = x_ref.shape[2]
    at = row * side // piece
    if piece >= side:
        start = row * side % piece
        return x_ref[at, tile, start : start + side]
    return x_ref[at : at + side // piece, tile].reshape(side, x_ref.shape[3])


def write_row(ref, tile, row, side, line):
    piece = ref.shape[2]
    at = row * side // piece
    if piece >= side:
        start = row * side % piece
        ref[at, tile, start : start + side] = line
    else:
        count = side // piece
        ref[at : at + count, tile] = line.reshape(count, piece, line.shape[-1])


def row_spans(piece, side):
    cuts = [16] + list(range(piece, side, piece)) + [side - 16]
    return [(a, b) for a, b in zip(cuts, cuts[1:]) if a < b]


def read_part(ref, tile, row, side, begin, end):
    piece = ref.shape[2]
    first = row * side + begin
    start = first % piece
    return ref[first // piece, tile, start : start + end - begin]


def convolve_tile(padded, prepare, w_ref, bias, y, masked, finish):
    side = padded.shape[2]
    chan = padded.shape[3]
    blocks = y.shape[0]
    step = side // 2 // blocks
    rows = lax.broadcasted_iota(jnp.int32, (side, chan), 0)

    def multiply(block):
        begin = 2 * step * block
        for row in range(begin + 1 if block else -1, begin + 2 * step + 1):
            prepare(row)
        lhs = jnp.concatenate(
            [
                padded[pl.ds(step * block + j // 2, step), j % 2].reshape(step * side, chan)
                for j in range(4)
            ],
            axis=1,
        )
        y[block] = jnp.dot(lhs, w_ref[...], preferred_element_type=F32)

    multiply(0)
    for block in range(blocks):
        if block + 1 < blocks:
            multiply(block + 1)
        for i in range(step):
            for half in range(2):
                row = (block * step + i) * 2 + half
                a, b, c = (
                    y[block, pl.ds(i * side, side), pl.ds((half * 3 + dx) * chan, chan)]
                    for dx in range(3)
                )
                a = pltpu.roll(a, 1, 0)
                c = pltpu.roll(c, side - 1, 0)
                if masked:
                    a = jnp.where(rows == 0, 0.0, a)
                    c = jnp.where(rows == side - 1, 0.0, c)
                finish(row, (a + c) + (b + bias))


def first_kernel(side, tiles, *refs):
    w_ref, b_ref = refs[:2]
    fields, padded, y = refs[-3:]
    x_ref, h_ref = fields.at[0], fields.at[1]
    for tile in tiles:

        def prepare(row):
            if 0 <= row < side:
                line = read_row(x_ref, tile, row, side)
            else:
                line = jnp.zeros(padded.shape[2:], BF16)
            padded[(row + 1) // 2, (row + 1) % 2] = line

        def finish(row, value):
            write_row(h_ref, tile, row, side, gelu(value).astype(BF16))

        convolve_tile(padded, prepare, w_ref, b_ref[...], y, False, finish)


def second_kernel(side, tiles, *refs):
    ring_ref, w_ref, b_ref = refs[:3]
    fields, out_ref, strips, sums, padded, y, columns, result, sems = refs[-9:]
    x_ref, h_ref = fields.at[0], fields.at[1]
    chan = fields.shape[-1]
    rows = lax.broadcasted_iota(jnp.int32, (16, chan), 0)
    blocks = y.shape[0]
    size = side // blocks
    inner = pl.ds(16, side - 32)
    copies = []
    for at_tile, tile in enumerate(tiles):
        columns[0] = ring_ref[tile, 2].astype(F32)
        columns[1] = ring_ref[tile, 3].astype(F32)

        def prepare(row):
            m, e = (row + 1) // 2, (row + 1) % 2
            if row < 0 or row == side:
                padded[m, e] = jnp.zeros((side, chan), BF16)
            elif row == 0 or row == side - 1:
                padded[m, e] = ring_ref[tile, 0 if row == 0 else 1]
            else:
                for begin, end in row_spans(fields.shape[-2], side):
                    padded[m, e, begin:end] = read_part(h_ref, tile, row, side, begin, end)
                for at, begin, place in ((0, 0, 0), (1, side - 16, 15)):
                    old = read_part(h_ref, tile, row, side, begin, begin + 16).astype(F32)
                    new = jnp.where(rows == place, columns[at, row : row + 1], old)
                    padded[m, e, begin : begin + 16] = new.astype(BF16)

        def finish(row, value):
            total = read_row(x_ref, tile, row, side).astype(F32) + value
            line = total.astype(BF16)
            strips[tile, 0, row] = line[:16]
            strips[tile, 1, row] = line[side - 16 :]
            result[at_tile, row] = line[16 : side - 16]
            if row == 0 or row == side - 1:
                sums[tile, 0 if row == 0 else 1] = total
            sums[tile, 2, row : row + 1] = total[:1]
            sums[tile, 3, row : row + 1] = total[side - 1 :]
            if (row + 1) % size == 0:
                part = pl.ds(row + 1 - size, size)
                copies.append(
                    pltpu.make_async_copy(
                        result.at[at_tile, part],
                        out_ref.at[tile, part, inner],
                        sems.at[len(copies)],
                    )
                )
                copies[-1].start()

        convolve_tile(padded, prepare, w_ref, b_ref[...], y, True, finish)
    for copy in copies:
        copy.wait()


def last_kernel(side, upper, lower, before, after, w_ref, old_strips, sums, *refs):
    out_ref, ends, strips, sems = refs[-4:]
    tiles, chan = sums.shape[0], sums.shape[3]
    split = tiles * side
    got = (upper, lower, before, after)
    groups = [got[2 + k % 2][pl.ds(split + k // 2 * CORNERS, CORNERS), :] for k in range(4)]
    corners = [group.astype(F32) for group in groups]
    zero = jnp.zeros((1, chan), F32)
    added = []
    weights = (w_ref[0], w_ref[2], w_ref[:, 0], w_ref[:, 2])
    for edge in range(4):
        stacked = []
        for tile in range(tiles):
            line = got[edge][pl.ds(tile * side, side), :]
            first = corners[2 * edge][tile : tile + 1] if edge < 2 else zero
            last = corners[2 * edge + 1][tile : tile + 1] if edge < 2 else zero
            wide = line.astype(F32)
            stacked.append(
                jnp.concatenate(
                    [
                        shift_down(wide, first).astype(BF16),
                        line,
                        shift_up(wide, last).astype(BF16),
                    ],
                    axis=1,
                )
            )
        added.append(
            jnp.dot(
                jnp.concatenate(stacked, axis=0),
                weights[edge].reshape(3 * chan, chan),
                preferred_element_type=F32,
            )
        )
    rows = lax.broadcasted_iota(jnp.int32, (side, chan), 0)
    few = lax.broadcasted_iota(jnp.int32, (16, chan), 0)
    copies = []
    for tile in range(tiles):
        span = slice(tile * side, (tile + 1) * side)
        for edge in range(2):
            total = sums[tile, edge] + added[edge][span]
            at = 0 if edge == 0 else side - 1
            left = added[2][span][at : at + 1]
            right = added[3][span][at : at + 1]
            total = total + jnp.where(rows == 0, left, 0.0)
            total = total + jnp.where(rows == side - 1, right, 0.0)
            ends[tile, edge] = total.astype(BF16)
            copies.append(
                pltpu.make_async_copy(
                    ends.at[tile, edge], out_ref.at[tile, at], sems.at[len(copies)]
                )
            )
            copies[-1].start()
        for edge, begin, place in ((2, 0, 0), (3, side - 16, 15)):
            column = sums[tile, edge] + added[edge][span]
            for row in range(1, side - 1):
                old = old_strips[tile, edge - 2, row].astype(F32)
                new = jnp.where(few == place, column[row : row + 1], old)
                strips[tile, edge - 2, row] = new.astype(BF16)
            inner = pl.ds(1, side - 2)
            copies.append(
                pltpu.make_async_copy(
                    strips.at[tile, edge - 2, inner],
                    out_ref.at[tile, inner, pl.ds(begin, 16)],
                    sems.at[len(copies)],
                )
            )
            copies[-1].start()
    for copy in copies:
        copy.wait()


def paired_weights(weight):
    chan_in, chan_out = weight.shape[2:]
    by_tap = weight.transpose(0, 2, 1, 3).reshape(3, chan_in, 3 * chan_out)
    zero = jnp.zeros((1, chan_in, 3 * chan_out), weight.dtype)
    first = jnp.concatenate([by_tap, zero], 0)
    second = jnp.concatenate([zero, by_tap], 0)
    return jnp.stack([first, second], 2).reshape(4 * chan_in, 6 * chan_out)


def swap_far(array, axis):
    size = lax.axis_size(axis)
    pairs = [(i, (i + 1 if i % 2 else i - 1) % size) for i in range(size)]
    return lax.ppermute(array, axis, pairs)


def swap_near(array, axis):
    return lax.ppermute(array, axis, [(i, i ^ 1) for i in range(lax.axis_size(axis))])


def neighbours_along(array, axis):
    size = lax.axis_size(axis)
    after = lax.ppermute(array, axis, [(i, (i - 1) % size) for i in range(size)])
    before = lax.ppermute(array, axis, [(i, (i + 1) % size) for i in range(size)])
    return after, before


def shards(latitude_rows, tile_order, neighbours, rotations, w_first, b_first, w_second, b_second):
    devices = lax.axis_size("face") * lax.axis_size("tile")
    tiles = neighbours.shape[0]
    piece, chan = latitude_rows.shape[1:]
    side = int(round((piece * devices) ** 0.5))
    vmem_spec = pl.BlockSpec(memory_space=VMEM)
    smem_spec = pl.BlockSpec(memory_space=pltpu.SMEM)
    hbm_spec = pl.BlockSpec(memory_space=pltpu.HBM)
    params = pltpu.CompilerParams(vmem_limit_bytes=LIMIT)

    asked = neighbours % tiles * 4 + rotations
    after, before = neighbours_along(asked, "face")

    groups = 8 if latitude_rows.shape[0] % 8 == 0 else 1
    ordered = pl.pallas_call(
        gather_kernel,
        in_specs=[smem_spec, hbm_spec],
        out_specs=hbm_spec,
        out_shape=jax.ShapeDtypeStruct(latitude_rows.shape, latitude_rows.dtype),
        scratch_shapes=[
            VMEM(latitude_rows.shape, latitude_rows.dtype),
            pltpu.SemaphoreType.DMA((groups,)),
            pltpu.SemaphoreType.DMA,
        ],
        compiler_params=pltpu.CompilerParams(vmem_limit_bytes=WIDE_LIMIT),
        name="order",
    )(tile_order, latitude_rows)
    ordered, after, before = lax.optimization_barrier((ordered, after, before))
    gathered = lax.all_to_all(ordered, AXES, split_axis=0, concat_axis=0, tiled=True)
    column = jnp.stack([asked, after, before], 0)
    on, back = neighbours_along(column, "tile")
    asked = jnp.stack(
        [after, before] + [side_rows[i] for i in range(3) for side_rows in (on, back)], 0
    )
    turn = (asked % 4)[..., None] == jnp.arange(4, dtype=jnp.int32)
    strip = jnp.sum(jnp.where(turn, jnp.asarray(STRIP_TABLE), 0), -1)
    flip = jnp.sum(jnp.where(turn, jnp.asarray(FLIP_TABLE), 0), -1)
    codes = ((flip * tiles + asked // 4) * 4 + strip).reshape(8, tiles * 8)
    odd = jnp.stack([lax.axis_index("face") % 2, lax.axis_index("tile") % 2]).astype(jnp.int32)
    codes = jnp.concatenate([codes, jnp.pad(odd, (0, tiles * 8 - 2))[None]], 0)
    constants = (
        paired_weights(w_first),
        paired_weights(w_second),
        w_second,
        w_first.reshape(9 * chan, chan),
        b_first.reshape(1, chan),
        b_second.reshape(1, chan),
    )
    odd = (odd[0] == 1, odd[1] == 1)
    gathered, codes, odd, constants = lax.optimization_barrier((gathered, codes, odd, constants))
    w_one, w_two, w_pads, w_edges, b_one, b_two = constants
    pieces = gathered.reshape(devices, tiles, piece, chan)

    split = tiles * side
    message_shape = jax.ShapeDtypeStruct((split + 2 * CORNERS, chan), BF16)
    line_shape = (tiles, 8, side, chan)
    fields_shape = jax.ShapeDtypeStruct((2,) + pieces.shape, BF16)
    four = VMEM((4,) + message_shape.shape, BF16)
    lines_scratch = VMEM((8 * tiles, side, chan), BF16)
    fields, ring, *sends = pl.pallas_call(
        functools.partial(border_kernel, side),
        in_specs=[smem_spec, hbm_spec],
        out_specs=[vmem_spec] * 6,
        out_shape=[
            fields_shape,
            jax.ShapeDtypeStruct((tiles, 8, side, chan), BF16),
        ]
        + [message_shape] * 4,
        scratch_shapes=[lines_scratch, four, pltpu.SemaphoreType.DMA((tiles,))],
        compiler_params=params,
        name="borders",
    )(codes, pieces)

    blocks = 4
    field = VMEM((side // 2 + 1, 2, side, chan), BF16)
    products = VMEM((blocks, side // 2 // blocks * side, 6 * chan), F32)
    field_shape = jax.ShapeDtypeStruct((tiles, side, side, chan), BF16)

    def first(part, done):
        return (
            pl.pallas_call(
                functools.partial(first_kernel, side, part),
                in_specs=[vmem_spec] * 3,
                out_specs=vmem_spec,
                out_shape=fields_shape,
                input_output_aliases={2: 0},
                scratch_shapes=[field, products],
                compiler_params=params,
                name="first",
            )(w_one, b_one, *(done or (fields,))),
        )

    odd_face, odd_tile = odd

    def halo(sends, work):
        second, first = swap_far(sends[1], "face"), swap_near(sends[0], "face")
        done = work[0](())
        first, second, done = lax.optimization_barrier((first, second, done))
        groups = [
            jnp.where(odd_face, a[split:], b[split:]).reshape(2, CORNERS, chan)
            for a, b in ((first, second), (second, first))
        ]
        near, far = (
            jnp.concatenate(
                [own[:split]] + [jnp.where(odd_tile, g[1 - at], g[at]) for g in groups], 0
            )
            for at, own in enumerate(sends[2:])
        )
        third, fourth = swap_far(far, "tile"), swap_near(near, "tile")
        done = work[1](done)
        third, fourth, done = lax.optimization_barrier((third, fourth, done))
        return (first, second, fourth, third), done

    middle = (tiles + 1) // 2
    halves = [range(middle), range(middle, tiles)]
    got, fields = halo(sends, [functools.partial(first, part) for part in halves])
    *sends, hidden_ring = pl.pallas_call(
        ring_kernel,
        in_specs=[smem_spec] + [vmem_spec] * 7,
        out_specs=[vmem_spec] * 5,
        out_shape=[message_shape] * 4 + [jax.ShapeDtypeStruct((tiles, 4, side, chan), BF16)],
        scratch_shapes=[lines_scratch, four, four],
        compiler_params=params,
        name="hidden_ring",
    )(codes, ring, w_edges, b_one, *got)

    result_specs = [vmem_spec, hbm_spec, vmem_spec, vmem_spec]
    strips_shape = jax.ShapeDtypeStruct((tiles, 2, side, 16, chan), BF16)
    sums_shape = jax.ShapeDtypeStruct((tiles, 4, side, chan), F32)

    def second(part, done):
        done = done or fields
        return pl.pallas_call(
            functools.partial(second_kernel, side, part),
            in_specs=[vmem_spec] * 3 + result_specs[: len(done)],
            out_specs=result_specs,
            out_shape=[fields_shape, field_shape, strips_shape, sums_shape],
            input_output_aliases={3 + i: i for i in range(len(done))},
            scratch_shapes=[
                field,
                products,
                VMEM((2, side, chan), F32),
                VMEM((len(part), side, side - 32, chan), BF16),
                pltpu.SemaphoreType.DMA((len(part) * blocks,)),
            ],
            compiler_params=params,
            name="second",
        )(hidden_ring, w_two, b_two, *done)

    got, (_, out, strips, sums) = halo(sends, [functools.partial(second, part) for part in halves])
    pads = [
        jnp.where(flag, a, b)
        for flag, pair in ((odd_face, got[:2]), (odd_tile, got[2:]))
        for a, b in (pair, pair[::-1])
    ]
    return pl.pallas_call(
        functools.partial(last_kernel, side),
        in_specs=[vmem_spec] * 7 + [hbm_spec],
        out_specs=hbm_spec,
        out_shape=field_shape,
        input_output_aliases={7: 0},
        scratch_shapes=[
            VMEM((tiles, 2, side, chan), BF16),
            VMEM(strips_shape.shape, BF16),
            pltpu.SemaphoreType.DMA((4 * tiles,)),
        ],
        compiler_params=params,
        name="last",
    )(*pads, w_pads, strips, sums, out)


def solution(mesh):
    return jax.shard_map(
        shards,
        mesh=mesh,
        in_specs=(
            P(None, ("face", "tile"), None),
            P(),
            P(("face", "tile"), None),
            P(("face", "tile"), None),
            P(),
            P(),
            P(),
            P(),
        ),
        out_specs=P(("face", "tile"), None, None, None),
        check_vma=False,
    )
```

```python
import functools

import jax
import jax.numpy as jnp
import numpy as np
from jax import lax
from jax.experimental import pallas as pl
from jax.experimental.pallas import tpu as pltpu
from jax.sharding import PartitionSpec as P

STRIP_TABLE = np.array(
    [
        [1, 2, 0, 3],
        [0, 3, 1, 2],
        [3, 1, 2, 0],
        [2, 0, 3, 1],
        [1, 2, 0, 3],
        [1, 2, 0, 3],
        [0, 3, 1, 2],
        [0, 3, 1, 2],
    ],
    np.int32,
)
FLIP_TABLE = np.array(
    [
        [0, 0, 1, 1],
        [0, 0, 1, 1],
        [0, 1, 1, 0],
        [0, 1, 1, 0],
        [0, 0, 1, 1],
        [0, 0, 1, 1],
        [0, 0, 1, 1],
        [0, 0, 1, 1],
    ],
    np.int32,
)
DIRECTIONS = [(-1, 0), (1, 0), (0, -1), (0, 1), (-1, -1), (-1, 1), (1, -1), (1, 1)]
AXES = ("face", "tile")
VMEM = pltpu.VMEM
F32 = jnp.float32
BF16 = jnp.bfloat16
LIMIT = 32 * 1024 * 1024
WIDE_LIMIT = 60 * 1024 * 1024
CORNERS = 16


def shift_down(line, first):
    moved = pltpu.roll(line, 1, 0)
    rows = lax.broadcasted_iota(jnp.int32, moved.shape, 0)
    return jnp.where(rows == 0, first, moved)


def shift_up(line, last):
    size = line.shape[0]
    moved = pltpu.roll(line, size - 1, 0)
    rows = lax.broadcasted_iota(jnp.int32, moved.shape, 0)
    return jnp.where(rows == size - 1, last, moved)


def gelu(value):
    return (0.5 * value) * (1.0 + lax.erf(value * np.float32(np.sqrt(0.5))))


def pick_lines(codes_ref, lines, picked, message_refs, tiles):
    side = lines.shape[1]
    shape = (CORNERS, lines.shape[2])
    rows = lax.broadcasted_iota(jnp.int32, shape, 0)
    for direction in range(8):
        corner = jnp.zeros(shape, F32)
        for tile in range(tiles):
            line = lines[codes_ref[direction, tile * 8 + direction]]
            if direction < 4:
                picked[direction, pl.ds(tile * side, side), :] = line
            else:
                at = side - 1 if direction in (4, 6) else 0
                pixel = line.astype(F32)[at : at + 1]
                corner = jnp.where(rows == tile, pixel, corner)
        if direction >= 4:
            group = tiles * side + (direction % 2) * CORNERS
            picked[direction // 2 - 2, pl.ds(group, CORNERS), :] = corner.astype(BF16)
            picked[direction // 2, pl.ds(group, CORNERS), :] = jnp.zeros(shape, BF16)
    for axis in range(2):
        odd = codes_ref[8, axis]
        message_refs[2 * axis][...] = picked[2 * axis + odd]
        message_refs[2 * axis + 1][...] = picked[2 * axis + 1 - odd]


def in_order(odd, first_ref, second_ref):
    first, second = first_ref[...], second_ref[...]
    return jnp.where(odd == 1, first, second), jnp.where(odd == 1, second, first)


def flip_line(line):
    size = line.shape[0]
    row = lax.broadcasted_iota(jnp.int32, (size, size), 0)
    col = lax.broadcasted_iota(jnp.int32, (size, size), 1)
    turn = jnp.where(row + col == size - 1, 1.0, 0.0).astype(BF16)
    return jnp.dot(turn, line, preferred_element_type=F32).astype(BF16)


def gather_kernel(order_ref, x_ref, o_ref, held, in_sems, out_sem):
    groups = in_sems.shape[0]
    size = held.shape[0] // groups

    def start(at, carry):
        pltpu.make_async_copy(
            x_ref.at[order_ref[at]], held.at[at], in_sems.at[at // size]
        ).start()
        return carry

    lax.fori_loop(0, held.shape[0], start, 0)
    for group in range(groups):
        part = pl.ds(group * size, size)
        pltpu.make_async_copy(x_ref.at[part], held.at[part], in_sems.at[group]).wait()
        pltpu.make_async_copy(held.at[part], o_ref.at[part], out_sem).start()
    pltpu.make_async_copy(held, o_ref, out_sem).wait()


def border_kernel(side, codes_ref, source, fields, ring_ref, *rest):
    x_ref = fields.at[0]
    message_refs, lines, picked, sems = rest[:4], rest[4], rest[5], rest[6]
    devices, tiles, piece, chan = x_ref.shape
    copies = [
        pltpu.make_async_copy(source.at[:, tile], x_ref.at[:, tile], sems.at[tile])
        for tile in range(tiles)
    ]
    for copy in copies:
        copy.start()
    for tile in range(tiles):
        copies[tile].wait()
        ring = [read_row(x_ref, tile, row, side) for row in (0, 1, side - 2, side - 1)]
        if piece >= side:
            low, high = (
                jnp.stack(
                    [
                        x_ref[:, tile, row * side + at : row * side + at + 16]
                        for row in range(piece // side)
                    ],
                    1,
                ).reshape(side, 16, chan)
                for at in (0, side - 16)
            )
        else:
            image = x_ref[:, tile].reshape(side, side // piece, piece, chan)
            low, high = image[:, 0, :16], image[:, -1, piece - 16 :]
        low, high = low.astype(F32), high.astype(F32)
        ring += [v.astype(BF16) for v in (low[:, 0], low[:, 1], high[:, 14], high[:, 15])]
        for at, line in enumerate(ring):
            ring_ref[tile, at] = line
        for strip, at in enumerate((0, 3, 4, 7)):
            lines[tile * 4 + strip] = ring[at]
            lines[tiles * 4 + tile * 4 + strip] = flip_line(ring[at])
    pick_lines(codes_ref, lines, picked, message_refs, tiles)


def ring_kernel(codes_ref, ring_ref, w_ref, b_ref, *rest):
    got_refs, message_refs, (own_ref, lines, picked, got) = rest[:4], rest[4:8], rest[8:]
    got[0], got[1] = in_order(codes_ref[8, 0], got_refs[0], got_refs[1])
    got[2], got[3] = in_order(codes_ref[8, 1], got_refs[2], got_refs[3])
    tiles = ring_ref.shape[0]
    side = ring_ref.shape[2]
    pads = [[got[k, pl.ds(t * side, side), :] for t in range(tiles)] for k in range(4)]
    corners = [
        got[2 + k % 2, pl.ds(tiles * side + k // 2 * CORNERS, CORNERS), :].astype(F32)
        for k in range(4)
    ]
    plans = [
        (0, 0, 1, 0, 1, 2, 3, 0, 1, lambda dy, dx: (dy, dx)),
        (1, 2, 3, 3, 2, 2, 3, side - 1, side - 2, lambda dy, dx: (2 - dy, dx)),
        (2, 0, 2, 4, 5, 0, 1, 0, 1, lambda dy, dx: (dx, dy)),
        (3, 1, 3, 7, 6, 0, 1, side - 1, side - 2, lambda dy, dx: (2 - dx, dy)),
    ]
    stacked = []
    for pad, c_first, c_last, line_0, line_1, end_a, end_b, at_0, at_1, tap in plans:
        for tile in range(tiles):
            begin = pads[end_a][tile].astype(F32)
            finish = pads[end_b][tile].astype(F32)
            parts = []
            for line, first, last in (
                (
                    pads[pad][tile],
                    corners[c_first][tile : tile + 1],
                    corners[c_last][tile : tile + 1],
                ),
                (ring_ref[tile, line_0], begin[at_0 : at_0 + 1], finish[at_0 : at_0 + 1]),
                (ring_ref[tile, line_1], begin[at_1 : at_1 + 1], finish[at_1 : at_1 + 1]),
            ):
                wide = line.astype(F32)
                parts.append(
                    (
                        shift_down(wide, first).astype(BF16),
                        line,
                        shift_up(wide, last).astype(BF16),
                    )
                )
            taps = [tap(dy, dx) for dy in range(3) for dx in range(3)]
            stacked.append(jnp.concatenate([parts[d][j] for d, j in taps], axis=1))
    summed = jnp.dot(
        jnp.concatenate(stacked, axis=0), w_ref[...], preferred_element_type=F32
    )
    hidden = gelu(summed + b_ref[...]).astype(BF16)
    for edge in range(4):
        for tile in range(tiles):
            at = (edge * tiles + tile) * side
            line = hidden[at : at + side]
            own_ref[tile, edge] = line
            lines[tile * 4 + edge] = line
            lines[tiles * 4 + tile * 4 + edge] = flip_line(line)
    pick_lines(codes_ref, lines, picked, message_refs, tiles)


def read_row(x_ref, tile, row, side):
    piece = x_ref.shape[2]
    at = row * side // piece
    if piece >= side:
        start = row * side % piece
        return x_ref[at, tile, start : start + side]
    return x_ref[at : at + side // piece, tile].reshape(side, x_ref.shape[3])


def write_row(ref, tile, row, side, line):
    piece = ref.shape[2]
    at = row * side // piece
    if piece >= side:
        start = row * side % piece
        ref[at, tile, start : start + side] = line
    else:
        count = side // piece
        ref[at : at + count, tile] = line.reshape(count, piece, line.shape[-1])


def row_spans(piece, side):
    cuts = [16] + list(range(piece, side, piece)) + [side - 16]
    return [(a, b) for a, b in zip(cuts, cuts[1:]) if a < b]


def read_part(ref, tile, row, side, begin, end):
    piece = ref.shape[2]
    first = row * side + begin
    start = first % piece
    return ref[first // piece, tile, start : start + end - begin]


def convolve_tile(padded, prepare, w_ref, bias, y, masked, finish):
    side = padded.shape[2]
    chan = padded.shape[3]
    blocks = y.shape[0]
    step = side // 2 // blocks
    rows = lax.broadcasted_iota(jnp.int32, (side, chan), 0)

    def multiply(block):
        begin = 2 * step * block
        for row in range(begin + 1 if block else -1, begin + 2 * step + 1):
            prepare(row)
        lhs = jnp.concatenate(
            [
                padded[pl.ds(step * block + j // 2, step), j % 2].reshape(step * side, chan)
                for j in range(4)
            ],
            axis=1,
        )
        y[block] = jnp.dot(lhs, w_ref[...], preferred_element_type=F32)

    multiply(0)
    for block in range(blocks):
        if block + 1 < blocks:
            multiply(block + 1)
        for i in range(step):
            for half in range(2):
                row = (block * step + i) * 2 + half
                a, b, c = (
                    y[block, pl.ds(i * side, side), pl.ds((half * 3 + dx) * chan, chan)]
                    for dx in range(3)
                )
                a = pltpu.roll(a, 1, 0)
                c = pltpu.roll(c, side - 1, 0)
                if masked:
                    a = jnp.where(rows == 0, 0.0, a)
                    c = jnp.where(rows == side - 1, 0.0, c)
                finish(row, (a + c) + (b + bias))


def first_kernel(side, tiles, *refs):
    w_ref, b_ref = refs[:2]
    fields, padded, y = refs[-3:]
    x_ref, h_ref = fields.at[0], fields.at[1]
    for tile in tiles:

        def prepare(row):
            if 0 <= row < side:
                line = read_row(x_ref, tile, row, side)
            else:
                line = jnp.zeros(padded.shape[2:], BF16)
            padded[(row + 1) // 2, (row + 1) % 2] = line

        def finish(row, value):
            write_row(h_ref, tile, row, side, gelu(value).astype(BF16))

        convolve_tile(padded, prepare, w_ref, b_ref[...], y, False, finish)


def second_kernel(side, tiles, *refs):
    ring_ref, w_ref, b_ref = refs[:3]
    fields, out_ref, strips, sums, padded, y, columns, result, sems = refs[-9:]
    x_ref, h_ref = fields.at[0], fields.at[1]
    chan = fields.shape[-1]
    rows = lax.broadcasted_iota(jnp.int32, (16, chan), 0)
    blocks = y.shape[0]
    size = side // blocks
    inner = pl.ds(16, side - 32)
    copies = []
    for at_tile, tile in enumerate(tiles):
        columns[0] = ring_ref[tile, 2].astype(F32)
        columns[1] = ring_ref[tile, 3].astype(F32)

        def prepare(row):
            m, e = (row + 1) // 2, (row + 1) % 2
            if row < 0 or row == side:
                padded[m, e] = jnp.zeros((side, chan), BF16)
            elif row == 0 or row == side - 1:
                padded[m, e] = ring_ref[tile, 0 if row == 0 else 1]
            else:
                for begin, end in row_spans(fields.shape[-2], side):
                    padded[m, e, begin:end] = read_part(h_ref, tile, row, side, begin, end)
                for at, begin, place in ((0, 0, 0), (1, side - 16, 15)):
                    old = read_part(h_ref, tile, row, side, begin, begin + 16).astype(F32)
                    new = jnp.where(rows == place, columns[at, row : row + 1], old)
                    padded[m, e, begin : begin + 16] = new.astype(BF16)

        def finish(row, value):
            total = read_row(x_ref, tile, row, side).astype(F32) + value
            line = total.astype(BF16)
            strips[tile, 0, row] = line[:16]
            strips[tile, 1, row] = line[side - 16 :]
            result[at_tile, row] = line[16 : side - 16]
            if row == 0 or row == side - 1:
                sums[tile, 0 if row == 0 else 1] = total
            sums[tile, 2, row : row + 1] = total[:1]
            sums[tile, 3, row : row + 1] = total[side - 1 :]
            if (row + 1) % size == 0:
                part = pl.ds(row + 1 - size, size)
                copies.append(
                    pltpu.make_async_copy(
                        result.at[at_tile, part],
                        out_ref.at[tile, part, inner],
                        sems.at[len(copies)],
                    )
                )
                copies[-1].start()

        convolve_tile(padded, prepare, w_ref, b_ref[...], y, True, finish)
    for copy in copies:
        copy.wait()


def last_kernel(side, upper, lower, before, after, w_ref, old_strips, sums, *refs):
    out_ref, ends, strips, sems = refs[-4:]
    tiles, chan = sums.shape[0], sums.shape[3]
    split = tiles * side
    got = (upper, lower, before, after)
    groups = [got[2 + k % 2][pl.ds(split + k // 2 * CORNERS, CORNERS), :] for k in range(4)]
    corners = [group.astype(F32) for group in groups]
    zero = jnp.zeros((1, chan), F32)
    added = []
    weights = (w_ref[0], w_ref[2], w_ref[:, 0], w_ref[:, 2])
    for edge in range(4):
        stacked = []
        for tile in range(tiles):
            line = got[edge][pl.ds(tile * side, side), :]
            first = corners[2 * edge][tile : tile + 1] if edge < 2 else zero
            last = corners[2 * edge + 1][tile : tile + 1] if edge < 2 else zero
            wide = line.astype(F32)
            stacked.append(
                jnp.concatenate(
                    [
                        shift_down(wide, first).astype(BF16),
                        line,
                        shift_up(wide, last).astype(BF16),
                    ],
                    axis=1,
                )
            )
        added.append(
            jnp.dot(
                jnp.concatenate(stacked, axis=0),
                weights[edge].reshape(3 * chan, chan),
                preferred_element_type=F32,
            )
        )
    rows = lax.broadcasted_iota(jnp.int32, (side, chan), 0)
    few = lax.broadcasted_iota(jnp.int32, (16, chan), 0)
    copies = []
    for tile in range(tiles):
        span = slice(tile * side, (tile + 1) * side)
        for edge in range(2):
            total = sums[tile, edge] + added[edge][span]
            at = 0 if edge == 0 else side - 1
            left = added[2][span][at : at + 1]
            right = added[3][span][at : at + 1]
            total = total + jnp.where(rows == 0, left, 0.0)
            total = total + jnp.where(rows == side - 1, right, 0.0)
            ends[tile, edge] = total.astype(BF16)
            copies.append(
                pltpu.make_async_copy(
                    ends.at[tile, edge], out_ref.at[tile, at], sems.at[len(copies)]
                )
            )
            copies[-1].start()
        for edge, begin, place in ((2, 0, 0), (3, side - 16, 15)):
            column = sums[tile, edge] + added[edge][span]
            for row in range(1, side - 1):
                old = old_strips[tile, edge - 2, row].astype(F32)
                new = jnp.where(few == place, column[row : row + 1], old)
                strips[tile, edge - 2, row] = new.astype(BF16)
            inner = pl.ds(1, side - 2)
            copies.append(
                pltpu.make_async_copy(
                    strips.at[tile, edge - 2, inner],
                    out_ref.at[tile, inner, pl.ds(begin, 16)],
                    sems.at[len(copies)],
                )
            )
            copies[-1].start()
    for copy in copies:
        copy.wait()


def paired_weights(weight):
    chan_in, chan_out = weight.shape[2:]
    by_tap = weight.transpose(0, 2, 1, 3).reshape(3, chan_in, 3 * chan_out)
    zero = jnp.zeros((1, chan_in, 3 * chan_out), weight.dtype)
    first = jnp.concatenate([by_tap, zero], 0)
    second = jnp.concatenate([zero, by_tap], 0)
    return jnp.stack([first, second], 2).reshape(4 * chan_in, 6 * chan_out)


def swap_far(array, axis):
    size = lax.axis_size(axis)
    pairs = [(i, (i + 1 if i % 2 else i - 1) % size) for i in range(size)]
    return lax.ppermute(array, axis, pairs)


def swap_near(array, axis):
    return lax.ppermute(array, axis, [(i, i ^ 1) for i in range(lax.axis_size(axis))])


def neighbours_along(array, axis):
    size = lax.axis_size(axis)
    after = lax.ppermute(array, axis, [(i, (i - 1) % size) for i in range(size)])
    before = lax.ppermute(array, axis, [(i, (i + 1) % size) for i in range(size)])
    return after, before


def shards(latitude_rows, tile_order, neighbours, rotations, w_first, b_first, w_second, b_second):
    devices = lax.axis_size("face") * lax.axis_size("tile")
    tiles = neighbours.shape[0]
    piece, chan = latitude_rows.shape[1:]
    side = int(round((piece * devices) ** 0.5))
    vmem_spec = pl.BlockSpec(memory_space=VMEM)
    smem_spec = pl.BlockSpec(memory_space=pltpu.SMEM)
    hbm_spec = pl.BlockSpec(memory_space=pltpu.HBM)
    params = pltpu.CompilerParams(vmem_limit_bytes=LIMIT)

    groups = 8 if latitude_rows.shape[0] % 8 == 0 else 1
    ordered = pl.pallas_call(
        gather_kernel,
        in_specs=[smem_spec, hbm_spec],
        out_specs=hbm_spec,
        out_shape=jax.ShapeDtypeStruct(latitude_rows.shape, latitude_rows.dtype),
        scratch_shapes=[
            VMEM(latitude_rows.shape, latitude_rows.dtype),
            pltpu.SemaphoreType.DMA((groups,)),
            pltpu.SemaphoreType.DMA,
        ],
        compiler_params=pltpu.CompilerParams(vmem_limit_bytes=WIDE_LIMIT),
        name="order",
    )(tile_order, latitude_rows)
    gathered = lax.all_to_all(ordered, AXES, split_axis=0, concat_axis=0, tiled=True)

    asked = neighbours % tiles * 4 + rotations
    after, before = neighbours_along(asked, "face")
    column = jnp.stack([asked, after, before], 0)
    on, back = neighbours_along(column, "tile")
    asked = jnp.stack(
        [after, before] + [side_rows[i] for i in range(3) for side_rows in (on, back)], 0
    )
    turn = (asked % 4)[..., None] == jnp.arange(4, dtype=jnp.int32)
    strip = jnp.sum(jnp.where(turn, jnp.asarray(STRIP_TABLE), 0), -1)
    flip = jnp.sum(jnp.where(turn, jnp.asarray(FLIP_TABLE), 0), -1)
    codes = ((flip * tiles + asked // 4) * 4 + strip).reshape(8, tiles * 8)
    odd = jnp.stack([lax.axis_index("face") % 2, lax.axis_index("tile") % 2]).astype(jnp.int32)
    codes = jnp.concatenate([codes, jnp.pad(odd, (0, tiles * 8 - 2))[None]], 0)
    constants = (
        paired_weights(w_first),
        paired_weights(w_second),
        w_second,
        w_first.reshape(9 * chan, chan),
        b_first.reshape(1, chan),
        b_second.reshape(1, chan),
    )
    odd = (odd[0] == 1, odd[1] == 1)
    gathered, codes, odd, constants = lax.optimization_barrier((gathered, codes, odd, constants))
    w_one, w_two, w_pads, w_edges, b_one, b_two = constants
    pieces = gathered.reshape(devices, tiles, piece, chan)

    split = tiles * side
    message_shape = jax.ShapeDtypeStruct((split + 2 * CORNERS, chan), BF16)
    line_shape = (tiles, 8, side, chan)
    fields_shape = jax.ShapeDtypeStruct((2,) + pieces.shape, BF16)
    four = VMEM((4,) + message_shape.shape, BF16)
    lines_scratch = VMEM((8 * tiles, side, chan), BF16)
    fields, ring, *sends = pl.pallas_call(
        functools.partial(border_kernel, side),
        in_specs=[smem_spec, hbm_spec],
        out_specs=[vmem_spec] * 6,
        out_shape=[
            fields_shape,
            jax.ShapeDtypeStruct((tiles, 8, side, chan), BF16),
        ]
        + [message_shape] * 4,
        scratch_shapes=[lines_scratch, four, pltpu.SemaphoreType.DMA((tiles,))],
        compiler_params=params,
        name="borders",
    )(codes, pieces)

    blocks = 4
    field = VMEM((side // 2 + 1, 2, side, chan), BF16)
    products = VMEM((blocks, side // 2 // blocks * side, 6 * chan), F32)
    field_shape = jax.ShapeDtypeStruct((tiles, side, side, chan), BF16)

    def first(part, done):
        return (
            pl.pallas_call(
                functools.partial(first_kernel, side, part),
                in_specs=[vmem_spec] * 3,
                out_specs=vmem_spec,
                out_shape=fields_shape,
                input_output_aliases={2: 0},
                scratch_shapes=[field, products],
                compiler_params=params,
                name="first",
            )(w_one, b_one, *(done or (fields,))),
        )

    odd_face, odd_tile = odd

    def halo(sends, work):
        second, first = swap_far(sends[1], "face"), swap_near(sends[0], "face")
        done = work[0](())
        first, second, done = lax.optimization_barrier((first, second, done))
        groups = [
            jnp.where(odd_face, a[split:], b[split:]).reshape(2, CORNERS, chan)
            for a, b in ((first, second), (second, first))
        ]
        near, far = (
            jnp.concatenate(
                [own[:split]] + [jnp.where(odd_tile, g[1 - at], g[at]) for g in groups], 0
            )
            for at, own in enumerate(sends[2:])
        )
        third, fourth = swap_far(far, "tile"), swap_near(near, "tile")
        done = work[1](done)
        third, fourth, done = lax.optimization_barrier((third, fourth, done))
        return (first, second, fourth, third), done

    middle = (tiles + 1) // 2
    halves = [range(middle), range(middle, tiles)]
    got, fields = halo(sends, [functools.partial(first, part) for part in halves])
    *sends, hidden_ring = pl.pallas_call(
        ring_kernel,
        in_specs=[smem_spec] + [vmem_spec] * 7,
        out_specs=[vmem_spec] * 5,
        out_shape=[message_shape] * 4 + [jax.ShapeDtypeStruct((tiles, 4, side, chan), BF16)],
        scratch_shapes=[lines_scratch, four, four],
        compiler_params=params,
        name="hidden_ring",
    )(codes, ring, w_edges, b_one, *got)

    result_specs = [vmem_spec, hbm_spec, vmem_spec, vmem_spec]
    strips_shape = jax.ShapeDtypeStruct((tiles, 2, side, 16, chan), BF16)
    sums_shape = jax.ShapeDtypeStruct((tiles, 4, side, chan), F32)

    def second(part, done):
        done = done or fields
        return pl.pallas_call(
            functools.partial(second_kernel, side, part),
            in_specs=[vmem_spec] * 3 + result_specs[: len(done)],
            out_specs=result_specs,
            out_shape=[fields_shape, field_shape, strips_shape, sums_shape],
            input_output_aliases={3 + i: i for i in range(len(done))},
            scratch_shapes=[
                field,
                products,
                VMEM((2, side, chan), F32),
                VMEM((len(part), side, side - 32, chan), BF16),
                pltpu.SemaphoreType.DMA((len(part) * blocks,)),
            ],
            compiler_params=params,
            name="second",
        )(hidden_ring, w_two, b_two, *done)

    got, (_, out, strips, sums) = halo(sends, [functools.partial(second, part) for part in halves])
    pads = [
        jnp.where(flag, a, b)
        for flag, pair in ((odd_face, got[:2]), (odd_tile, got[2:]))
        for a, b in (pair, pair[::-1])
    ]
    return pl.pallas_call(
        functools.partial(last_kernel, side),
        in_specs=[vmem_spec] * 7 + [hbm_spec],
        out_specs=hbm_spec,
        out_shape=field_shape,
        input_output_aliases={7: 0},
        scratch_shapes=[
            VMEM((tiles, 2, side, chan), BF16),
            VMEM(strips_shape.shape, BF16),
            pltpu.SemaphoreType.DMA((4 * tiles,)),
        ],
        compiler_params=params,
        name="last",
    )(*pads, w_pads, strips, sums, out)


def solution(mesh):
    return jax.shard_map(
        shards,
        mesh=mesh,
        in_specs=(
            P(None, ("face", "tile"), None),
            P(),
            P(("face", "tile"), None),
            P(("face", "tile"), None),
            P(),
            P(),
            P(),
            P(),
        ),
        out_specs=P(("face", "tile"), None, None, None),
        check_vma=False,
    )
```

```python
import functools

import jax
import jax.numpy as jnp
import numpy as np
from jax import lax
from jax.experimental import pallas as pl
from jax.experimental.pallas import tpu as pltpu
from jax.sharding import PartitionSpec as P

STRIP_TABLE = np.array(
    [
        [1, 2, 0, 3],
        [0, 3, 1, 2],
        [3, 1, 2, 0],
        [2, 0, 3, 1],
        [1, 2, 0, 3],
        [1, 2, 0, 3],
        [0, 3, 1, 2],
        [0, 3, 1, 2],
    ],
    np.int32,
)
FLIP_TABLE = np.array(
    [
        [0, 0, 1, 1],
        [0, 0, 1, 1],
        [0, 1, 1, 0],
        [0, 1, 1, 0],
        [0, 0, 1, 1],
        [0, 0, 1, 1],
        [0, 0, 1, 1],
        [0, 0, 1, 1],
    ],
    np.int32,
)
DIRECTIONS = [(-1, 0), (1, 0), (0, -1), (0, 1), (-1, -1), (-1, 1), (1, -1), (1, 1)]
AXES = ("face", "tile")
VMEM = pltpu.VMEM
F32 = jnp.float32
BF16 = jnp.bfloat16
LIMIT = 32 * 1024 * 1024
WIDE_LIMIT = 60 * 1024 * 1024
CORNERS = 16


def shift_down(line, first):
    moved = pltpu.roll(line, 1, 0)
    rows = lax.broadcasted_iota(jnp.int32, moved.shape, 0)
    return jnp.where(rows == 0, first, moved)


def shift_up(line, last):
    size = line.shape[0]
    moved = pltpu.roll(line, size - 1, 0)
    rows = lax.broadcasted_iota(jnp.int32, moved.shape, 0)
    return jnp.where(rows == size - 1, last, moved)


def gelu(value):
    return (0.5 * value) * (1.0 + lax.erf(value * np.float32(np.sqrt(0.5))))


def pick_lines(codes_ref, lines, picked, message_refs, tiles):
    side = lines.shape[1]
    shape = (CORNERS, lines.shape[2])
    rows = lax.broadcasted_iota(jnp.int32, shape, 0)
    for direction in range(8):
        corner = jnp.zeros(shape, F32)
        for tile in range(tiles):
            line = lines[codes_ref[direction, tile * 8 + direction]]
            if direction < 4:
                picked[direction, pl.ds(tile * side, side), :] = line
            else:
                at = side - 1 if direction in (4, 6) else 0
                pixel = line.astype(F32)[at : at + 1]
                corner = jnp.where(rows == tile, pixel, corner)
        if direction >= 4:
            group = tiles * side + (direction % 2) * CORNERS
            picked[direction // 2 - 2, pl.ds(group, CORNERS), :] = corner.astype(BF16)
            picked[direction // 2, pl.ds(group, CORNERS), :] = jnp.zeros(shape, BF16)
    for axis in range(2):
        odd = codes_ref[8, axis]
        message_refs[2 * axis][...] = picked[2 * axis + odd]
        message_refs[2 * axis + 1][...] = picked[2 * axis + 1 - odd]


def in_order(odd, first_ref, second_ref):
    first, second = first_ref[...].astype(F32), second_ref[...].astype(F32)
    before, after = jnp.where(odd == 1, first, second), jnp.where(odd == 1, second, first)
    return before.astype(BF16), after.astype(BF16)


def flip_line(line):
    size = line.shape[0]
    row = lax.broadcasted_iota(jnp.int32, (size, size), 0)
    col = lax.broadcasted_iota(jnp.int32, (size, size), 1)
    turn = jnp.where(row + col == size - 1, 1.0, 0.0).astype(BF16)
    return jnp.dot(turn, line, preferred_element_type=F32).astype(BF16)


def gather_kernel(order_ref, x_ref, o_ref, held, in_sems, out_sem):
    groups = in_sems.shape[0]
    size = held.shape[0] // groups

    def start(at, carry):
        pltpu.make_async_copy(
            x_ref.at[order_ref[at]], held.at[at], in_sems.at[at // size]
        ).start()
        return carry

    lax.fori_loop(0, held.shape[0], start, 0)
    for group in range(groups):
        part = pl.ds(group * size, size)
        pltpu.make_async_copy(x_ref.at[part], held.at[part], in_sems.at[group]).wait()
        pltpu.make_async_copy(held.at[part], o_ref.at[part], out_sem).start()
    pltpu.make_async_copy(held, o_ref, out_sem).wait()


def border_kernel(side, codes, source, fields, ring_ref, *rest):
    x_ref = fields.at[0]
    message_refs, (lines, picked, codes_ref, sems) = rest[:4], rest[4:]
    devices, tiles, piece, chan = x_ref.shape
    copies = [
        pltpu.make_async_copy(source.at[:, tile], x_ref.at[:, tile], sems.at[tile])
        for tile in range(tiles)
    ]
    copies.append(pltpu.make_async_copy(codes, codes_ref, sems.at[tiles]))
    for copy in copies:
        copy.start()
    for tile in range(tiles):
        copies[tile].wait()
        ring = [read_row(x_ref, tile, row, side) for row in (0, 1, side - 2, side - 1)]
        if piece >= side:
            low, high = (
                jnp.stack(
                    [
                        x_ref[:, tile, row * side + at : row * side + at + 16]
                        for row in range(piece // side)
                    ],
                    1,
                ).reshape(side, 16, chan)
                for at in (0, side - 16)
            )
        else:
            image = x_ref[:, tile].reshape(side, side // piece, piece, chan)
            low, high = image[:, 0, :16], image[:, -1, piece - 16 :]
        low, high = low.astype(F32), high.astype(F32)
        ring += [v.astype(BF16) for v in (low[:, 0], low[:, 1], high[:, 14], high[:, 15])]
        for at, line in enumerate(ring):
            ring_ref[tile, at] = line
        for strip, at in enumerate((0, 3, 4, 7)):
            lines[tile * 4 + strip] = ring[at]
            lines[tiles * 4 + tile * 4 + strip] = flip_line(ring[at])
    copies[tiles].wait()
    pick_lines(codes_ref, lines, picked, message_refs, tiles)


def ring_kernel(codes, odd_ref, ring_ref, w_ref, b_ref, *rest):
    got_refs, message_refs, (own_ref, lines, picked, got, codes_ref, sem) = (
        rest[:4],
        rest[4:8],
        rest[8:],
    )
    copy = pltpu.make_async_copy(codes, codes_ref, sem)
    copy.start()
    for axis in range(2):
        first, second = got_refs[2 * axis], got_refs[2 * axis + 1]
        got[2 * axis], got[2 * axis + 1] = in_order(odd_ref[axis : axis + 1], first, second)
    tiles = ring_ref.shape[0]
    side = ring_ref.shape[2]
    pads = [[got[k, pl.ds(t * side, side), :] for t in range(tiles)] for k in range(4)]
    corners = [
        got[2 + k % 2, pl.ds(tiles * side + k // 2 * CORNERS, CORNERS), :].astype(F32)
        for k in range(4)
    ]
    plans = [
        (0, 0, 1, 0, 1, 2, 3, 0, 1, lambda dy, dx: (dy, dx)),
        (1, 2, 3, 3, 2, 2, 3, side - 1, side - 2, lambda dy, dx: (2 - dy, dx)),
        (2, 0, 2, 4, 5, 0, 1, 0, 1, lambda dy, dx: (dx, dy)),
        (3, 1, 3, 7, 6, 0, 1, side - 1, side - 2, lambda dy, dx: (2 - dx, dy)),
    ]
    stacked = []
    for pad, c_first, c_last, line_0, line_1, end_a, end_b, at_0, at_1, tap in plans:
        for tile in range(tiles):
            begin = pads[end_a][tile].astype(F32)
            finish = pads[end_b][tile].astype(F32)
            parts = []
            for line, first, last in (
                (
                    pads[pad][tile],
                    corners[c_first][tile : tile + 1],
                    corners[c_last][tile : tile + 1],
                ),
                (ring_ref[tile, line_0], begin[at_0 : at_0 + 1], finish[at_0 : at_0 + 1]),
                (ring_ref[tile, line_1], begin[at_1 : at_1 + 1], finish[at_1 : at_1 + 1]),
            ):
                wide = line.astype(F32)
                parts.append(
                    (
                        shift_down(wide, first).astype(BF16),
                        line,
                        shift_up(wide, last).astype(BF16),
                    )
                )
            taps = [tap(dy, dx) for dy in range(3) for dx in range(3)]
            stacked.append(jnp.concatenate([parts[d][j] for d, j in taps], axis=1))
    summed = jnp.dot(
        jnp.concatenate(stacked, axis=0), w_ref[...], preferred_element_type=F32
    )
    hidden = gelu(summed + b_ref[...]).astype(BF16)
    for edge in range(4):
        for tile in range(tiles):
            at = (edge * tiles + tile) * side
            line = hidden[at : at + side]
            own_ref[tile, edge] = line
            lines[tile * 4 + edge] = line
            lines[tiles * 4 + tile * 4 + edge] = flip_line(line)
    copy.wait()
    pick_lines(codes_ref, lines, picked, message_refs, tiles)


def read_row(x_ref, tile, row, side):
    piece = x_ref.shape[2]
    at = row * side // piece
    if piece >= side:
        start = row * side % piece
        return x_ref[at, tile, start : start + side]
    return x_ref[at : at + side // piece, tile].reshape(side, x_ref.shape[3])


def write_row(ref, tile, row, side, line):
    piece = ref.shape[2]
    at = row * side // piece
    if piece >= side:
        start = row * side % piece
        ref[at, tile, start : start + side] = line
    else:
        count = side // piece
        ref[at : at + count, tile] = line.reshape(count, piece, line.shape[-1])


def row_spans(piece, side):
    cuts = [16] + list(range(piece, side, piece)) + [side - 16]
    return [(a, b) for a, b in zip(cuts, cuts[1:]) if a < b]


def read_part(ref, tile, row, side, begin, end):
    piece = ref.shape[2]
    first = row * side + begin
    start = first % piece
    return ref[first // piece, tile, start : start + end - begin]


def convolve_tile(padded, prepare, w_ref, bias, y, masked, finish):
    side = padded.shape[2]
    chan = padded.shape[3]
    blocks = y.shape[0]
    step = side // 2 // blocks
    rows = lax.broadcasted_iota(jnp.int32, (side, chan), 0)

    def multiply(block):
        begin = 2 * step * block
        for row in range(begin + 1 if block else -1, begin + 2 * step + 1):
            prepare(row)
        lhs = jnp.concatenate(
            [
                padded[pl.ds(step * block + j // 2, step), j % 2].reshape(step * side, chan)
                for j in range(4)
            ],
            axis=1,
        )
        y[block] = jnp.dot(lhs, w_ref[...], preferred_element_type=F32)

    multiply(0)
    for block in range(blocks):
        if block + 1 < blocks:
            multiply(block + 1)
        for i in range(step):
            for half in range(2):
                row = (block * step + i) * 2 + half
                a, b, c = (
                    y[block, pl.ds(i * side, side), pl.ds((half * 3 + dx) * chan, chan)]
                    for dx in range(3)
                )
                a = pltpu.roll(a, 1, 0)
                c = pltpu.roll(c, side - 1, 0)
                if masked:
                    a = jnp.where(rows == 0, 0.0, a)
                    c = jnp.where(rows == side - 1, 0.0, c)
                finish(row, (a + c) + (b + bias))


def first_kernel(side, tiles, *refs):
    w_ref, b_ref = refs[:2]
    fields, padded, y = refs[-3:]
    x_ref, h_ref = fields.at[0], fields.at[1]
    for tile in tiles:

        def prepare(row):
            if 0 <= row < side:
                line = read_row(x_ref, tile, row, side)
            else:
                line = jnp.zeros(padded.shape[2:], BF16)
            padded[(row + 1) // 2, (row + 1) % 2] = line

        def finish(row, value):
            write_row(h_ref, tile, row, side, gelu(value).astype(BF16))

        convolve_tile(padded, prepare, w_ref, b_ref[...], y, False, finish)


def second_kernel(side, tiles, first_tile, *refs):
    ring_ref, w_ref, b_ref = refs[:3]
    late = refs[3] if first_tile else None
    fields, out_ref, strips, sums, kept, padded, y, columns, result, sems = refs[-10:]
    x_ref, h_ref = fields.at[0], fields.at[1]
    chan = fields.shape[-1]
    rows = lax.broadcasted_iota(jnp.int32, (16, chan), 0)
    blocks = y.shape[0]
    size = side // blocks
    inner = pl.ds(16, side - 32)
    copies = []
    if first_tile:
        part = pl.ds(side - size, size)
        copies.append(
            pltpu.make_async_copy(
                late, out_ref.at[first_tile - 1, part, inner], sems.at[len(tiles) * blocks]
            )
        )
        copies[-1].start()
    for at_tile, tile in enumerate(tiles):
        columns[0] = ring_ref[tile, 2].astype(F32)
        columns[1] = ring_ref[tile, 3].astype(F32)

        def prepare(row):
            m, e = (row + 1) // 2, (row + 1) % 2
            if row < 0 or row == side:
                padded[m, e] = jnp.zeros((side, chan), BF16)
            elif row == 0 or row == side - 1:
                padded[m, e] = ring_ref[tile, 0 if row == 0 else 1]
            else:
                for begin, end in row_spans(fields.shape[-2], side):
                    padded[m, e, begin:end] = read_part(h_ref, tile, row, side, begin, end)
                for at, begin, place in ((0, 0, 0), (1, side - 16, 15)):
                    old = read_part(h_ref, tile, row, side, begin, begin + 16).astype(F32)
                    new = jnp.where(rows == place, columns[at, row : row + 1], old)
                    padded[m, e, begin : begin + 16] = new.astype(BF16)

        def finish(row, value):
            total = read_row(x_ref, tile, row, side).astype(F32) + value
            line = total.astype(BF16)
            strips[tile, 0, row] = line[:16]
            strips[tile, 1, row] = line[side - 16 :]
            held = tile == tiles[-1] and row >= side - size
            if held and first_tile and row == side - size:
                copies.pop(0).wait()
            if held:
                kept[row - (side - size)] = line[16 : side - 16]
            else:
                result[at_tile, row] = line[16 : side - 16]
            if row == 0 or row == side - 1:
                sums[tile, 0 if row == 0 else 1] = total
            sums[tile, 2, row : row + 1] = total[:1]
            sums[tile, 3, row : row + 1] = total[side - 1 :]
            if (row + 1) % size == 0 and not held:
                part = pl.ds(row + 1 - size, size)
                copies.append(
                    pltpu.make_async_copy(
                        result.at[at_tile, part],
                        out_ref.at[tile, part, inner],
                        sems.at[at_tile * blocks + row // size],
                    )
                )
                copies[-1].start()

        convolve_tile(padded, prepare, w_ref, b_ref[...], y, True, finish)
    for copy in copies:
        copy.wait()


def last_kernel(side, upper, lower, before, after, w_ref, old_strips, sums, late, *refs):
    out_ref, ends, strips, sems = refs[-4:]
    tiles, chan = sums.shape[0], sums.shape[3]
    split = tiles * side
    count = late.shape[0] - 1
    part = pl.ds(side - 1 - count, count)
    copies = [
        pltpu.make_async_copy(
            late.at[pl.ds(0, count)],
            out_ref.at[tiles - 1, part, pl.ds(16, side - 32)],
            sems.at[4 * tiles],
        )
    ]
    copies[-1].start()
    got = (upper, lower, before, after)
    groups = [got[2 + k % 2][pl.ds(split + k // 2 * CORNERS, CORNERS), :] for k in range(4)]
    corners = [group.astype(F32) for group in groups]
    zero = jnp.zeros((1, chan), F32)
    added = []
    weights = (w_ref[0], w_ref[2], w_ref[:, 0], w_ref[:, 2])
    for edge in range(4):
        stacked = []
        for tile in range(tiles):
            line = got[edge][pl.ds(tile * side, side), :]
            first = corners[2 * edge][tile : tile + 1] if edge < 2 else zero
            last = corners[2 * edge + 1][tile : tile + 1] if edge < 2 else zero
            wide = line.astype(F32)
            stacked.append(
                jnp.concatenate(
                    [
                        shift_down(wide, first).astype(BF16),
                        line,
                        shift_up(wide, last).astype(BF16),
                    ],
                    axis=1,
                )
            )
        added.append(
            jnp.dot(
                jnp.concatenate(stacked, axis=0),
                weights[edge].reshape(3 * chan, chan),
                preferred_element_type=F32,
            )
        )
    rows = lax.broadcasted_iota(jnp.int32, (side, chan), 0)
    few = lax.broadcasted_iota(jnp.int32, (16, chan), 0)
    for tile in range(tiles):
        span = slice(tile * side, (tile + 1) * side)
        for edge in range(2):
            total = sums[tile, edge] + added[edge][span]
            at = 0 if edge == 0 else side - 1
            left = added[2][span][at : at + 1]
            right = added[3][span][at : at + 1]
            total = total + jnp.where(rows == 0, left, 0.0)
            total = total + jnp.where(rows == side - 1, right, 0.0)
            ends[tile, edge] = total.astype(BF16)
            copies.append(
                pltpu.make_async_copy(
                    ends.at[tile, edge], out_ref.at[tile, at], sems.at[len(copies) - 1]
                )
            )
            copies[-1].start()
        for edge, begin, place in ((2, 0, 0), (3, side - 16, 15)):
            column = sums[tile, edge] + added[edge][span]
            for row in range(1, side - 1):
                old = old_strips[tile, edge - 2, row].astype(F32)
                new = jnp.where(few == place, column[row : row + 1], old)
                strips[tile, edge - 2, row] = new.astype(BF16)
            inner = pl.ds(1, side - 2)
            copies.append(
                pltpu.make_async_copy(
                    strips.at[tile, edge - 2, inner],
                    out_ref.at[tile, inner, pl.ds(begin, 16)],
                    sems.at[len(copies) - 1],
                )
            )
            copies[-1].start()
    for copy in copies:
        copy.wait()


def paired_weights(weight):
    chan_in, chan_out = weight.shape[2:]
    by_tap = weight.transpose(0, 2, 1, 3).reshape(3, chan_in, 3 * chan_out)
    zero = jnp.zeros((1, chan_in, 3 * chan_out), weight.dtype)
    first = jnp.concatenate([by_tap, zero], 0)
    second = jnp.concatenate([zero, by_tap], 0)
    return jnp.stack([first, second], 2).reshape(4 * chan_in, 6 * chan_out)


def swap_far(array, axis):
    size = lax.axis_size(axis)
    pairs = [(i, (i + 1 if i % 2 else i - 1) % size) for i in range(size)]
    return lax.ppermute(array, axis, pairs)


def swap_near(array, axis):
    return lax.ppermute(array, axis, [(i, i ^ 1) for i in range(lax.axis_size(axis))])


def neighbours_along(array, axis):
    size = lax.axis_size(axis)
    after = lax.ppermute(array, axis, [(i, (i - 1) % size) for i in range(size)])
    before = lax.ppermute(array, axis, [(i, (i + 1) % size) for i in range(size)])
    return after, before


def shards(latitude_rows, tile_order, neighbours, rotations, w_first, b_first, w_second, b_second):
    devices = lax.axis_size("face") * lax.axis_size("tile")
    tiles = neighbours.shape[0]
    piece, chan = latitude_rows.shape[1:]
    side = int(round((piece * devices) ** 0.5))
    vmem_spec = pl.BlockSpec(memory_space=VMEM)
    smem_spec = pl.BlockSpec(memory_space=pltpu.SMEM)
    hbm_spec = pl.BlockSpec(memory_space=pltpu.HBM)
    params = pltpu.CompilerParams(vmem_limit_bytes=LIMIT)

    groups = 8 if latitude_rows.shape[0] % 8 == 0 else 1
    ordered = pl.pallas_call(
        gather_kernel,
        in_specs=[smem_spec, hbm_spec],
        out_specs=hbm_spec,
        out_shape=jax.ShapeDtypeStruct(latitude_rows.shape, latitude_rows.dtype),
        scratch_shapes=[
            VMEM(latitude_rows.shape, latitude_rows.dtype),
            pltpu.SemaphoreType.DMA((groups,)),
            pltpu.SemaphoreType.DMA,
        ],
        compiler_params=pltpu.CompilerParams(vmem_limit_bytes=WIDE_LIMIT),
        name="order",
    )(tile_order, latitude_rows)
    gathered = lax.all_to_all(ordered, AXES, split_axis=0, concat_axis=0, tiled=True)

    asked = neighbours % tiles * 4 + rotations
    after, before = neighbours_along(asked, "face")
    column = jnp.stack([asked, after, before], 0)
    on, back = neighbours_along(column, "tile")
    asked = jnp.stack(
        [after, before] + [side_rows[i] for i in range(3) for side_rows in (on, back)], 0
    )
    turn = (asked % 4)[..., None] == jnp.arange(4, dtype=jnp.int32)
    strip = jnp.sum(jnp.where(turn, jnp.asarray(STRIP_TABLE), 0), -1)
    flip = jnp.sum(jnp.where(turn, jnp.asarray(FLIP_TABLE), 0), -1)
    codes = ((flip * tiles + asked // 4) * 4 + strip).reshape(8, tiles * 8)
    odd = jnp.stack([lax.axis_index("face") % 2, lax.axis_index("tile") % 2]).astype(jnp.int32)
    codes = jnp.concatenate([codes, jnp.pad(odd, (0, tiles * 8 - 2))[None]], 0)
    constants = (
        paired_weights(w_first),
        paired_weights(w_second),
        w_second,
        w_first.reshape(9 * chan, chan),
        b_first.reshape(1, chan),
        b_second.reshape(1, chan),
    )
    odd_rows = jnp.broadcast_to(jnp.pad(odd, (0, 6))[:, None], (8, chan))
    odd = (odd[0] == 1, odd[1] == 1)
    gathered, codes, odd, odd_rows, constants = lax.optimization_barrier(
        (gathered, codes, odd, odd_rows, constants)
    )
    w_one, w_two, w_pads, w_edges, b_one, b_two = constants
    pieces = gathered.reshape(devices, tiles, piece, chan)

    split = tiles * side
    message_shape = jax.ShapeDtypeStruct((split + 2 * CORNERS, chan), BF16)
    line_shape = (tiles, 8, side, chan)
    fields_shape = jax.ShapeDtypeStruct((2,) + pieces.shape, BF16)
    codes_scratch = pltpu.SMEM(codes.shape, jnp.int32)
    four = VMEM((4,) + message_shape.shape, BF16)
    lines_scratch = VMEM((8 * tiles, side, chan), BF16)
    fields, ring, *sends = pl.pallas_call(
        functools.partial(border_kernel, side),
        in_specs=[hbm_spec, hbm_spec],
        out_specs=[vmem_spec] * 6,
        out_shape=[
            fields_shape,
            jax.ShapeDtypeStruct((tiles, 8, side, chan), BF16),
        ]
        + [message_shape] * 4,
        scratch_shapes=[lines_scratch, four, codes_scratch, pltpu.SemaphoreType.DMA((tiles + 1,))],
        compiler_params=params,
        name="borders",
    )(codes, pieces)

    blocks = 4
    field = VMEM((side // 2 + 1, 2, side, chan), BF16)
    products = VMEM((blocks, side // 2 // blocks * side, 6 * chan), F32)
    field_shape = jax.ShapeDtypeStruct((tiles, side, side, chan), BF16)

    def first(part, done):
        return (
            pl.pallas_call(
                functools.partial(first_kernel, side, part),
                in_specs=[vmem_spec] * 3,
                out_specs=vmem_spec,
                out_shape=fields_shape,
                input_output_aliases={2: 0},
                scratch_shapes=[field, products],
                compiler_params=params,
                name="first",
            )(w_one, b_one, *(done or (fields,))),
        )

    odd_face, odd_tile = odd

    def halo(sends, work):
        second, first = swap_far(sends[1], "face"), swap_near(sends[0], "face")
        done = work[0](())
        first, second, done = lax.optimization_barrier((first, second, done))
        groups = [
            jnp.where(odd_face, a[split:], b[split:]).reshape(2, CORNERS, chan)
            for a, b in ((first, second), (second, first))
        ]
        near, far = (
            jnp.concatenate(
                [own[:split]] + [jnp.where(odd_tile, g[1 - at], g[at]) for g in groups], 0
            )
            for at, own in enumerate(sends[2:])
        )
        third, fourth = swap_far(far, "tile"), swap_near(near, "tile")
        done = work[1](done)
        third, fourth, done = lax.optimization_barrier((third, fourth, done))
        return (first, second, fourth, third), done

    middle = (tiles + 1) // 2
    halves = [range(middle), range(middle, tiles)]
    got, fields = halo(sends, [functools.partial(first, part) for part in halves])
    *sends, hidden_ring = pl.pallas_call(
        ring_kernel,
        in_specs=[hbm_spec] + [vmem_spec] * 8,
        out_specs=[vmem_spec] * 5,
        out_shape=[message_shape] * 4 + [jax.ShapeDtypeStruct((tiles, 4, side, chan), BF16)],
        scratch_shapes=[lines_scratch, four, four, codes_scratch, pltpu.SemaphoreType.DMA],
        compiler_params=params,
        name="hidden_ring",
    )(codes, odd_rows, ring, w_edges, b_one, *got)

    result_specs = [vmem_spec, hbm_spec, vmem_spec, vmem_spec]
    strips_shape = jax.ShapeDtypeStruct((tiles, 2, side, 16, chan), BF16)
    sums_shape = jax.ShapeDtypeStruct((tiles, 4, side, chan), F32)
    kept_shape = jax.ShapeDtypeStruct((side // blocks, side - 32, chan), BF16)

    def second(part, done):
        *done, late = done or (*fields, None)
        late = [] if late is None else [late]
        return pl.pallas_call(
            functools.partial(second_kernel, side, part, part[0]),
            in_specs=[vmem_spec] * (3 + len(late)) + result_specs[: len(done)],
            out_specs=result_specs + [vmem_spec],
            out_shape=[fields_shape, field_shape, strips_shape, sums_shape, kept_shape],
            input_output_aliases={3 + len(late) + i: i for i in range(len(done))},
            scratch_shapes=[
                field,
                products,
                VMEM((2, side, chan), F32),
                VMEM((len(part), side, side - 32, chan), BF16),
                pltpu.SemaphoreType.DMA((len(part) * blocks + 1,)),
            ],
            compiler_params=params,
            name="second",
        )(hidden_ring, w_two, b_two, *late, *done)

    got, (_, out, strips, sums, late) = halo(
        sends, [functools.partial(second, part) for part in halves]
    )
    pads = [
        jnp.where(flag, a, b)
        for flag, pair in ((odd_face, got[:2]), (odd_tile, got[2:]))
        for a, b in (pair, pair[::-1])
    ]
    return pl.pallas_call(
        functools.partial(last_kernel, side),
        in_specs=[vmem_spec] * 8 + [hbm_spec],
        out_specs=hbm_spec,
        out_shape=field_shape,
        input_output_aliases={8: 0},
        scratch_shapes=[
            VMEM((tiles, 2, side, chan), BF16),
            VMEM(strips_shape.shape, BF16),
            pltpu.SemaphoreType.DMA((4 * tiles + 1,)),
        ],
        compiler_params=params,
        name="last",
    )(*pads, w_pads, strips, sums, late, out)


def solution(mesh):
    return jax.shard_map(
        shards,
        mesh=mesh,
        in_specs=(
            P(None, ("face", "tile"), None),
            P(),
            P(("face", "tile"), None),
            P(("face", "tile"), None),
            P(),
            P(),
            P(),
            P(),
        ),
        out_specs=P(("face", "tile"), None, None, None),
        check_vma=False,
    )
```

```python
import functools

import jax
import jax.numpy as jnp
import numpy as np
from jax import lax
from jax.experimental import pallas as pl
from jax.experimental.pallas import tpu as pltpu
from jax.sharding import PartitionSpec as P

STRIP_TABLE = np.array(
    [
        [1, 2, 0, 3],
        [0, 3, 1, 2],
        [3, 1, 2, 0],
        [2, 0, 3, 1],
        [1, 2, 0, 3],
        [1, 2, 0, 3],
        [0, 3, 1, 2],
        [0, 3, 1, 2],
    ],
    np.int32,
)
FLIP_TABLE = np.array(
    [
        [0, 0, 1, 1],
        [0, 0, 1, 1],
        [0, 1, 1, 0],
        [0, 1, 1, 0],
        [0, 0, 1, 1],
        [0, 0, 1, 1],
        [0, 0, 1, 1],
        [0, 0, 1, 1],
    ],
    np.int32,
)
DIRECTIONS = [(-1, 0), (1, 0), (0, -1), (0, 1), (-1, -1), (-1, 1), (1, -1), (1, 1)]
AXES = ("face", "tile")
VMEM = pltpu.VMEM
F32 = jnp.float32
BF16 = jnp.bfloat16
LIMIT = 32 * 1024 * 1024
WIDE_LIMIT = 60 * 1024 * 1024
CORNERS = 16


def shift_down(line, first):
    moved = pltpu.roll(line, 1, 0)
    rows = lax.broadcasted_iota(jnp.int32, moved.shape, 0)
    return jnp.where(rows == 0, first, moved)


def shift_up(line, last):
    size = line.shape[0]
    moved = pltpu.roll(line, size - 1, 0)
    rows = lax.broadcasted_iota(jnp.int32, moved.shape, 0)
    return jnp.where(rows == size - 1, last, moved)


def gelu(value):
    return (0.5 * value) * (1.0 + lax.erf(value * np.float32(np.sqrt(0.5))))


def pick_lines(codes_ref, lines, picked, message_refs, tiles):
    side = lines.shape[1]
    shape = (CORNERS, lines.shape[2])
    rows = lax.broadcasted_iota(jnp.int32, shape, 0)
    for direction in range(8):
        corner = jnp.zeros(shape, F32)
        for tile in range(tiles):
            line = lines[codes_ref[direction, tile * 8 + direction]]
            if direction < 4:
                picked[direction, pl.ds(tile * side, side), :] = line
            else:
                at = side - 1 if direction in (4, 6) else 0
                pixel = line.astype(F32)[at : at + 1]
                corner = jnp.where(rows == tile, pixel, corner)
        if direction >= 4:
            group = tiles * side + (direction % 2) * CORNERS
            picked[direction // 2 - 2, pl.ds(group, CORNERS), :] = corner.astype(BF16)
            picked[direction // 2, pl.ds(group, CORNERS), :] = jnp.zeros(shape, BF16)
    for axis in range(2):
        odd = codes_ref[8, axis]
        message_refs[2 * axis][...] = picked[2 * axis + odd]
        message_refs[2 * axis + 1][...] = picked[2 * axis + 1 - odd]


def in_order(odd, first_ref, second_ref):
    first, second = first_ref[...].astype(F32), second_ref[...].astype(F32)
    before, after = jnp.where(odd == 1, first, second), jnp.where(odd == 1, second, first)
    return before.astype(BF16), after.astype(BF16)


def flip_line(line):
    size = line.shape[0]
    row = lax.broadcasted_iota(jnp.int32, (size, size), 0)
    col = lax.broadcasted_iota(jnp.int32, (size, size), 1)
    turn = jnp.where(row + col == size - 1, 1.0, 0.0).astype(BF16)
    return jnp.dot(turn, line, preferred_element_type=F32).astype(BF16)


def gather_kernel(order_ref, x_ref, o_ref, held, in_sems, out_sem):
    groups = in_sems.shape[0]
    size = held.shape[0] // groups

    def start(at, carry):
        pltpu.make_async_copy(
            x_ref.at[order_ref[at]], held.at[at], in_sems.at[at // size]
        ).start()
        return carry

    lax.fori_loop(0, held.shape[0], start, 0)
    for group in range(groups):
        part = pl.ds(group * size, size)
        pltpu.make_async_copy(x_ref.at[part], held.at[part], in_sems.at[group]).wait()
        pltpu.make_async_copy(held.at[part], o_ref.at[part], out_sem).start()
    pltpu.make_async_copy(held, o_ref, out_sem).wait()


def border_kernel(side, codes, source, fields, ring_ref, *rest):
    x_ref = fields.at[0]
    message_refs, (lines, picked, codes_ref, sems) = rest[:4], rest[4:]
    devices, tiles, piece, chan = x_ref.shape
    copies = [
        pltpu.make_async_copy(source.at[:, tile], x_ref.at[:, tile], sems.at[tile])
        for tile in range(tiles)
    ]
    copies.append(pltpu.make_async_copy(codes, codes_ref, sems.at[tiles]))
    for copy in copies:
        copy.start()
    for tile in range(tiles):
        copies[tile].wait()
        ring = [read_row(x_ref, tile, row, side) for row in (0, 1, side - 2, side - 1)]
        if piece >= side:
            low, high = (
                jnp.stack(
                    [
                        x_ref[:, tile, row * side + at : row * side + at + 16]
                        for row in range(piece // side)
                    ],
                    1,
                ).reshape(side, 16, chan)
                for at in (0, side - 16)
            )
        else:
            image = x_ref[:, tile].reshape(side, side // piece, piece, chan)
            low, high = image[:, 0, :16], image[:, -1, piece - 16 :]
        low, high = low.astype(F32), high.astype(F32)
        ring += [v.astype(BF16) for v in (low[:, 0], low[:, 1], high[:, 14], high[:, 15])]
        for at, line in enumerate(ring):
            ring_ref[tile, at] = line
        for strip, at in enumerate((0, 3, 4, 7)):
            lines[tile * 4 + strip] = ring[at]
            lines[tiles * 4 + tile * 4 + strip] = flip_line(ring[at])
    copies[tiles].wait()
    pick_lines(codes_ref, lines, picked, message_refs, tiles)


def ring_kernel(codes, odd_ref, ring_ref, w_ref, b_ref, *rest):
    got_refs, message_refs, (own_ref, lines, picked, got, codes_ref, sem) = (
        rest[:4],
        rest[4:8],
        rest[8:],
    )
    copy = pltpu.make_async_copy(codes, codes_ref, sem)
    copy.start()
    for axis in range(2):
        first, second = got_refs[2 * axis], got_refs[2 * axis + 1]
        got[2 * axis], got[2 * axis + 1] = in_order(odd_ref[axis : axis + 1], first, second)
    tiles = ring_ref.shape[0]
    side = ring_ref.shape[2]
    pads = [[got[k, pl.ds(t * side, side), :] for t in range(tiles)] for k in range(4)]
    corners = [
        got[2 + k % 2, pl.ds(tiles * side + k // 2 * CORNERS, CORNERS), :].astype(F32)
        for k in range(4)
    ]
    plans = [
        (0, 0, 1, 0, 1, 2, 3, 0, 1, lambda dy, dx: (dy, dx)),
        (1, 2, 3, 3, 2, 2, 3, side - 1, side - 2, lambda dy, dx: (2 - dy, dx)),
        (2, 0, 2, 4, 5, 0, 1, 0, 1, lambda dy, dx: (dx, dy)),
        (3, 1, 3, 7, 6, 0, 1, side - 1, side - 2, lambda dy, dx: (2 - dx, dy)),
    ]
    stacked = []
    for pad, c_first, c_last, line_0, line_1, end_a, end_b, at_0, at_1, tap in plans:
        for tile in range(tiles):
            begin = pads[end_a][tile].astype(F32)
            finish = pads[end_b][tile].astype(F32)
            parts = []
            for line, first, last in (
                (
                    pads[pad][tile],
                    corners[c_first][tile : tile + 1],
                    corners[c_last][tile : tile + 1],
                ),
                (ring_ref[tile, line_0], begin[at_0 : at_0 + 1], finish[at_0 : at_0 + 1]),
                (ring_ref[tile, line_1], begin[at_1 : at_1 + 1], finish[at_1 : at_1 + 1]),
            ):
                wide = line.astype(F32)
                parts.append(
                    (
                        shift_down(wide, first).astype(BF16),
                        line,
                        shift_up(wide, last).astype(BF16),
                    )
                )
            taps = [tap(dy, dx) for dy in range(3) for dx in range(3)]
            stacked.append(jnp.concatenate([parts[d][j] for d, j in taps], axis=1))
    summed = jnp.dot(
        jnp.concatenate(stacked, axis=0), w_ref[...], preferred_element_type=F32
    )
    hidden = gelu(summed + b_ref[...]).astype(BF16)
    for edge in range(4):
        for tile in range(tiles):
            at = (edge * tiles + tile) * side
            line = hidden[at : at + side]
            own_ref[tile, edge] = line
            lines[tile * 4 + edge] = line
            lines[tiles * 4 + tile * 4 + edge] = flip_line(line)
    copy.wait()
    pick_lines(codes_ref, lines, picked, message_refs, tiles)


def read_row(x_ref, tile, row, side):
    piece = x_ref.shape[2]
    at = row * side // piece
    if piece >= side:
        start = row * side % piece
        return x_ref[at, tile, start : start + side]
    return x_ref[at : at + side // piece, tile].reshape(side, x_ref.shape[3])


def write_row(ref, tile, row, side, line):
    piece = ref.shape[2]
    at = row * side // piece
    if piece >= side:
        start = row * side % piece
        ref[at, tile, start : start + side] = line
    else:
        count = side // piece
        ref[at : at + count, tile] = line.reshape(count, piece, line.shape[-1])


def row_spans(piece, side):
    cuts = [16] + list(range(piece, side, piece)) + [side - 16]
    return [(a, b) for a, b in zip(cuts, cuts[1:]) if a < b]


def read_part(ref, tile, row, side, begin, end):
    piece = ref.shape[2]
    first = row * side + begin
    start = first % piece
    return ref[first // piece, tile, start : start + end - begin]


def convolve_tile(padded, prepare, w_ref, bias, y, masked, finish):
    side = padded.shape[2]
    chan = padded.shape[3]
    blocks = y.shape[0]
    step = side // 2 // blocks
    rows = lax.broadcasted_iota(jnp.int32, (side, chan), 0)

    def multiply(block):
        begin = 2 * step * block
        for row in range(begin + 1 if block else -1, begin + 2 * step + 1):
            prepare(row)
        lhs = jnp.concatenate(
            [
                padded[pl.ds(step * block + j // 2, step), j % 2].reshape(step * side, chan)
                for j in range(4)
            ],
            axis=1,
        )
        y[block] = jnp.dot(lhs, w_ref[...], preferred_element_type=F32)

    multiply(0)
    for block in range(blocks):
        if block + 1 < blocks:
            multiply(block + 1)
        for i in range(step):
            for half in range(2):
                row = (block * step + i) * 2 + half
                a, b, c = (
                    y[block, pl.ds(i * side, side), pl.ds((half * 3 + dx) * chan, chan)]
                    for dx in range(3)
                )
                a = pltpu.roll(a, 1, 0)
                c = pltpu.roll(c, side - 1, 0)
                if masked:
                    a = jnp.where(rows == 0, 0.0, a)
                    c = jnp.where(rows == side - 1, 0.0, c)
                finish(row, (a + c) + (b + bias))


def first_kernel(side, tiles, *refs):
    w_ref, b_ref = refs[:2]
    fields, padded, y = refs[-3:]
    x_ref, h_ref = fields.at[0], fields.at[1]
    for tile in tiles:

        def prepare(row):
            if 0 <= row < side:
                line = read_row(x_ref, tile, row, side)
            else:
                line = jnp.zeros(padded.shape[2:], BF16)
            padded[(row + 1) // 2, (row + 1) % 2] = line

        def finish(row, value):
            write_row(h_ref, tile, row, side, gelu(value).astype(BF16))

        convolve_tile(padded, prepare, w_ref, b_ref[...], y, False, finish)


def second_kernel(side, tiles, first_tile, *refs):
    ring_ref, w_ref, b_ref = refs[:3]
    late = refs[3] if first_tile else None
    fields, out_ref, strips, sums, kept, padded, y, columns, result, sems = refs[-10:]
    x_ref, h_ref = fields.at[0], fields.at[1]
    chan = fields.shape[-1]
    rows = lax.broadcasted_iota(jnp.int32, (16, chan), 0)
    blocks = y.shape[0]
    size = side // blocks
    hold = kept.shape[0]
    inner = pl.ds(16, side - 32)
    copies = []
    if first_tile:
        part = pl.ds(side - hold, hold)
        copies.append(
            pltpu.make_async_copy(
                late, out_ref.at[first_tile - 1, part, inner], sems.at[len(tiles) * blocks]
            )
        )
        copies[-1].start()
    for at_tile, tile in enumerate(tiles):
        columns[0] = ring_ref[tile, 2].astype(F32)
        columns[1] = ring_ref[tile, 3].astype(F32)

        def prepare(row):
            m, e = (row + 1) // 2, (row + 1) % 2
            if row < 0 or row == side:
                padded[m, e] = jnp.zeros((side, chan), BF16)
            elif row == 0 or row == side - 1:
                padded[m, e] = ring_ref[tile, 0 if row == 0 else 1]
            else:
                for begin, end in row_spans(fields.shape[-2], side):
                    padded[m, e, begin:end] = read_part(h_ref, tile, row, side, begin, end)
                for at, begin, place in ((0, 0, 0), (1, side - 16, 15)):
                    old = read_part(h_ref, tile, row, side, begin, begin + 16).astype(F32)
                    new = jnp.where(rows == place, columns[at, row : row + 1], old)
                    padded[m, e, begin : begin + 16] = new.astype(BF16)

        def finish(row, value):
            total = read_row(x_ref, tile, row, side).astype(F32) + value
            line = total.astype(BF16)
            strips[tile, 0, row] = line[:16]
            strips[tile, 1, row] = line[side - 16 :]
            held = tile == tiles[-1] and row >= side - hold
            if held:
                kept[row - (side - hold)] = line[16 : side - 16]
            else:
                result[at_tile, row] = line[16 : side - 16]
            if row == 0 or row == side - 1:
                sums[tile, 0 if row == 0 else 1] = total
            sums[tile, 2, row : row + 1] = total[:1]
            sums[tile, 3, row : row + 1] = total[side - 1 :]
            if (row + 1) % size == 0 and not held:
                part = pl.ds(row + 1 - size, size)
                copies.append(
                    pltpu.make_async_copy(
                        result.at[at_tile, part],
                        out_ref.at[tile, part, inner],
                        sems.at[at_tile * blocks + row // size],
                    )
                )
                copies[-1].start()

        convolve_tile(padded, prepare, w_ref, b_ref[...], y, True, finish)
    for copy in copies:
        copy.wait()


def last_kernel(side, upper, lower, before, after, w_ref, old_strips, sums, late, *refs):
    out_ref, ends, strips, sems = refs[-4:]
    tiles, chan = sums.shape[0], sums.shape[3]
    split = tiles * side
    count = late.shape[0] - 1
    part = pl.ds(side - 1 - count, count)
    copies = [
        pltpu.make_async_copy(
            late.at[pl.ds(0, count)],
            out_ref.at[tiles - 1, part, pl.ds(16, side - 32)],
            sems.at[4 * tiles],
        )
    ]
    copies[-1].start()
    got = (upper, lower, before, after)
    groups = [got[2 + k % 2][pl.ds(split + k // 2 * CORNERS, CORNERS), :] for k in range(4)]
    corners = [group.astype(F32) for group in groups]
    zero = jnp.zeros((1, chan), F32)
    added = {}
    weights = (w_ref[0], w_ref[2], w_ref[:, 0], w_ref[:, 2])
    for edge in (2, 3, 0, 1):
        stacked = []
        for tile in range(tiles):
            line = got[edge][pl.ds(tile * side, side), :]
            first = corners[2 * edge][tile : tile + 1] if edge < 2 else zero
            last = corners[2 * edge + 1][tile : tile + 1] if edge < 2 else zero
            wide = line.astype(F32)
            stacked.append(
                jnp.concatenate(
                    [
                        shift_down(wide, first).astype(BF16),
                        line,
                        shift_up(wide, last).astype(BF16),
                    ],
                    axis=1,
                )
            )
        added[edge] = jnp.dot(
            jnp.concatenate(stacked, axis=0),
            weights[edge].reshape(3 * chan, chan),
            preferred_element_type=F32,
        )
    rows = lax.broadcasted_iota(jnp.int32, (side, chan), 0)
    few = lax.broadcasted_iota(jnp.int32, (16, chan), 0)
    spans = [slice(tile * side, (tile + 1) * side) for tile in range(tiles)]
    inner = pl.ds(1, side - 2)
    for tile in range(tiles):
        for edge, begin, place in ((2, 0, 0), (3, side - 16, 15)):
            column = sums[tile, edge] + added[edge][spans[tile]]
            for row in range(1, side - 1):
                old = old_strips[tile, edge - 2, row].astype(F32)
                new = jnp.where(few == place, column[row : row + 1], old)
                strips[tile, edge - 2, row] = new.astype(BF16)
            copies.append(
                pltpu.make_async_copy(
                    strips.at[tile, edge - 2, inner],
                    out_ref.at[tile, inner, pl.ds(begin, 16)],
                    sems.at[len(copies) - 1],
                )
            )
            copies[-1].start()
    for tile in range(tiles):
        for edge in range(2):
            total = sums[tile, edge] + added[edge][spans[tile]]
            at = 0 if edge == 0 else side - 1
            left = added[2][spans[tile]][at : at + 1]
            right = added[3][spans[tile]][at : at + 1]
            total = total + jnp.where(rows == 0, left, 0.0)
            total = total + jnp.where(rows == side - 1, right, 0.0)
            ends[tile, edge] = total.astype(BF16)
            copies.append(
                pltpu.make_async_copy(
                    ends.at[tile, edge], out_ref.at[tile, at], sems.at[len(copies) - 1]
                )
            )
            copies[-1].start()
    for copy in copies:
        copy.wait()


def paired_weights(weight):
    chan_in, chan_out = weight.shape[2:]
    by_tap = weight.transpose(0, 2, 1, 3).reshape(3, chan_in, 3 * chan_out)
    zero = jnp.zeros((1, chan_in, 3 * chan_out), weight.dtype)
    first = jnp.concatenate([by_tap, zero], 0)
    second = jnp.concatenate([zero, by_tap], 0)
    return jnp.stack([first, second], 2).reshape(4 * chan_in, 6 * chan_out)


def swap_far(array, axis):
    size = lax.axis_size(axis)
    pairs = [(i, (i + 1 if i % 2 else i - 1) % size) for i in range(size)]
    return lax.ppermute(array, axis, pairs)


def swap_near(array, axis):
    return lax.ppermute(array, axis, [(i, i ^ 1) for i in range(lax.axis_size(axis))])


def neighbours_along(array, axis):
    size = lax.axis_size(axis)
    after = lax.ppermute(array, axis, [(i, (i - 1) % size) for i in range(size)])
    before = lax.ppermute(array, axis, [(i, (i + 1) % size) for i in range(size)])
    return after, before


def shards(latitude_rows, tile_order, neighbours, rotations, w_first, b_first, w_second, b_second):
    devices = lax.axis_size("face") * lax.axis_size("tile")
    tiles = neighbours.shape[0]
    piece, chan = latitude_rows.shape[1:]
    side = int(round((piece * devices) ** 0.5))
    vmem_spec = pl.BlockSpec(memory_space=VMEM)
    smem_spec = pl.BlockSpec(memory_space=pltpu.SMEM)
    hbm_spec = pl.BlockSpec(memory_space=pltpu.HBM)
    params = pltpu.CompilerParams(vmem_limit_bytes=LIMIT)

    groups = 8 if latitude_rows.shape[0] % 8 == 0 else 1
    ordered = pl.pallas_call(
        gather_kernel,
        in_specs=[smem_spec, hbm_spec],
        out_specs=hbm_spec,
        out_shape=jax.ShapeDtypeStruct(latitude_rows.shape, latitude_rows.dtype),
        scratch_shapes=[
            VMEM(latitude_rows.shape, latitude_rows.dtype),
            pltpu.SemaphoreType.DMA((groups,)),
            pltpu.SemaphoreType.DMA,
        ],
        compiler_params=pltpu.CompilerParams(vmem_limit_bytes=WIDE_LIMIT),
        name="order",
    )(tile_order, latitude_rows)
    gathered = lax.all_to_all(ordered, AXES, split_axis=0, concat_axis=0, tiled=True)

    asked = neighbours % tiles * 4 + rotations
    after, before = neighbours_along(asked, "face")
    column = jnp.stack([asked, after, before], 0)
    on, back = neighbours_along(column, "tile")
    asked = jnp.stack(
        [after, before] + [side_rows[i] for i in range(3) for side_rows in (on, back)], 0
    )
    turn = (asked % 4)[..., None] == jnp.arange(4, dtype=jnp.int32)
    strip = jnp.sum(jnp.where(turn, jnp.asarray(STRIP_TABLE), 0), -1)
    flip = jnp.sum(jnp.where(turn, jnp.asarray(FLIP_TABLE), 0), -1)
    codes = ((flip * tiles + asked // 4) * 4 + strip).reshape(8, tiles * 8)
    odd = jnp.stack([lax.axis_index("face") % 2, lax.axis_index("tile") % 2]).astype(jnp.int32)
    codes = jnp.concatenate([codes, jnp.pad(odd, (0, tiles * 8 - 2))[None]], 0)
    constants = (
        paired_weights(w_first),
        paired_weights(w_second),
        w_second,
        w_first.reshape(9 * chan, chan),
        b_first.reshape(1, chan),
        b_second.reshape(1, chan),
    )
    odd_rows = jnp.broadcast_to(jnp.pad(odd, (0, 6))[:, None], (8, chan))
    odd = (odd[0] == 1, odd[1] == 1)
    gathered, codes, odd, odd_rows, constants = lax.optimization_barrier(
        (gathered, codes, odd, odd_rows, constants)
    )
    w_one, w_two, w_pads, w_edges, b_one, b_two = constants
    pieces = gathered.reshape(devices, tiles, piece, chan)

    split = tiles * side
    message_shape = jax.ShapeDtypeStruct((split + 2 * CORNERS, chan), BF16)
    line_shape = (tiles, 8, side, chan)
    fields_shape = jax.ShapeDtypeStruct((2,) + pieces.shape, BF16)
    codes_scratch = pltpu.SMEM(codes.shape, jnp.int32)
    four = VMEM((4,) + message_shape.shape, BF16)
    lines_scratch = VMEM((8 * tiles, side, chan), BF16)
    fields, ring, *sends = pl.pallas_call(
        functools.partial(border_kernel, side),
        in_specs=[hbm_spec, hbm_spec],
        out_specs=[vmem_spec] * 6,
        out_shape=[
            fields_shape,
            jax.ShapeDtypeStruct((tiles, 8, side, chan), BF16),
        ]
        + [message_shape] * 4,
        scratch_shapes=[lines_scratch, four, codes_scratch, pltpu.SemaphoreType.DMA((tiles + 1,))],
        compiler_params=params,
        name="borders",
    )(codes, pieces)

    blocks = 4
    field = VMEM((side // 2 + 1, 2, side, chan), BF16)
    products = VMEM((blocks, side // 2 // blocks * side, 6 * chan), F32)
    field_shape = jax.ShapeDtypeStruct((tiles, side, side, chan), BF16)

    def first(part, done):
        return (
            pl.pallas_call(
                functools.partial(first_kernel, side, part),
                in_specs=[vmem_spec] * 3,
                out_specs=vmem_spec,
                out_shape=fields_shape,
                input_output_aliases={2: 0},
                scratch_shapes=[field, products],
                compiler_params=params,
                name="first",
            )(w_one, b_one, *(done or (fields,))),
        )

    odd_face, odd_tile = odd

    def halo(sends, work):
        second, first = swap_far(sends[1], "face"), swap_near(sends[0], "face")
        done = work[0](())
        first, second, done = lax.optimization_barrier((first, second, done))
        groups = [
            jnp.where(odd_face, a[split:], b[split:]).reshape(2, CORNERS, chan)
            for a, b in ((first, second), (second, first))
        ]
        near, far = (
            jnp.concatenate(
                [own[:split]] + [jnp.where(odd_tile, g[1 - at], g[at]) for g in groups], 0
            )
            for at, own in enumerate(sends[2:])
        )
        third, fourth = swap_far(far, "tile"), swap_near(near, "tile")
        done = work[1](done)
        third, fourth, done = lax.optimization_barrier((third, fourth, done))
        return (first, second, fourth, third), done

    middle = (tiles + 1) // 2
    halves = [range(middle), range(middle, tiles)]
    got, fields = halo(sends, [functools.partial(first, part) for part in halves])
    *sends, hidden_ring = pl.pallas_call(
        ring_kernel,
        in_specs=[hbm_spec] + [vmem_spec] * 8,
        out_specs=[vmem_spec] * 5,
        out_shape=[message_shape] * 4 + [jax.ShapeDtypeStruct((tiles, 4, side, chan), BF16)],
        scratch_shapes=[lines_scratch, four, four, codes_scratch, pltpu.SemaphoreType.DMA],
        compiler_params=params,
        name="hidden_ring",
    )(codes, odd_rows, ring, w_edges, b_one, *got)

    result_specs = [vmem_spec, hbm_spec, vmem_spec, vmem_spec]
    strips_shape = jax.ShapeDtypeStruct((tiles, 2, side, 16, chan), BF16)
    sums_shape = jax.ShapeDtypeStruct((tiles, 4, side, chan), F32)
    kept_shape = jax.ShapeDtypeStruct((2 * (side // blocks), side - 32, chan), BF16)

    def second(part, done):
        *done, late = done or (*fields, None)
        late = [] if late is None else [late]
        return pl.pallas_call(
            functools.partial(second_kernel, side, part, part[0]),
            in_specs=[vmem_spec] * (3 + len(late)) + result_specs[: len(done)],
            out_specs=result_specs + [vmem_spec],
            out_shape=[fields_shape, field_shape, strips_shape, sums_shape, kept_shape],
            input_output_aliases={3 + len(late) + i: i for i in range(len(done))},
            scratch_shapes=[
                field,
                products,
                VMEM((2, side, chan), F32),
                VMEM((len(part), side, side - 32, chan), BF16),
                pltpu.SemaphoreType.DMA((len(part) * blocks + 1,)),
            ],
            compiler_params=params,
            name="second",
        )(hidden_ring, w_two, b_two, *late, *done)

    got, (_, out, strips, sums, late) = halo(
        sends, [functools.partial(second, part) for part in halves]
    )
    pads = [
        jnp.where(flag, a, b)
        for flag, pair in ((odd_face, got[:2]), (odd_tile, got[2:]))
        for a, b in (pair, pair[::-1])
    ]
    return pl.pallas_call(
        functools.partial(last_kernel, side),
        in_specs=[vmem_spec] * 8 + [hbm_spec],
        out_specs=hbm_spec,
        out_shape=field_shape,
        input_output_aliases={8: 0},
        scratch_shapes=[
            VMEM((tiles, 2, side, chan), BF16),
            VMEM(strips_shape.shape, BF16),
            pltpu.SemaphoreType.DMA((4 * tiles + 1,)),
        ],
        compiler_params=params,
        name="last",
    )(*pads, w_pads, strips, sums, late, out)


def solution(mesh):
    return jax.shard_map(
        shards,
        mesh=mesh,
        in_specs=(
            P(None, ("face", "tile"), None),
            P(),
            P(("face", "tile"), None),
            P(("face", "tile"), None),
            P(),
            P(),
            P(),
            P(),
        ),
        out_specs=P(("face", "tile"), None, None, None),
        check_vma=False,
    )
```

```python
import functools

import jax
import jax.numpy as jnp
import numpy as np
from jax import lax
from jax.experimental import pallas as pl
from jax.experimental.pallas import tpu as pltpu
from jax.sharding import PartitionSpec as P

STRIP_TABLE = np.array(
    [
        [1, 2, 0, 3],
        [0, 3, 1, 2],
        [3, 1, 2, 0],
        [2, 0, 3, 1],
        [1, 2, 0, 3],
        [1, 2, 0, 3],
        [0, 3, 1, 2],
        [0, 3, 1, 2],
    ],
    np.int32,
)
FLIP_TABLE = np.array(
    [
        [0, 0, 1, 1],
        [0, 0, 1, 1],
        [0, 1, 1, 0],
        [0, 1, 1, 0],
        [0, 0, 1, 1],
        [0, 0, 1, 1],
        [0, 0, 1, 1],
        [0, 0, 1, 1],
    ],
    np.int32,
)
DIRECTIONS = [(-1, 0), (1, 0), (0, -1), (0, 1), (-1, -1), (-1, 1), (1, -1), (1, 1)]
AXES = ("face", "tile")
VMEM = pltpu.VMEM
F32 = jnp.float32
BF16 = jnp.bfloat16
LIMIT = 32 * 1024 * 1024
WIDE_LIMIT = 60 * 1024 * 1024
CORNERS = 16


def shift_down(line, first):
    moved = pltpu.roll(line, 1, 0)
    rows = lax.broadcasted_iota(jnp.int32, moved.shape, 0)
    return jnp.where(rows == 0, first, moved)


def shift_up(line, last):
    size = line.shape[0]
    moved = pltpu.roll(line, size - 1, 0)
    rows = lax.broadcasted_iota(jnp.int32, moved.shape, 0)
    return jnp.where(rows == size - 1, last, moved)


def gelu(value):
    return (0.5 * value) * (1.0 + lax.erf(value * np.float32(np.sqrt(0.5))))


def pick_lines(codes_ref, lines, picked, message_refs, tiles):
    side = lines.shape[1]
    shape = (CORNERS, lines.shape[2])
    rows = lax.broadcasted_iota(jnp.int32, shape, 0)
    for direction in range(8):
        corner = jnp.zeros(shape, F32)
        for tile in range(tiles):
            line = lines[codes_ref[direction, tile * 8 + direction]]
            if direction < 4:
                picked[direction, pl.ds(tile * side, side), :] = line
            else:
                at = side - 1 if direction in (4, 6) else 0
                pixel = line.astype(F32)[at : at + 1]
                corner = jnp.where(rows == tile, pixel, corner)
        if direction >= 4:
            group = tiles * side + (direction % 2) * CORNERS
            picked[direction // 2 - 2, pl.ds(group, CORNERS), :] = corner.astype(BF16)
            picked[direction // 2, pl.ds(group, CORNERS), :] = jnp.zeros(shape, BF16)
    for axis in range(2):
        odd = codes_ref[8, axis]
        message_refs[2 * axis][...] = picked[2 * axis + odd]
        message_refs[2 * axis + 1][...] = picked[2 * axis + 1 - odd]


def in_order(odd, first_ref, second_ref):
    first, second = first_ref[...].astype(F32), second_ref[...].astype(F32)
    before, after = jnp.where(odd == 1, first, second), jnp.where(odd == 1, second, first)
    return before.astype(BF16), after.astype(BF16)


def flip_line(line):
    size = line.shape[0]
    row = lax.broadcasted_iota(jnp.int32, (size, size), 0)
    col = lax.broadcasted_iota(jnp.int32, (size, size), 1)
    turn = jnp.where(row + col == size - 1, 1.0, 0.0).astype(BF16)
    return jnp.dot(turn, line, preferred_element_type=F32).astype(BF16)


def gather_kernel(order_ref, x_ref, o_ref, held, in_sems, out_sem):
    groups = in_sems.shape[0]
    size = held.shape[0] // groups

    def start(at, carry):
        pltpu.make_async_copy(
            x_ref.at[order_ref[at]], held.at[at], in_sems.at[at // size]
        ).start()
        return carry

    lax.fori_loop(0, held.shape[0], start, 0)
    for group in range(groups):
        part = pl.ds(group * size, size)
        pltpu.make_async_copy(x_ref.at[part], held.at[part], in_sems.at[group]).wait()
        pltpu.make_async_copy(held.at[part], o_ref.at[part], out_sem).start()
    pltpu.make_async_copy(held, o_ref, out_sem).wait()


def border_kernel(side, codes, source, fields, ring_ref, *rest):
    x_ref = fields.at[0]
    message_refs, (lines, picked, codes_ref, sems) = rest[:4], rest[4:]
    devices, tiles, piece, chan = x_ref.shape
    copies = [
        pltpu.make_async_copy(source.at[:, tile], x_ref.at[:, tile], sems.at[tile])
        for tile in range(tiles)
    ]
    copies.append(pltpu.make_async_copy(codes, codes_ref, sems.at[tiles]))
    for copy in copies:
        copy.start()
    for tile in range(tiles):
        copies[tile].wait()
        ring = [read_row(x_ref, tile, row, side) for row in (0, 1, side - 2, side - 1)]
        if piece >= side:
            low, high = (
                jnp.stack(
                    [
                        x_ref[:, tile, row * side + at : row * side + at + 16]
                        for row in range(piece // side)
                    ],
                    1,
                ).reshape(side, 16, chan)
                for at in (0, side - 16)
            )
        else:
            image = x_ref[:, tile].reshape(side, side // piece, piece, chan)
            low, high = image[:, 0, :16], image[:, -1, piece - 16 :]
        low, high = low.astype(F32), high.astype(F32)
        ring += [v.astype(BF16) for v in (low[:, 0], low[:, 1], high[:, 14], high[:, 15])]
        for at, line in enumerate(ring):
            ring_ref[tile, at] = line
        for strip, at in enumerate((0, 3, 4, 7)):
            lines[tile * 4 + strip] = ring[at]
            lines[tiles * 4 + tile * 4 + strip] = flip_line(ring[at])
    copies[tiles].wait()
    pick_lines(codes_ref, lines, picked, message_refs, tiles)


def ring_kernel(codes, odd_ref, ring_ref, w_ref, b_ref, *rest):
    got_refs, message_refs, (own_ref, lines, picked, got, codes_ref, sem) = (
        rest[:4],
        rest[4:8],
        rest[8:],
    )
    copy = pltpu.make_async_copy(codes, codes_ref, sem)
    copy.start()
    for axis in range(2):
        first, second = got_refs[2 * axis], got_refs[2 * axis + 1]
        got[2 * axis], got[2 * axis + 1] = in_order(odd_ref[axis : axis + 1], first, second)
    tiles = ring_ref.shape[0]
    side = ring_ref.shape[2]
    pads = [[got[k, pl.ds(t * side, side), :] for t in range(tiles)] for k in range(4)]
    corners = [
        got[2 + k % 2, pl.ds(tiles * side + k // 2 * CORNERS, CORNERS), :].astype(F32)
        for k in range(4)
    ]
    plans = [
        (0, 0, 1, 0, 1, 2, 3, 0, 1, lambda dy, dx: (dy, dx)),
        (1, 2, 3, 3, 2, 2, 3, side - 1, side - 2, lambda dy, dx: (2 - dy, dx)),
        (2, 0, 2, 4, 5, 0, 1, 0, 1, lambda dy, dx: (dx, dy)),
        (3, 1, 3, 7, 6, 0, 1, side - 1, side - 2, lambda dy, dx: (2 - dx, dy)),
    ]
    stacked = []
    for pad, c_first, c_last, line_0, line_1, end_a, end_b, at_0, at_1, tap in plans:
        for tile in range(tiles):
            begin = pads[end_a][tile].astype(F32)
            finish = pads[end_b][tile].astype(F32)
            parts = []
            for line, first, last in (
                (
                    pads[pad][tile],
                    corners[c_first][tile : tile + 1],
                    corners[c_last][tile : tile + 1],
                ),
                (ring_ref[tile, line_0], begin[at_0 : at_0 + 1], finish[at_0 : at_0 + 1]),
                (ring_ref[tile, line_1], begin[at_1 : at_1 + 1], finish[at_1 : at_1 + 1]),
            ):
                wide = line.astype(F32)
                parts.append(
                    (
                        shift_down(wide, first).astype(BF16),
                        line,
                        shift_up(wide, last).astype(BF16),
                    )
                )
            taps = [tap(dy, dx) for dy in range(3) for dx in range(3)]
            stacked.append(jnp.concatenate([parts[d][j] for d, j in taps], axis=1))
    summed = jnp.dot(
        jnp.concatenate(stacked, axis=0), w_ref[...], preferred_element_type=F32
    )
    hidden = gelu(summed + b_ref[...]).astype(BF16)
    for edge in range(4):
        for tile in range(tiles):
            at = (edge * tiles + tile) * side
            line = hidden[at : at + side]
            own_ref[tile, edge] = line
            lines[tile * 4 + edge] = line
            lines[tiles * 4 + tile * 4 + edge] = flip_line(line)
    copy.wait()
    pick_lines(codes_ref, lines, picked, message_refs, tiles)


def read_row(x_ref, tile, row, side):
    piece = x_ref.shape[2]
    at = row * side // piece
    if piece >= side:
        start = row * side % piece
        return x_ref[at, tile, start : start + side]
    return x_ref[at : at + side // piece, tile].reshape(side, x_ref.shape[3])


def write_row(ref, tile, row, side, line):
    piece = ref.shape[2]
    at = row * side // piece
    if piece >= side:
        start = row * side % piece
        ref[at, tile, start : start + side] = line
    else:
        count = side // piece
        ref[at : at + count, tile] = line.reshape(count, piece, line.shape[-1])


def row_spans(piece, side):
    cuts = [16] + list(range(piece, side, piece)) + [side - 16]
    return [(a, b) for a, b in zip(cuts, cuts[1:]) if a < b]


def read_part(ref, tile, row, side, begin, end):
    piece = ref.shape[2]
    first = row * side + begin
    start = first % piece
    return ref[first // piece, tile, start : start + end - begin]


def convolve_tile(padded, prepare, w_ref, bias, y, masked, finish):
    side = padded.shape[2]
    chan = padded.shape[3]
    blocks = y.shape[0]
    step = side // 2 // blocks
    rows = lax.broadcasted_iota(jnp.int32, (side, chan), 0)

    def multiply(block):
        begin = 2 * step * block
        for row in range(begin + 1 if block else -1, begin + 2 * step + 1):
            prepare(row)
        lhs = jnp.concatenate(
            [
                padded[pl.ds(step * block + j // 2, step), j % 2].reshape(step * side, chan)
                for j in range(4)
            ],
            axis=1,
        )
        y[block] = jnp.dot(lhs, w_ref[...], preferred_element_type=F32)

    multiply(0)
    for block in range(blocks):
        if block + 1 < blocks:
            multiply(block + 1)
        for i in range(step):
            for half in range(2):
                row = (block * step + i) * 2 + half
                a, b, c = (
                    y[block, pl.ds(i * side, side), pl.ds((half * 3 + dx) * chan, chan)]
                    for dx in range(3)
                )
                a = pltpu.roll(a, 1, 0)
                c = pltpu.roll(c, side - 1, 0)
                if masked:
                    a = jnp.where(rows == 0, 0.0, a)
                    c = jnp.where(rows == side - 1, 0.0, c)
                finish(row, (a + c) + (b + bias))


def first_kernel(side, tiles, *refs):
    w_ref, b_ref = refs[:2]
    fields, padded, y = refs[-3:]
    x_ref, h_ref = fields.at[0], fields.at[1]
    for tile in tiles:

        def prepare(row):
            if 0 <= row < side:
                line = read_row(x_ref, tile, row, side)
            else:
                line = jnp.zeros(padded.shape[2:], BF16)
            padded[(row + 1) // 2, (row + 1) % 2] = line

        def finish(row, value):
            write_row(h_ref, tile, row, side, gelu(value).astype(BF16))

        convolve_tile(padded, prepare, w_ref, b_ref[...], y, False, finish)


def second_kernel(side, tiles, first_tile, *refs):
    ring_ref, w_ref, b_ref = refs[:3]
    late = refs[3] if first_tile else None
    fields, out_ref, strips, sums, kept, padded, y, columns, result, sems = refs[-10:]
    x_ref, h_ref = fields.at[0], fields.at[1]
    chan = fields.shape[-1]
    rows = lax.broadcasted_iota(jnp.int32, (16, chan), 0)
    blocks = y.shape[0]
    size = side // blocks
    hold = kept.shape[0]
    inner = pl.ds(16, side - 32)
    copies = []
    if first_tile:
        part = pl.ds(side - hold, hold)
        copies.append(
            pltpu.make_async_copy(
                late, out_ref.at[first_tile - 1, part, inner], sems.at[len(tiles) * blocks]
            )
        )
        copies[-1].start()
    for at_tile, tile in enumerate(tiles):
        columns[0] = ring_ref[tile, 2].astype(F32)
        columns[1] = ring_ref[tile, 3].astype(F32)

        def prepare(row):
            m, e = (row + 1) // 2, (row + 1) % 2
            if row < 0 or row == side:
                padded[m, e] = jnp.zeros((side, chan), BF16)
            elif row == 0 or row == side - 1:
                padded[m, e] = ring_ref[tile, 0 if row == 0 else 1]
            else:
                for begin, end in row_spans(fields.shape[-2], side):
                    padded[m, e, begin:end] = read_part(h_ref, tile, row, side, begin, end)
                for at, begin, place in ((0, 0, 0), (1, side - 16, 15)):
                    old = read_part(h_ref, tile, row, side, begin, begin + 16).astype(F32)
                    new = jnp.where(rows == place, columns[at, row : row + 1], old)
                    padded[m, e, begin : begin + 16] = new.astype(BF16)

        def finish(row, value):
            total = read_row(x_ref, tile, row, side).astype(F32) + value
            line = total.astype(BF16)
            strips[tile, 0, row] = line[:16]
            strips[tile, 1, row] = line[side - 16 :]
            held = tile == tiles[-1] and row >= side - hold
            if held:
                kept[row - (side - hold)] = line[16 : side - 16]
            else:
                result[at_tile, row] = line[16 : side - 16]
            if row == 0 or row == side - 1:
                sums[tile, 0 if row == 0 else 1] = total
            sums[tile, 2, row : row + 1] = total[:1]
            sums[tile, 3, row : row + 1] = total[side - 1 :]
            if (row + 1) % size == 0 and not held:
                part = pl.ds(row + 1 - size, size)
                copies.append(
                    pltpu.make_async_copy(
                        result.at[at_tile, part],
                        out_ref.at[tile, part, inner],
                        sems.at[at_tile * blocks + row // size],
                    )
                )
                copies[-1].start()

        convolve_tile(padded, prepare, w_ref, b_ref[...], y, True, finish)
    for copy in copies:
        copy.wait()


def last_kernel(side, upper, lower, before, after, w_ref, old_strips, sums, late, *refs):
    out_ref, ends, strips, sems = refs[-4:]
    tiles, chan = sums.shape[0], sums.shape[3]
    split = tiles * side
    count = late.shape[0] - 1
    part = pl.ds(side - 1 - count, count)
    copies = [
        pltpu.make_async_copy(
            late.at[pl.ds(0, count)],
            out_ref.at[tiles - 1, part, pl.ds(16, side - 32)],
            sems.at[4 * tiles],
        )
    ]
    copies[-1].start()
    got = (upper, lower, before, after)
    groups = [got[2 + k % 2][pl.ds(split + k // 2 * CORNERS, CORNERS), :] for k in range(4)]
    corners = [group.astype(F32) for group in groups]
    zero = jnp.zeros((1, chan), F32)
    added = {}
    weights = (w_ref[0], w_ref[2], w_ref[:, 0], w_ref[:, 2])
    for edge in (2, 3, 0, 1):
        stacked = []
        for tile in range(tiles):
            line = got[edge][pl.ds(tile * side, side), :]
            first = corners[2 * edge][tile : tile + 1] if edge < 2 else zero
            last = corners[2 * edge + 1][tile : tile + 1] if edge < 2 else zero
            wide = line.astype(F32)
            stacked.append(
                jnp.concatenate(
                    [
                        shift_down(wide, first).astype(BF16),
                        line,
                        shift_up(wide, last).astype(BF16),
                    ],
                    axis=1,
                )
            )
        added[edge] = jnp.dot(
            jnp.concatenate(stacked, axis=0),
            weights[edge].reshape(3 * chan, chan),
            preferred_element_type=F32,
        )
    rows = lax.broadcasted_iota(jnp.int32, (side, chan), 0)
    few = lax.broadcasted_iota(jnp.int32, (16, chan), 0)
    spans = [slice(tile * side, (tile + 1) * side) for tile in range(tiles)]
    inner = pl.ds(1, side - 2)
    for tile in range(tiles):
        for edge, begin, place in ((2, 0, 0), (3, side - 16, 15)):
            column = sums[tile, edge] + added[edge][spans[tile]]
            for row in range(1, side - 1):
                old = old_strips[tile, edge - 2, row].astype(F32)
                new = jnp.where(few == place, column[row : row + 1], old)
                strips[tile, edge - 2, row] = new.astype(BF16)
            copies.append(
                pltpu.make_async_copy(
                    strips.at[tile, edge - 2, inner],
                    out_ref.at[tile, inner, pl.ds(begin, 16)],
                    sems.at[len(copies) - 1],
                )
            )
            copies[-1].start()
    for tile in range(tiles):
        for edge in range(2):
            total = sums[tile, edge] + added[edge][spans[tile]]
            at = 0 if edge == 0 else side - 1
            left = added[2][spans[tile]][at : at + 1]
            right = added[3][spans[tile]][at : at + 1]
            total = total + jnp.where(rows == 0, left, 0.0)
            total = total + jnp.where(rows == side - 1, right, 0.0)
            ends[tile, edge] = total.astype(BF16)
            copies.append(
                pltpu.make_async_copy(
                    ends.at[tile, edge], out_ref.at[tile, at], sems.at[len(copies) - 1]
                )
            )
            copies[-1].start()
    for copy in copies:
        copy.wait()


def paired_weights(weight):
    chan_in, chan_out = weight.shape[2:]
    by_tap = weight.transpose(0, 2, 1, 3).reshape(3, chan_in, 3 * chan_out)
    zero = jnp.zeros((1, chan_in, 3 * chan_out), weight.dtype)
    first = jnp.concatenate([by_tap, zero], 0)
    second = jnp.concatenate([zero, by_tap], 0)
    return jnp.stack([first, second], 2).reshape(4 * chan_in, 6 * chan_out)


def swap_far(array, axis):
    size = lax.axis_size(axis)
    pairs = [(i, (i + 1 if i % 2 else i - 1) % size) for i in range(size)]
    return lax.ppermute(array, axis, pairs)


def swap_near(array, axis):
    return lax.ppermute(array, axis, [(i, i ^ 1) for i in range(lax.axis_size(axis))])


def neighbours_along(array, axis):
    size = lax.axis_size(axis)
    after = lax.ppermute(array, axis, [(i, (i - 1) % size) for i in range(size)])
    before = lax.ppermute(array, axis, [(i, (i + 1) % size) for i in range(size)])
    return after, before


def shards(latitude_rows, tile_order, neighbours, rotations, w_first, b_first, w_second, b_second):
    devices = lax.axis_size("face") * lax.axis_size("tile")
    tiles = neighbours.shape[0]
    piece, chan = latitude_rows.shape[1:]
    side = int(round((piece * devices) ** 0.5))
    vmem_spec = pl.BlockSpec(memory_space=VMEM)
    smem_spec = pl.BlockSpec(memory_space=pltpu.SMEM)
    hbm_spec = pl.BlockSpec(memory_space=pltpu.HBM)
    params = pltpu.CompilerParams(vmem_limit_bytes=LIMIT)

    groups = 8 if latitude_rows.shape[0] % 8 == 0 else 1
    ordered = pl.pallas_call(
        gather_kernel,
        in_specs=[smem_spec, hbm_spec],
        out_specs=hbm_spec,
        out_shape=jax.ShapeDtypeStruct(latitude_rows.shape, latitude_rows.dtype),
        scratch_shapes=[
            VMEM(latitude_rows.shape, latitude_rows.dtype),
            pltpu.SemaphoreType.DMA((groups,)),
            pltpu.SemaphoreType.DMA,
        ],
        compiler_params=pltpu.CompilerParams(vmem_limit_bytes=WIDE_LIMIT),
        name="order",
    )(tile_order, latitude_rows)
    gathered = lax.all_to_all(ordered, AXES, split_axis=0, concat_axis=0, tiled=True)

    asked = neighbours % tiles * 4 + rotations
    after, before = neighbours_along(asked, "face")
    column = jnp.stack([asked, after, before], 0)
    on, back = neighbours_along(column, "tile")
    asked = jnp.stack(
        [after, before] + [side_rows[i] for i in range(3) for side_rows in (on, back)], 0
    )
    turn = (asked % 4)[..., None] == jnp.arange(4, dtype=jnp.int32)
    strip = jnp.sum(jnp.where(turn, jnp.asarray(STRIP_TABLE), 0), -1)
    flip = jnp.sum(jnp.where(turn, jnp.asarray(FLIP_TABLE), 0), -1)
    codes = ((flip * tiles + asked // 4) * 4 + strip).reshape(8, tiles * 8)
    odd = jnp.stack([lax.axis_index("face") % 2, lax.axis_index("tile") % 2]).astype(jnp.int32)
    codes = jnp.concatenate([codes, jnp.pad(odd, (0, tiles * 8 - 2))[None]], 0)
    constants = (
        paired_weights(w_first),
        paired_weights(w_second),
        w_second,
        w_first.reshape(9 * chan, chan),
        b_first.reshape(1, chan),
        b_second.reshape(1, chan),
    )
    odd_rows = jnp.broadcast_to(jnp.pad(odd, (0, 6))[:, None], (8, chan))
    odd = (odd[0] == 1, odd[1] == 1)
    gathered, codes, odd, odd_rows, constants = lax.optimization_barrier(
        (gathered, codes, odd, odd_rows, constants)
    )
    w_one, w_two, w_pads, w_edges, b_one, b_two = constants
    pieces = gathered.reshape(devices, tiles, piece, chan)

    split = tiles * side
    message_shape = jax.ShapeDtypeStruct((split + 2 * CORNERS, chan), BF16)
    line_shape = (tiles, 8, side, chan)
    fields_shape = jax.ShapeDtypeStruct((2,) + pieces.shape, BF16)
    codes_scratch = pltpu.SMEM(codes.shape, jnp.int32)
    four = VMEM((4,) + message_shape.shape, BF16)
    lines_scratch = VMEM((8 * tiles, side, chan), BF16)
    fields, ring, *sends = pl.pallas_call(
        functools.partial(border_kernel, side),
        in_specs=[hbm_spec, hbm_spec],
        out_specs=[vmem_spec] * 6,
        out_shape=[
            fields_shape,
            jax.ShapeDtypeStruct((tiles, 8, side, chan), BF16),
        ]
        + [message_shape] * 4,
        scratch_shapes=[lines_scratch, four, codes_scratch, pltpu.SemaphoreType.DMA((tiles + 1,))],
        compiler_params=params,
        name="borders",
    )(codes, pieces)

    blocks = 4
    field = VMEM((side // 2 + 1, 2, side, chan), BF16)
    products = VMEM((blocks, side // 2 // blocks * side, 6 * chan), F32)
    field_shape = jax.ShapeDtypeStruct((tiles, side, side, chan), BF16)

    def first(part, done):
        return (
            pl.pallas_call(
                functools.partial(first_kernel, side, part),
                in_specs=[vmem_spec] * 3,
                out_specs=vmem_spec,
                out_shape=fields_shape,
                input_output_aliases={2: 0},
                scratch_shapes=[field, products],
                compiler_params=params,
                name="first",
            )(w_one, b_one, *(done or (fields,))),
        )

    odd_face, odd_tile = odd

    def halo(sends, work):
        second, first = swap_far(sends[1], "face"), swap_near(sends[0], "face")
        done = work[0](())
        first, second, done = lax.optimization_barrier((first, second, done))
        groups = [
            jnp.where(odd_face, a[split:], b[split:]).reshape(2, CORNERS, chan)
            for a, b in ((first, second), (second, first))
        ]
        near, far = (
            jnp.concatenate(
                [own[:split]] + [jnp.where(odd_tile, g[1 - at], g[at]) for g in groups], 0
            )
            for at, own in enumerate(sends[2:])
        )
        fourth, third = swap_near(near, "tile"), swap_far(far, "tile")
        done = work[1](done)
        third, fourth, done = lax.optimization_barrier((third, fourth, done))
        return (first, second, fourth, third), done

    middle = (tiles + 1) // 2
    halves = [range(middle), range(middle, tiles)]
    got, fields = halo(sends, [functools.partial(first, part) for part in halves])
    *sends, hidden_ring = pl.pallas_call(
        ring_kernel,
        in_specs=[hbm_spec] + [vmem_spec] * 8,
        out_specs=[vmem_spec] * 5,
        out_shape=[message_shape] * 4 + [jax.ShapeDtypeStruct((tiles, 4, side, chan), BF16)],
        scratch_shapes=[lines_scratch, four, four, codes_scratch, pltpu.SemaphoreType.DMA],
        compiler_params=params,
        name="hidden_ring",
    )(codes, odd_rows, ring, w_edges, b_one, *got)

    result_specs = [vmem_spec, hbm_spec, vmem_spec, vmem_spec]
    strips_shape = jax.ShapeDtypeStruct((tiles, 2, side, 16, chan), BF16)
    sums_shape = jax.ShapeDtypeStruct((tiles, 4, side, chan), F32)
    kept_shape = jax.ShapeDtypeStruct((2 * (side // blocks), side - 32, chan), BF16)

    def second(part, done):
        *done, late = done or (*fields, None)
        late = [] if late is None else [late]
        return pl.pallas_call(
            functools.partial(second_kernel, side, part, part[0]),
            in_specs=[vmem_spec] * (3 + len(late)) + result_specs[: len(done)],
            out_specs=result_specs + [vmem_spec],
            out_shape=[fields_shape, field_shape, strips_shape, sums_shape, kept_shape],
            input_output_aliases={3 + len(late) + i: i for i in range(len(done))},
            scratch_shapes=[
                field,
                products,
                VMEM((2, side, chan), F32),
                VMEM((len(part), side, side - 32, chan), BF16),
                pltpu.SemaphoreType.DMA((len(part) * blocks + 1,)),
            ],
            compiler_params=params,
            name="second",
        )(hidden_ring, w_two, b_two, *late, *done)

    got, (_, out, strips, sums, late) = halo(
        sends, [functools.partial(second, part) for part in halves]
    )
    pads = [
        jnp.where(flag, a, b)
        for flag, pair in ((odd_face, got[:2]), (odd_tile, got[2:]))
        for a, b in (pair, pair[::-1])
    ]
    return pl.pallas_call(
        functools.partial(last_kernel, side),
        in_specs=[vmem_spec] * 8 + [hbm_spec],
        out_specs=hbm_spec,
        out_shape=field_shape,
        input_output_aliases={8: 0},
        scratch_shapes=[
            VMEM((tiles, 2, side, chan), BF16),
            VMEM(strips_shape.shape, BF16),
            pltpu.SemaphoreType.DMA((4 * tiles + 1,)),
        ],
        compiler_params=params,
        name="last",
    )(*pads, w_pads, strips, sums, late, out)


def solution(mesh):
    return jax.shard_map(
        shards,
        mesh=mesh,
        in_specs=(
            P(None, ("face", "tile"), None),
            P(),
            P(("face", "tile"), None),
            P(("face", "tile"), None),
            P(),
            P(),
            P(),
            P(),
        ),
        out_specs=P(("face", "tile"), None, None, None),
        check_vma=False,
    )
```
